32 devices in a mesh: wide: 8 (over z, y), narrow: 4 (over x, core).
Axes of the slice: x: 2, y: 2, z: 4, core: 2. Of those that a mesh axis runs over, the one named last changes fastest.
Arguments:
- cat_index: int32 [512, 32], P(('wide', 'narrow')), may hold values from 0 to 100351
- num_values: float32 [512, 95], P(('wide', 'narrow')), may hold values from -6 to 6
- cell_mask: int32 [512, 95], P(('wide', 'narrow')), may hold values from 0 to 1
- labels: int32 [512], P(('wide', 'narrow')), may hold values from 0 to 6
- table: float32 [100352, 192], P(('wide', 'narrow')), may hold values from -6 to 6
- table_first: float32 [100352, 192], P(('wide', 'narrow')), may hold values from -2.3841858e-07 to 2.3841858e-07
- table_second: float32 [100352, 192], P(('wide', 'narrow')), may hold values from 9.536498e-16 to 3.8145993e-15
- small: float32 [344, 192], P('narrow', 'wide')
- small_first: float32 [344, 192], P('narrow', 'wide'), may hold values from -2.3841858e-06 to 2.3841858e-06
- small_second: float32 [344, 192], P('narrow', 'wide'), may hold values from 9.486306e-14 to 3.7995415e-13
- w_qkv: float32 [2, 576, 192], P(None, 'narrow', 'wide'), may hold values from -0.4375 to 0.4375
- w_proj: float32 [2, 192, 192], P(None, 'narrow', 'wide'), may hold values from -1.75 to 1.75
- w_in: float32 [2, 512, 192], P(None, 'narrow', 'wide'), may hold values from -0.4375 to 0.4375
- w_down: float32 [2, 256, 192], P(None, 'narrow', 'wide'), may hold values from -0.375 to 0.375
- mom_qkv: float32 [2, 576, 192], P(None, 'narrow', 'wide'), may hold values from -6.67572e-06 to 6.67572e-06
- mom_proj: float32 [2, 192, 192], P(None, 'narrow', 'wide'), may hold values from -6.67572e-06 to 6.67572e-06
- mom_in: float32 [2, 512, 192], P(None, 'narrow', 'wide'), may hold values from -6.67572e-06 to 6.67572e-06
- mom_down: float32 [2, 256, 192], P(None, 'narrow', 'wide'), may hold values from -6.67572e-06 to 6.67572e-06
Outputs:
- loss_sum: float32 [], replicated
- masked_count: float32 [], replicated
- grad_norm: float32 [], replicated
- new_table: float32 [100352, 192], P(('wide', 'narrow'))
- new_table_first: float32 [100352, 192], P(('wide', 'narrow'))
- new_table_second: float32 [100352, 192], P(('wide', 'narrow'))
- new_small: float32 [344, 192], P('narrow', 'wide')
- new_small_first: float32 [344, 192], P('narrow', 'wide')
- new_small_second: float32 [344, 192], P('narrow', 'wide')
- new_qkv: float32 [2, 576, 192], P(None, 'narrow', 'wide')
- new_proj: float32 [2, 192, 192], P(None, 'narrow', 'wide')
- new_in: float32 [2, 512, 192], P(None, 'narrow', 'wide')
- new_down: float32 [2, 256, 192], P(None, 'narrow', 'wide')
- new_mom_qkv: float32 [2, 576, 192], P(None, 'narrow', 'wide')
- new_mom_proj: float32 [2, 192, 192], P(None, 'narrow', 'wide')
- new_mom_in: float32 [2, 512, 192], P(None, 'narrow', 'wide')
- new_mom_down: float32 [2, 256, 192], P(None, 'narrow', 'wide')
The draws below stay inside these ranges and needn't reach their ends.
All inputs are finite; a program needn't handle non-finite values.
Results may differ from the reference program's by a relative error of at most 0.0025.
The reference program's roundings to bfloat16 on the way (of `table_low`, `normed`, `weights`, `mixed`, `normed_two` and `hidden`) count: a program that leaves them out, or rounds other values in their place, can miss the bound.
Values may be sent and summed in bfloat16 or wider, within the bound.
A program may use at most 384 MiB of HBM per device.

```python
import math
import jax
import jax.numpy as jnp
import numpy as np
from jax import lax

D = 192
HEADS = 8
HD = 24
FF = 256
VOCAB = 100352
L = 2
NUMF = 95
CATF = 32
NCLASS = 7
STEP = 10
TOKS = 128
ROWS = 512
NSR = 344


def draw_cell_mask(key, part):
    key = jax.random.fold_in(key, 11)
    place = jnp.arange(ROWS, dtype=jnp.int32)[:, None]
    limit = 120 + 300 * place // max(ROWS - 1, 1)
    rolls = jax.random.randint(key, (ROWS, NUMF), 0, 1000)
    return (rolls < limit).astype(jnp.int32)


def draw_small(key, part):
    key = jax.random.fold_in(key, 23)
    first, second = jax.random.split(key)
    noise = jax.random.normal(first, (NSR, D), jnp.float32)
    rise = jnp.exp(jnp.log(3.0) * (jnp.arange(D, dtype=jnp.float32) / (D - 1) - 0.5))
    gains = rise[None, :] * jax.random.uniform(second, (NSR, D), jnp.float32, 0.7, 1.3)
    row = jnp.arange(NSR)[:, None]
    slot = row % 8
    in_layers = row < 8 * L
    off_fin = 8 * L + TOKS + NUMF + 1
    is_gain = in_layers & ((slot == 0) | (slot == 2)) | (row == off_fin)
    is_shift = in_layers & ~((slot == 0) | (slot == 2)) | (row == off_fin + 1)
    is_head = row >= off_fin + 2
    drawn = jnp.where(is_head, noise * D ** (-0.5), noise)
    return jnp.where(is_gain, gains, jnp.where(is_shift, 0.3 * noise, drawn))


def set_ends(drawn, rng, least, largest):
    spot = [jax.random.randint(jax.random.fold_in(rng, axis), (), 0, length) for axis, length in enumerate(drawn.shape)]
    longest = drawn.shape.index(max(drawn.shape))
    beside = spot[:longest] + [(spot[longest] + 1) % drawn.shape[longest]] + spot[longest + 1:]
    return drawn.at[tuple(spot)].set(least).at[tuple(beside)].set(largest)


def block_scale(own_key, dims, cuts, smallest, high):
    level = 1.0
    for position, shards_of in cuts:
        steps = jax.random.uniform(jax.random.fold_in(jax.random.fold_in(own_key, 6), position), (shards_of,), jnp.float32, smallest / len(cuts), high / len(cuts))
        level = level * jnp.repeat(jnp.exp(steps), dims[position] // shards_of).reshape((-1,) + (1,) * (len(dims) - 1 - position))
    return level


def skewed_wide(own_key, extent, number_of, slope):
    weights = [min(1 << octave, number_of + 1 - (1 << octave)) * (1 << 20) // math.isqrt((1 << octave) ** slope) + 1 for octave in range((number_of + 1).bit_length()) if 1 << octave <= number_of]
    deviation = 1 + sum(weights) // (1 << 30)
    table = np.cumsum(np.array([max(1, weight // deviation) for weight in weights]))
    ticket = jax.random.randint(jax.random.fold_in(own_key, 1), extent, 0, int(table[len(weights) - 1]))
    start = jnp.left_shift(1, jnp.searchsorted(jnp.asarray(table, jnp.int32), ticket, side="right").astype(jnp.int32))
    standing = start - 1 + jax.random.randint(jax.random.fold_in(own_key, 4), extent, 0, 1 << 30) % jnp.minimum(start, number_of + 1 - start)
    return jax.random.permutation(jax.random.fold_in(own_key, 2), number_of)[standing].astype(jnp.int32)


def normal_values(key, dims, width, reach, cuts=(), kind=jnp.bfloat16):
    entries = jax.random.normal(key, dims, jnp.float32) * width
    if len(cuts) > 0:
        entries = block_scale(key, dims, cuts, -0.22, 0.18) * entries
    return jnp.clip(entries, min=-reach, max=reach).astype(kind)


def setup_inputs(seed: int = 0) -> dict:
    key_of = jax.random.split(jax.random.key(seed), 19)
    return {
        "cat_index": set_ends(skewed_wide(key_of[0], (ROWS, CATF), VOCAB, 2), jax.random.fold_in(key_of[0], 3), 0, VOCAB - 1).astype(jnp.int32),
        "num_values": normal_values(key_of[1], (ROWS, NUMF), 1.0, 6.0, ((0, 32),), jnp.float32),
        "cell_mask": draw_cell_mask(jax.random.fold_in(key_of[18], 71), 0),
        "labels": set_ends(jax.random.randint(key_of[3], (ROWS,), 0, NCLASS), jax.random.fold_in(key_of[3], 1), 0, NCLASS - 1).astype(jnp.int32),
        "table": normal_values(key_of[4], (VOCAB, D), 1.0, 6.0, ((0, 32),), jnp.float32),
        "table_first": normal_values(key_of[5], (VOCAB, D), (0.0000667 * (VOCAB * D + L * (4 * D + 3 * FF) * D + NSR * D) ** -0.5), 2.384185791015625e-07, ((0, 32),), jnp.float32),
        "table_second": jnp.clip(jnp.exp(math.log(3.8145993254325855e-15) - 1.3862944 * jax.random.uniform(key_of[6], (VOCAB, D), jnp.float32) ** block_scale(key_of[6], (VOCAB, D), ((0, 32),), -0.2, 0.2)), 9.536498313581464e-16, 3.8145993254325855e-15),
        "small": draw_small(jax.random.fold_in(key_of[18], 71), 0),
        "small_first": normal_values(key_of[8], (NSR, D), (0.000667 * (VOCAB * D + L * (4 * D + 3 * FF) * D + NSR * D) ** -0.5), 2.384185791015625e-06, ((0, 4), (1, 8)), jnp.float32),
        "small_second": jnp.clip(jnp.exp(math.log(3.799541519085292e-13) - 1.3876162 * jax.random.uniform(key_of[9], (NSR, D), jnp.float32) ** block_scale(key_of[9], (NSR, D), ((0, 4), (1, 8)), -0.2, 0.2)), 9.486306190445784e-14, 3.799541519085292e-13),
        "w_qkv": normal_values(key_of[10], (L, 3 * D, D), D ** -0.5, 0.4375, ((1, 4), (2, 8)), jnp.float32),
        "w_proj": normal_values(key_of[11], (L, D, D), (D // 16) ** -0.5, 1.75, ((1, 4), (2, 8)), jnp.float32),
        "w_in": normal_values(key_of[12], (L, 2 * FF, D), D ** -0.5, 0.4375, ((1, 4), (2, 8)), jnp.float32),
        "w_down": normal_values(key_of[13], (L, FF, D), FF ** -0.5, 0.375, ((1, 4), (2, 8)), jnp.float32),
        "mom_qkv": normal_values(key_of[14], (L, 3 * D, D), (0.002 * (VOCAB * D + L * (4 * D + 3 * FF) * D + NSR * D) ** -0.5), 6.67572021484375e-06, ((1, 4), (2, 8)), jnp.float32),
        "mom_proj": normal_values(key_of[15], (L, D, D), (0.002 * (VOCAB * D + L * (4 * D + 3 * FF) * D + NSR * D) ** -0.5), 6.67572021484375e-06, ((1, 4), (2, 8)), jnp.float32),
        "mom_in": normal_values(key_of[16], (L, 2 * FF, D), (0.002 * (VOCAB * D + L * (4 * D + 3 * FF) * D + NSR * D) ** -0.5), 6.67572021484375e-06, ((1, 4), (2, 8)), jnp.float32),
        "mom_down": normal_values(key_of[17], (L, FF, D), (0.002 * (VOCAB * D + L * (4 * D + 3 * FF) * D + NSR * D) ** -0.5), 6.67572021484375e-06, ((1, 4), (2, 8)), jnp.float32),
    }


HIGHEST = lax.Precision.HIGHEST
NORM_EPS = 1e-05
CLIP = 0.002
BETA_ONE = 0.9
BETA_TWO = 0.95
ADAM_EPS = 1e-08
ADAM_RATE = 0.2
MUON_RATE = 1.0
MOMENTUM = 0.95
DECAY = 0.01
ORTHO_EPS = 1e-20
NS_ONE = 3.4445
NS_TWO = -4.775
NS_THREE = 2.0315

@jax.custom_vjp
def low(v):
    return lax.optimization_barrier(v.astype(jnp.bfloat16)).astype(jnp.float32)

@jax.custom_vjp
def low_back(v):
    return v

def low_keep(v):
    return (low(v), None)

def low_pass(kept, grad):
    return (grad,)

def back_keep(v):
    return (v, None)

def back_low(kept, grad):
    return (low(grad),)
low.defvjp(low_keep, low_pass)
low_back.defvjp(back_keep, back_low)

def normalize(value, gain, shift):
    center = value - lax.optimization_barrier(jnp.mean(value, -1, keepdims=True))
    spread = lax.optimization_barrier(jnp.mean(center * center, -1, keepdims=True))
    return center * lax.rsqrt(spread + NORM_EPS) * gain + shift

def gated(gate, upward):
    return jax.nn.gelu(gate, approximate=True) * upward

def split_heads(value, count_rows):
    return value.reshape(count_rows, TOKS, HEADS, HD)

def layer(state, matrices, vector):
    w_qkv, w_proj, w_in, w_down = matrices
    count_rows = state.shape[0]
    flat = state.reshape(-1, D)
    normed = low(normalize(flat, vector[0], vector[1]))
    joined = low_back(jnp.dot(normed, w_qkv.T, precision=HIGHEST))
    query = low(joined[:, :D] + vector[4])
    keys = low(joined[:, D:2 * D])
    values = low(joined[:, 2 * D:] + vector[5])
    scores = low_back(jnp.einsum('bqhd,bkhd->bhqk', split_heads(query, count_rows), split_heads(keys, count_rows), precision=HIGHEST))
    weights = low(jax.nn.softmax(scores * HD ** (-0.5), axis=-1))
    mixed = jnp.einsum('bhqk,bkhd->bqhd', weights, split_heads(values, count_rows), precision=HIGHEST).reshape(-1, D)
    mixed = low(low_back(mixed))
    after = flat + low_back(jnp.dot(mixed, w_proj.T, precision=HIGHEST)) + vector[6]
    normed_two = low(normalize(after, vector[2], vector[3]))
    gate_up = low_back(jnp.dot(normed_two, w_in.T, precision=HIGHEST))
    hidden = low(gated(gate_up[:, :FF], gate_up[:, FF:]))
    output = after + low_back(jnp.dot(hidden, w_down, precision=HIGHEST)) + vector[7]
    return output.reshape(state.shape)

def embed(table_low, small, index, values, cell_mask):
    count_rows = values.shape[0]
    keep = 1.0 - cell_mask.astype(values.dtype)
    off_scale = 8 * L + TOKS
    numeric = (keep * values)[:, :, None] * small[off_scale:off_scale + NUMF] + (1.0 - keep)[:, :, None] * small[off_scale + NUMF]
    looked = low_back(jnp.take(table_low, index, axis=0))
    first = jnp.zeros((count_rows, 1, D), values.dtype)
    return jnp.concatenate([first, numeric, looked], 1) + small[8 * L:off_scale]

def head_terms(state, small, class_low, values, cell_mask, labels):
    off_fin = 8 * L + TOKS + NUMF + 1
    normed = normalize(state, small[off_fin], small[off_fin + 1])
    logits = jnp.dot(low(normed[:, 0]), class_low.T, precision=HIGHEST)
    hits = labels[:, None] == jnp.arange(NCLASS)[None, :]
    picked = lax.optimization_barrier(jnp.sum(jnp.where(hits, logits, 0.0), -1))
    predict = lax.optimization_barrier(jnp.sum(normed[:, 1:1 + NUMF] * small[off_fin + 2 + NCLASS:], -1))
    error = predict - values
    return jnp.sum(cell_mask.astype(values.dtype) * error * error) + jnp.sum(jax.nn.logsumexp(logits, -1) - picked)

def adam_step(weight, gradient, first, second):
    first = BETA_ONE * first + (1.0 - BETA_ONE) * gradient
    second = BETA_TWO * second + (1.0 - BETA_TWO) * gradient * gradient
    ratio = first / (1.0 - BETA_ONE ** STEP) / (jnp.sqrt(second / (1.0 - BETA_TWO ** STEP)) + ADAM_EPS)
    return (weight - ADAM_RATE * (ratio + DECAY * weight), first, second)

def orthogonal(moment):
    block = moment * lax.rsqrt(jnp.sum(moment * moment) + ORTHO_EPS)
    for step in range(5):
        square = jnp.dot(block.T, block, precision=HIGHEST)
        block = NS_ONE * block + jnp.dot(block, NS_TWO * square + NS_THREE * jnp.dot(square, square, precision=HIGHEST), precision=HIGHEST)
    return block

def muon_step(weight, gradient, moment):
    moment = MOMENTUM * moment + gradient
    ortho = jax.vmap(orthogonal)(moment)
    scale = math.sqrt(max(1.0, weight.shape[1] / D))
    return (weight * (1.0 - MUON_RATE * DECAY) - MUON_RATE * scale * ortho, moment)

def reference(cat_index, num_values, cell_mask, labels, table, table_first, table_second, small, small_first, small_second, w_qkv, w_proj, w_in, w_down, mom_qkv, mom_proj, mom_in, mom_down):
    count = jnp.sum(cell_mask.astype(num_values.dtype))
    block_rows = math.gcd(ROWS, 32)
    blocks = ROWS // block_rows
    data = (cat_index.reshape(blocks, block_rows, CATF), num_values.reshape(blocks, block_rows, NUMF), cell_mask.reshape(blocks, block_rows, NUMF), labels.reshape(blocks, block_rows))
    class_start = 8 * L + TOKS + NUMF + 3

    def objective(table_w, small_w, qkv_w, proj_w, in_w, down_w):
        table_low = low(table_w)
        matrices = (low(qkv_w), low(proj_w), low(in_w), low(down_w))
        class_low = low(small_w[class_start:class_start + NCLASS])

        def one_block(carry, block):
            index, values, masked, targets = block
            state = embed(table_low, small_w, index, values, masked)
            for depth in range(L):
                state = layer(state, tuple((part[depth] for part in matrices)), small_w[8 * depth:8 * depth + 8])
            return (carry + head_terms(state, small_w, class_low, values, masked, targets), None)
        total, _ = lax.scan(jax.checkpoint(one_block), jnp.zeros((), num_values.dtype), data)
        return (total / count, total)
    loss_value, pull, total = jax.vjp(objective, table, small, w_qkv, w_proj, w_in, w_down, has_aux=True)
    grads = pull(jnp.ones((), num_values.dtype))
    squares = sum((jnp.sum(part * part) for part in grads))
    grad_norm = jnp.sqrt(squares)
    factor = CLIP / jnp.maximum(grad_norm, CLIP)
    clipped = [factor * part for part in grads]
    new_table, table_one, table_two = adam_step(table, clipped[0], table_first, table_second)
    new_small, small_one, small_two = adam_step(small, clipped[1], small_first, small_second)
    new_qkv, qkv_moment = muon_step(w_qkv, clipped[2], mom_qkv)
    new_proj, proj_moment = muon_step(w_proj, clipped[3], mom_proj)
    new_in, in_moment = muon_step(w_in, clipped[4], mom_in)
    new_down, down_moment = muon_step(w_down, clipped[5], mom_down)
    return (total, count, grad_norm, new_table, table_one, table_two, new_small, small_one, small_two, new_qkv, new_proj, new_in, new_down, qkv_moment, proj_moment, in_moment, down_moment)
```

```python
import functools
import math

import jax
import jax.numpy as jnp
import numpy as np
from jax import lax
from jax.experimental import pallas as pl
from jax.experimental.pallas import tpu as pltpu
from jax.sharding import PartitionSpec as P

D = 192
HEADS = 8
HD = 24
FF = 256
L = 2
NUMF = 95
CATF = 32
NCLASS = 7
STEP = 10
TOKS = 128

NORM_EPS = 1e-05
CLIP = 0.002
BETA_ONE = 0.9
BETA_TWO = 0.95
ADAM_EPS = 1e-08
ADAM_RATE = 0.2
MUON_RATE = 1.0
MOMENTUM = 0.95
DECAY = 0.01
ORTHO_EPS = 1e-20
NS_ONE = 3.4445
NS_TWO = -4.775
NS_THREE = 2.0315
GELU_A = math.sqrt(2.0 / math.pi)
GELU_B = 0.044715
SCALE = HD ** (-0.5)

F32 = jnp.float32
BF16 = jnp.bfloat16
MESH = pl.DeviceIdType.MESH

ROWS_OF = (3 * D, D, 2 * FF, FF)
ORDER = (2, 0, 1, 3)
NSR = 8 * L + TOKS + NUMF + 1 + 2 + NCLASS + NUMF
OFF_SCALE = 8 * L + TOKS
OFF_FIN = OFF_SCALE + NUMF + 1
CAP = 32
PACK = CAP + CAP // 2


def mm(left, right, left_dim=1, right_dim=0):
    return lax.dot_general(
        left, right, (((left_dim,), (right_dim,)), ((), ())), preferred_element_type=F32
    )


def up_to(value, unit):
    return -(-value // unit) * unit


def split_two(value):
    high = value.astype(BF16)
    return high, (value - high.astype(F32)).astype(BF16)


def split_three(value):
    high = value.astype(BF16)
    rest = value - high.astype(F32)
    middle = rest.astype(BF16)
    return high, middle, (rest - middle.astype(F32)).astype(BF16)


def place(wide, narrow):
    w = lax.axis_index("wide")
    n = lax.axis_index("narrow")
    return w, n, w * narrow + n


def greet_all(me, count, narrow):
    barrier = pltpu.get_barrier_semaphore()

    def signal(k, carry):
        p = lax.rem(me + k, count)
        pl.semaphore_signal(
            barrier, inc=1, device_id=(p // narrow, lax.rem(p, narrow)), device_id_type=MESH
        )
        return carry

    lax.fori_loop(1, count, signal, 0)
    return barrier


def quarter_offsets(narrow):
    offsets, total = {}, 0
    for which in ORDER:
        offsets[which] = total
        total += ROWS_OF[which] // narrow
    return offsets, total


def gather_kernel(
    index_ref, mask_ref, qkv_ref, proj_ref, in_ref, down_ref, small_ref, table_ref, pick_ref,
    out_qkv, out_proj, out_in, out_down, out_small, out_rows, out_slots, out_requests, out_stats,
    gat, ask, table_low, answers, landed,
    wide_send, wide_recv, narrow_send, narrow_recv, swide_send, swide_recv, snarrow_send, snarrow_recv,
    ask_send, ask_recv, row_send, row_recv,
    *, wide, narrow, chunk,
):
    count = wide * narrow
    w, n, me = place(wide, narrow)
    barrier = greet_all(me, count, narrow)

    def coords(p):
        return (p // narrow, lax.rem(p, narrow))

    offsets, total = quarter_offsets(narrow)
    width = qkv_ref.shape[1]
    rows_pad = gat.shape[2]
    shards = (qkv_ref, proj_ref, in_ref, down_ref)
    pieces = [
        jnp.concatenate([shards[which][l] for which in ORDER], 1) for l in range(L)
    ]
    if rows_pad > L * width:
        pieces.append(jnp.zeros((rows_pad - L * width, total), F32))
    gat[n, w] = jnp.concatenate(pieces, 0).astype(BF16)
    small = small_ref[...]
    own_rows = small.shape[1]
    pieces = [small]
    if out_small.shape[2] > width:
        pieces = [jnp.concatenate([small, jnp.zeros((out_small.shape[2] - width, own_rows), F32)], 0)]
    out_small[n, w] = jnp.concatenate(
        pieces + [jnp.zeros((out_small.shape[2], TOKS - own_rows), F32)], 1
    )

    entries = index_ref.shape[1]
    local = table_ref.shape[1]
    index_row = index_ref[...]
    owner_row = jnp.zeros_like(index_row)
    for k in range(1, count):
        owner_row = owner_row + (index_row >= k * local).astype(jnp.int32)
    base_row = owner_row * local
    index_col = jnp.transpose(jnp.broadcast_to(index_row, (8, entries)))[:, :1]
    before = lax.broadcasted_iota(jnp.int32, (entries, entries), 0)
    after = lax.broadcasted_iota(jnp.int32, (entries, entries), 1)
    same = index_col == index_row
    first_col = 1.0 - jnp.max(jnp.where(same & (after < before), 1.0, 0.0), 1, keepdims=True)
    first_row = 1.0 - jnp.max(jnp.where(same & (before < after), 1.0, 0.0), 0, keepdims=True)
    lower = (index_col >= base_row) & (index_col < index_row)
    rank_row = jnp.sum(jnp.where(lower, first_col, 0.0), 0, keepdims=True).astype(jnp.int32)
    out_slots[...] = owner_row * CAP + rank_row
    over = jnp.max(jnp.where(rank_row >= CAP, 1.0, 0.0), 1, keepdims=True)
    hidden_cells = jnp.sum(jnp.sum(mask_ref[...].astype(F32), 0, keepdims=True), 1, keepdims=True)
    place_row = index_row - base_row
    owners = lax.broadcasted_iota(jnp.int32, (count, entries), 0)
    mine = jnp.where(owners == owner_row, first_row, 0.0)
    high = lax.shift_right_logical(place_row, 6)
    low = place_row - high * 64
    at_rank = jnp.where(
        lax.broadcasted_iota(jnp.int32, (TOKS, entries), 0) == rank_row, 1.0, 0.0
    ).astype(BF16)
    wanted = 64.0 * mm((mine * high.astype(F32)).astype(BF16), at_rank, 1, 1) + mm(
        (mine * low.astype(F32)).astype(BF16), at_rank, 1, 1
    )
    lane = lax.broadcasted_iota(jnp.int32, (count, TOKS), 1)
    wanted = jnp.where(lane < CAP, wanted, 0.0)
    wanted = jnp.where(lane == CAP, over, wanted)
    wanted = jnp.where(lane == CAP + 1, hidden_cells, wanted)
    for k in range(count):
        ask[k] = jnp.broadcast_to(wanted[k : k + 1], (8, TOKS))

    pl.semaphore_wait(barrier, count - 1)

    def wide_copy(p, slot):
        return (
            pltpu.make_async_remote_copy(
                src_ref=gat.at[n, w], dst_ref=gat.at[n, slot], send_sem=wide_send.at[p],
                recv_sem=wide_recv.at[slot], device_id=(p, n), device_id_type=MESH,
            ),
            pltpu.make_async_remote_copy(
                src_ref=out_small.at[n, w], dst_ref=out_small.at[n, slot], send_sem=swide_send.at[p],
                recv_sem=swide_recv.at[slot], device_id=(p, n), device_id_type=MESH,
            ),
        )

    def ask_copy(p, slot):
        return pltpu.make_async_remote_copy(
            src_ref=ask.at[p], dst_ref=out_requests.at[slot], send_sem=ask_send.at[p],
            recv_sem=ask_recv.at[slot], device_id=coords(p), device_id_type=MESH,
        )

    def narrow_copy(p, slot):
        return (
            pltpu.make_async_remote_copy(
                src_ref=gat.at[n], dst_ref=gat.at[slot], send_sem=narrow_send.at[p],
                recv_sem=narrow_recv.at[slot], device_id=(w, p), device_id_type=MESH,
            ),
            pltpu.make_async_remote_copy(
                src_ref=out_small.at[n], dst_ref=out_small.at[slot], send_sem=snarrow_send.at[p],
                recv_sem=snarrow_recv.at[slot], device_id=(w, p), device_id_type=MESH,
            ),
        )

    def row_copy(p, slot):
        return pltpu.make_async_remote_copy(
            src_ref=answers.at[p], dst_ref=landed.at[slot], send_sem=row_send.at[p],
            recv_sem=row_recv.at[slot], device_id=coords(p), device_id_type=MESH,
        )

    def over_peers(origin, size, body):
        def run(k, carry):
            body(lax.rem(origin + k, size))
            return carry

        lax.fori_loop(1, size, run, 0)

    def start_wide(p):
        for copy in wide_copy(p, w):
            copy.start()

    def end_wide(p):
        for copy in wide_copy(p, p):
            copy.wait_recv()

    def start_narrow(p):
        for copy in narrow_copy(p, n):
            copy.start()

    def end_narrow(p):
        for copy in narrow_copy(p, p):
            copy.wait_recv()

    over_peers(me, count, lambda p: ask_copy(p, me).start())
    over_peers(w, wide, start_wide)
    out_requests[me] = ask[me]
    table_low[...] = table_ref[...].astype(BF16)
    over_peers(w, wide, end_wide)
    over_peers(n, narrow, start_narrow)
    over_peers(me, count, lambda p: ask_copy(p, p).wait_recv())

    eye = lax.broadcasted_iota(jnp.int32, (CAP, TOKS), 0) == lax.broadcasted_iota(
        jnp.int32, (CAP, TOKS), 1
    )
    spots = lax.broadcasted_iota(jnp.int32, (CAP, local), 1)

    def wanted_hits(q):
        row = jnp.concatenate([out_requests[q]] * (CAP // 8), 0)
        column = jnp.sum(jnp.where(eye, row, 0.0), 1, keepdims=True).astype(jnp.int32)
        return jnp.where(spots == column, 1.0, 0.0).astype(BF16)

    half_lane = lax.broadcasted_iota(jnp.int32, (CAP // 2, TOKS), 1) < D - TOKS

    def answer(c, carry):
        found = [wanted_hits(c * chunk + j) for j in range(chunk)]
        got = mm(jnp.concatenate(found, 0), table_low[...], 1, 1)
        got = jnp.concatenate([got, jnp.zeros((got.shape[0], 2 * TOKS - D), F32)], 1)
        for j in range(chunk):
            q = c * chunk + j
            part = got[j * CAP : (j + 1) * CAP]
            tail = part[:, TOKS:]
            rolled = pltpu.roll(tail[CAP // 2 :], D - TOKS, 1)
            packed = jnp.where(half_lane, tail[: CAP // 2], rolled)
            answers[q] = jnp.concatenate([part[:, :TOKS], packed], 0).astype(BF16)

            @pl.when(q != me)
            def _():
                row_copy(q, me).start()

        return carry

    lax.fori_loop(0, count // chunk, answer, 0)
    landed[me] = answers[me]

    over_peers(n, narrow, end_narrow)
    outs = (out_qkv, out_proj, out_in, out_down)
    for q in range(narrow):
        held = gat[q].reshape(wide * rows_pad, total)
        for l in range(L):
            matrix = mm(held, pick_ref[l], 0, 0).astype(BF16)
            for which in ORDER:
                size = ROWS_OF[which] // narrow
                outs[which][l, q * size : (q + 1) * size] = matrix[
                    offsets[which] : offsets[which] + size
                ]

    requests = out_requests[...]
    reached = jnp.max(requests, 0)
    summed = jnp.sum(requests, 0)
    lane = lax.broadcasted_iota(jnp.int32, (8, TOKS), 1)
    out_stats[...] = jnp.where(lane == CAP, reached, summed)

    over_peers(me, count, lambda p: row_copy(p, p).wait_recv())

    def unpack(q, carry):
        part = landed[q].astype(F32)
        out_rows[q, :, :TOKS] = part[:CAP].astype(BF16)
        tail = part[CAP:]
        spread = jnp.concatenate([tail, pltpu.roll(tail, D - TOKS, 1)], 0)
        out_rows[q, :, TOKS:] = spread[:, : D - TOKS].astype(BF16)
        return carry

    lax.fori_loop(0, count, unpack, 0)

    def drain_wide(p):
        for copy in wide_copy(p, w):
            copy.wait_send()

    def drain_narrow(p):
        for copy in narrow_copy(p, n):
            copy.wait_send()

    over_peers(w, wide, drain_wide)
    over_peers(n, narrow, drain_narrow)
    over_peers(me, count, lambda p: ask_copy(p, me).wait_send())
    over_peers(me, count, lambda p: row_copy(p, me).wait_send())


def gather_call(index_row, cell_mask, shards_t, small_t, table_t, wide, narrow):
    count = wide * narrow
    width = small_t.shape[0]
    rows_pad = up_to(L * width, 16)
    small_pad = up_to(width, 8)
    _, total = quarter_offsets(narrow)
    pick = np.zeros((L, wide * rows_pad, D), np.float32)
    for l in range(L):
        for block in range(wide):
            for c in range(width):
                pick[l, block * rows_pad + l * width + c, block * width + c] = 1.0
    local = table_t.shape[1]
    entries = index_row.shape[1]
    shape = jax.ShapeDtypeStruct
    outs = [shape((L, rows, D), BF16) for rows in ROWS_OF] + [
        shape((narrow, wide, small_pad, TOKS), F32),
        shape((count, CAP, D), BF16),
        shape((1, entries), jnp.int32),
        shape((count, 8, TOKS), F32),
        shape((8, TOKS), F32),
    ]
    vmem = pl.BlockSpec(memory_space=pltpu.VMEM)
    dma = pltpu.SemaphoreType.DMA
    return pl.pallas_call(
        functools.partial(gather_kernel, wide=wide, narrow=narrow, chunk=8),
        out_shape=outs,
        in_specs=[vmem] * 9,
        out_specs=[vmem] * len(outs),
        scratch_shapes=[
            pltpu.VMEM((narrow, wide, rows_pad, total), BF16),
            pltpu.VMEM((count, 8, TOKS), F32),
            pltpu.VMEM((D, local), BF16),
            pltpu.VMEM((count, PACK, TOKS), BF16),
            pltpu.VMEM((count, PACK, TOKS), BF16),
            dma((wide,)), dma((wide,)), dma((narrow,)), dma((narrow,)),
            dma((wide,)), dma((wide,)), dma((narrow,)), dma((narrow,)),
            dma((count,)), dma((count,)), dma((count,)), dma((count,)),
        ],
        compiler_params=pltpu.CompilerParams(
            collective_id=0, has_side_effects=True, vmem_limit_bytes=56 << 20
        ),
        name="gather",
    )(index_row, cell_mask, *shards_t, small_t, table_t, jnp.asarray(pick, BF16))


def lanes(vector, width):
    return jnp.concatenate([vector] * (width // vector.shape[1]), 1)


def fold(value):
    total = value[:, :TOKS]
    for start in range(TOKS, value.shape[1], TOKS):
        total = total + value[:, start : start + TOKS]
    return total


def norm_forward(value, gain, shift):
    center = value - jnp.sum(value, 0, keepdims=True) * (1.0 / D)
    spread = jnp.sum(center * center, 0, keepdims=True) * (1.0 / D)
    inverse = lax.rsqrt(spread + NORM_EPS)
    unit = center * inverse
    return unit, inverse, unit * gain + shift


def norm_backward(unit, inverse, grad_unit):
    mean_one = jnp.sum(grad_unit, 0, keepdims=True) * (1.0 / D)
    mean_two = jnp.sum(grad_unit * unit, 0, keepdims=True) * (1.0 / D)
    return inverse * (grad_unit - mean_one - unit * mean_two)


NVEC = 8 * L + 3


def model_kernel(
    count_ref, rows_ref, slots_ref, coef_ref, num_ref, mask_ref, labels_ref,
    qkv_ref, proj_ref, in_ref, down_ref, small_ref,
    loss_ref, dmats_ref, dsmall_ref, dslots_ref,
    rows_t, qkv_t, proj_t, in_t, down_t, tok_s, scale_s, rec_s, class_s, class_t_s,
    dtok_s, dscale_s, drec_s, dclass_s, slots_acc,
    vecb, probs_s, unit_one_s, inv_one_s, normed_s, q_s, k_s, v_s, mixed_s,
    unit_two_s, inv_two_s, normed_two_s, gate_s, hidden_s, acc_s, hits_s,
    *, pair, wide, narrow,
):
    width = pair * TOKS
    blocks = slots_ref.shape[0]
    columns = D // wide
    own_rows = NSR // narrow
    slots = rows_ref.shape[0]
    offsets, total = quarter_offsets(narrow)
    inv_count = 1.0 / count_ref[0, 0]

    rows_t[...] = jnp.transpose(rows_ref[...].astype(F32)).astype(BF16)
    for l in range(L):
        qkv_t[l] = jnp.transpose(qkv_ref[l].astype(F32)).astype(BF16)
        proj_t[l] = jnp.transpose(proj_ref[l].astype(F32)).astype(BF16)
        in_t[l] = jnp.transpose(in_ref[l].astype(F32)).astype(BF16)
        down_t[l] = jnp.transpose(down_ref[l].astype(F32)).astype(BF16)
    pieces = []
    for n in range(narrow):
        if small_ref.shape[2] == columns:
            piece = small_ref[n].reshape(D, TOKS)
        else:
            piece = jnp.concatenate([small_ref[n, w, :columns] for w in range(wide)], 0)
        pieces.append(piece[:, :own_rows])
    small = jnp.concatenate(pieces, 1)
    for i in range(NVEC):
        at = i if i < 8 * L else (OFF_FIN + i - 8 * L if i < 8 * L + 2 else OFF_SCALE + NUMF)
        vecb[i] = jnp.broadcast_to(small[:, at : at + 1], (D, TOKS))
    gap_one = jnp.zeros((D, 1), F32)
    gap_end = jnp.zeros((D, TOKS - 1 - NUMF), F32)
    tok_s[...] = small[:, 8 * L : OFF_SCALE]
    scale_s[...] = jnp.concatenate([gap_one, small[:, OFF_SCALE : OFF_SCALE + NUMF], gap_end], 1)
    rec_s[...] = jnp.concatenate([gap_one, small[:, OFF_FIN + 2 + NCLASS :], gap_end], 1)
    class_t = jnp.concatenate(
        [small[:, OFF_FIN + 2 : OFF_FIN + 2 + NCLASS], jnp.zeros((D, TOKS - NCLASS), F32)], 1
    )
    class_s[...] = jnp.transpose(class_t)[:16].astype(BF16)
    class_t_s[...] = jnp.concatenate([class_t[:, :16]] * 3, 1).astype(BF16)
    for ref in (loss_ref, dmats_ref, dtok_s, dscale_s, drec_s, dclass_s, acc_s, slots_acc):
        ref[...] = jnp.zeros_like(ref)

    def vec(i):
        return lanes(vecb[i], width)

    def head_rows(value, h, b):
        return value[h * HD : h * HD + HD, b * TOKS : b * TOKS + TOKS]

    def add_mats(l, which, value):
        size = ROWS_OF[which] // narrow
        for n in range(narrow):
            at = l * total + offsets[which]
            dmats_ref[n, at : at + size] += value[n * size : (n + 1) * size]

    def add_vec(i, value):
        acc_s[i] += fold(value)

    def forward(l, x):
        base = 8 * l
        unit, inverse, normed = norm_forward(x, vec(base), vec(base + 1))
        normed = normed.astype(BF16)
        unit_one_s[l] = unit
        inv_one_s[l] = inverse
        normed_s[l] = normed
        joined = mm(qkv_ref[l], normed)
        q_f = joined[:D] + vec(base + 4)
        k_f = joined[D : 2 * D]
        v_f = joined[2 * D :] + vec(base + 5)
        mixed_cols = []
        for b in range(pair):
            rows = []
            for h in range(HEADS):
                qh = head_rows(q_f, h, b).astype(BF16)
                kh = head_rows(k_f, h, b).astype(BF16)
                vh = head_rows(v_f, h, b).astype(BF16)
                u = b * HEADS + h
                q_s[l, u] = qh
                k_s[l, u] = kh
                v_s[l, u] = vh
                scores = mm(kh, qh, 0, 0)
                top = jnp.max(scores, 0, keepdims=True)
                weight = jnp.exp((scores - top) * SCALE)
                probs = weight * (1.0 / jnp.sum(weight, 0, keepdims=True))
                probs_s[l, u] = probs
                rows.append(mm(vh, probs.astype(BF16)))
            mixed_cols.append(jnp.concatenate(rows, 0))
        mixed = jnp.concatenate(mixed_cols, 1).astype(BF16)
        mixed_s[l] = mixed
        after = x + mm(proj_ref[l], mixed) + vec(base + 6)
        unit, inverse, normed = norm_forward(after, vec(base + 2), vec(base + 3))
        normed = normed.astype(BF16)
        unit_two_s[l] = unit
        inv_two_s[l] = inverse
        normed_two_s[l] = normed
        gate_up = mm(in_ref[l], normed)
        gate_s[l] = gate_up
        gate, up = gate_up[:FF], gate_up[FF:]
        inner = GELU_A * (gate + GELU_B * gate * gate * gate)
        hidden = (0.5 * gate * (1.0 + jnp.tanh(inner)) * up).astype(BF16)
        hidden_s[l] = hidden
        return after + mm(down_t[l], hidden) + vec(base + 7)

    def backward(l, dout):
        base = 8 * l
        add_vec(base + 7, dout)
        up_low = dout.astype(BF16)
        add_mats(l, 3, mm(hidden_s[l], up_low, 1, 1))
        dhidden = mm(down_ref[l], up_low)
        gate, up = gate_s[l, :FF], gate_s[l, FF:]
        square = gate * gate
        tanh = jnp.tanh(GELU_A * (gate + GELU_B * square * gate))
        half = 0.5 * (1.0 + tanh)
        slope = half + 0.5 * gate * (1.0 - tanh * tanh) * (GELU_A * (1.0 + 3.0 * GELU_B * square))
        dgate = dhidden * up * slope
        dup = dhidden * (gate * half)
        dgl = jnp.concatenate([dgate, dup], 0).astype(BF16)
        add_mats(l, 2, mm(dgl, normed_two_s[l], 1, 1))
        dnormed = mm(in_t[l], dgl)
        unit = unit_two_s[l]
        add_vec(base + 2, dnormed * unit)
        add_vec(base + 3, dnormed)
        dafter = dout + norm_backward(unit, inv_two_s[l], dnormed * vec(base + 2))
        add_vec(base + 6, dafter)
        after_low = dafter.astype(BF16)
        add_mats(l, 1, mm(after_low, mixed_s[l], 1, 1))
        dmixed = mm(proj_t[l], after_low)
        q_cols, k_cols, v_cols = [], [], []
        for b in range(pair):
            q_rows, k_rows, v_rows = [], [], []
            for h in range(HEADS):
                u = b * HEADS + h
                dm = head_rows(dmixed, h, b).astype(BF16)
                probs = probs_s[l, u]
                dprobs = mm(v_s[l, u], dm, 0, 0)
                v_rows.append(mm(dm, probs.astype(BF16), 1, 1))
                inner = jnp.sum(dprobs * probs, 0, keepdims=True)
                dscores = (probs * (dprobs - inner) * SCALE).astype(BF16)
                q_rows.append(mm(k_s[l, u], dscores))
                k_rows.append(mm(q_s[l, u], dscores, 1, 1))
            q_cols.append(jnp.concatenate(q_rows, 0))
            k_cols.append(jnp.concatenate(k_rows, 0))
            v_cols.append(jnp.concatenate(v_rows, 0))
        dq = jnp.concatenate(q_cols, 1)
        dk = jnp.concatenate(k_cols, 1)
        dv = jnp.concatenate(v_cols, 1)
        add_vec(base + 4, dq)
        add_vec(base + 5, dv)
        dj = jnp.concatenate([dq, dk, dv], 0).astype(BF16)
        add_mats(l, 0, mm(dj, normed_s[l], 1, 1))
        dnormed = mm(qkv_t[l], dj)
        unit = unit_one_s[l]
        add_vec(base, dnormed * unit)
        add_vec(base + 1, dnormed)
        return dafter + norm_backward(unit, inv_one_s[l], dnormed * vec(base))

    def step(i, carry):
        coef = coef_ref[i]
        num = num_ref[i]
        mask = mask_ref[i]
        slot = lax.broadcasted_iota(jnp.int32, (slots, width), 0)
        hits_s[...] = jnp.where(slot == slots_ref[i], 1.0, 0.0).astype(BF16)
        x = mm(rows_t[...], hits_s[...]) + lanes(tok_s[...], width)
        x = x + coef * lanes(scale_s[...], width) + mask * vec(8 * L + 2)
        for l in range(L):
            x = forward(l, x)
        unit, inverse, final = norm_forward(x, vec(8 * L), vec(8 * L + 1))
        rec = lanes(rec_s[...], width)
        error = jnp.sum(final * rec, 0, keepdims=True) - num
        final_low = final.astype(BF16)
        logits = mm(class_s[...], final_low)
        row = lax.broadcasted_iota(jnp.int32, logits.shape, 0)
        lane = lax.broadcasted_iota(jnp.int32, logits.shape, 1)
        live = row < NCLASS
        logits = jnp.where(live, logits, -1e30)
        top = jnp.max(logits, 0, keepdims=True)
        weight = jnp.where(live, jnp.exp(logits - top), 0.0)
        sums = jnp.sum(weight, 0, keepdims=True)
        first = (lane % TOKS) == 0
        hit = jnp.where(first & (row == labels_ref[i]), 1.0, 0.0)
        firsts = jnp.where(first[:1], 1.0, 0.0)
        picked = jnp.sum(jnp.where(hit > 0, logits, 0.0), 0, keepdims=True)
        loss_ref[...] += fold(mask * error * error + firsts * (top + jnp.log(sums)) - picked)
        dlogits = (firsts * weight / sums - hit) * inv_count
        dpredict = (2.0 * inv_count) * mask * error
        parts = jnp.concatenate([p.astype(F32) for p in split_three(dlogits)], 0).astype(BF16)
        dclass_s[...] += mm(final_low, parts, 1, 1)
        drec_s[...] += fold(final * dpredict)
        dfinal = rec * dpredict + mm(class_t_s[...], parts)
        add_vec(8 * L, dfinal * unit)
        add_vec(8 * L + 1, dfinal)
        dx = norm_backward(unit, inverse, dfinal * vec(8 * L))
        for l in reversed(range(L)):
            dx = backward(l, dx)
        dtok_s[...] += fold(dx)
        dscale_s[...] += fold(coef * dx)
        acc_s[8 * L + 2] += fold(mask * dx)
        slots_acc[...] += mm(hits_s[...], dx.astype(BF16), 1, 1)
        return carry

    lax.fori_loop(0, blocks, step, 0)

    dvec = [jnp.sum(acc_s[i], 1, keepdims=True) for i in range(NVEC)]
    dclass = dclass_s[...]
    dclass = dclass[:, :16] + dclass[:, 16:32] + dclass[:, 32:]
    dsmall = jnp.concatenate(
        dvec[: 8 * L]
        + [dtok_s[...], dscale_s[:, 1 : 1 + NUMF], dvec[8 * L + 2]]
        + dvec[8 * L : 8 * L + 2]
        + [dclass[:, :NCLASS], drec_s[:, 1 : 1 + NUMF]],
        1,
    )
    blank = jnp.zeros((D, TOKS - own_rows), F32)
    for n in range(narrow):
        piece = jnp.concatenate([dsmall[:, n * own_rows : (n + 1) * own_rows], blank], 1)
        if dsmall_ref.shape[2] == columns:
            dsmall_ref[n] = piece.reshape(wide, columns, TOKS)
        else:
            dsmall_ref[n] = jnp.zeros(dsmall_ref.shape[1:], F32)
            for w in range(wide):
                dsmall_ref[n, w, :columns] = piece[w * columns : (w + 1) * columns]

    half_lane = lax.broadcasted_iota(jnp.int32, (CAP // 2, TOKS), 1) < D - TOKS

    def pack(q, carry):
        at = pl.multiple_of(q * CAP, CAP)
        part = slots_acc[pl.ds(at, CAP), :]
        tail = jnp.concatenate([part[:, TOKS:], jnp.zeros((CAP, 2 * TOKS - D), F32)], 1)
        rolled = pltpu.roll(tail[CAP // 2 :], D - TOKS, 1)
        packed = jnp.where(half_lane, tail[: CAP // 2], rolled)
        dslots_ref[q] = jnp.concatenate([part[:, :TOKS], packed], 0)
        return carry

    lax.fori_loop(0, slots // CAP, pack, 0)


def model_call(count, rows, slots, coef, num, mask, labels, mats, small, pair, wide, narrow):
    blocks, _, width = slots.shape
    used = rows.shape[0]
    _, total = quarter_offsets(narrow)
    shape = jax.ShapeDtypeStruct
    outs = [
        shape((1, TOKS), F32),
        shape((narrow, L * total, D), F32),
        shape(small.shape, F32),
        shape((used // CAP, PACK, TOKS), F32),
    ]
    units = pair * HEADS
    vm = pltpu.VMEM
    scratch = [
        vm((D, used), BF16),
        vm((L, D, 3 * D), BF16), vm((L, D, D), BF16), vm((L, D, 2 * FF), BF16), vm((L, D, FF), BF16),
        vm((D, TOKS), F32), vm((D, TOKS), F32), vm((D, TOKS), F32), vm((16, D), BF16), vm((D, 48), BF16),
        vm((D, TOKS), F32), vm((D, TOKS), F32), vm((D, TOKS), F32), vm((D, 48), F32), vm((used, D), F32),
        vm((NVEC, D, TOKS), F32), vm((L, units, TOKS, TOKS), F32),
        vm((L, D, width), F32), vm((L, 1, width), F32), vm((L, D, width), BF16),
        vm((L, units, HD, TOKS), BF16), vm((L, units, HD, TOKS), BF16), vm((L, units, HD, TOKS), BF16),
        vm((L, D, width), BF16),
        vm((L, D, width), F32), vm((L, 1, width), F32), vm((L, D, width), BF16),
        vm((L, 2 * FF, width), F32), vm((L, FF, width), BF16),
        vm((NVEC, D, TOKS), F32), vm((used, width), BF16),
    ]
    spec = pl.BlockSpec(memory_space=pltpu.VMEM)
    return pl.pallas_call(
        functools.partial(model_kernel, pair=pair, wide=wide, narrow=narrow),
        out_shape=outs,
        in_specs=[pl.BlockSpec(memory_space=pltpu.SMEM)] + [spec] * 11,
        out_specs=[spec] * len(outs),
        scratch_shapes=scratch,
        compiler_params=pltpu.CompilerParams(vmem_limit_bytes=58 << 20),
        name="model",
    )(count, rows, slots, coef, num, mask, labels, *mats, small)


def levels_of(size):
    return size.bit_length() - 1


def reduce_kernel(
    *refs, wide, narrow, chunk,
):
    levels = levels_of(narrow)
    dmats_ref, dsmall_ref, dslots_ref, requests_ref = refs[:4]
    out_grad, out_small, out_table = refs[4:7]
    rest = list(refs[7:])
    mats_held = [dmats_ref] + [rest.pop(0) for _ in range(levels)]
    mats_came = [rest.pop(0) for _ in range(levels)]
    small_held = [dsmall_ref] + [rest.pop(0) for _ in range(levels)]
    small_came = [rest.pop(0) for _ in range(levels)]
    (
        landed, mats_landed, small_landed,
        slot_send, slot_recv, mats_send, mats_recv, small_send, small_recv,
        block_send, block_recv, own_send, own_recv,
    ) = rest
    count = wide * narrow
    w, n, me = place(wide, narrow)
    barrier = greet_all(me, count, narrow)
    offsets, total = quarter_offsets(narrow)
    stride = wide // (4 * L)
    local = out_table.shape[1]

    def over_peers(origin, size, body):
        def run(k, carry):
            body(lax.rem(origin + k, size))
            return carry

        lax.fori_loop(1, size, run, 0)

    def slot_copy(p, slot):
        return pltpu.make_async_remote_copy(
            src_ref=dslots_ref.at[p], dst_ref=landed.at[slot], send_sem=slot_send.at[p],
            recv_sem=slot_recv.at[slot], device_id=(p // narrow, lax.rem(p, narrow)),
            device_id_type=MESH,
        )

    pl.semaphore_wait(barrier, count - 1)

    def level_copies(s):
        bit = lax.rem(n // (1 << s), 2)
        partner = n + (1 - 2 * bit) * (1 << s)
        copies = []
        for j in range(narrow >> (s + 1)):
            copies.append(
                pltpu.make_async_remote_copy(
                    src_ref=mats_held[s].at[2 * j + 1 - bit], dst_ref=mats_came[s].at[j],
                    send_sem=mats_send.at[s, j], recv_sem=mats_recv.at[s, j],
                    device_id=(w, partner), device_id_type=MESH,
                )
            )
            copies.append(
                pltpu.make_async_remote_copy(
                    src_ref=small_held[s].at[2 * j + 1 - bit], dst_ref=small_came[s].at[j],
                    send_sem=small_send.at[s, j], recv_sem=small_recv.at[s, j],
                    device_id=(w, partner), device_id_type=MESH,
                )
            )
        return bit, copies

    for s in range(levels):
        bit, copies = level_copies(s)
        for copy in copies:
            copy.start()
        if s == 0:
            over_peers(me, count, lambda p: slot_copy(p, me).start())
            landed[me] = dslots_ref[me]
        for copy in copies:
            copy.wait_recv()
        for j in range(narrow >> (s + 1)):
            mats_held[s + 1][j] = mats_held[s][2 * j + bit] + mats_came[s][j]
            small_held[s + 1][j] = small_held[s][2 * j + bit] + small_came[s][j]

    def block_of(m):
        layer, which = m // 4, m % 4
        return layer * total + offsets[which], ROWS_OF[which] // narrow

    def block_copy(m, slot):
        start, size = block_of(m)
        return pltpu.make_async_remote_copy(
            src_ref=mats_held[levels].at[0, pl.ds(start, size)],
            dst_ref=mats_landed.at[slot, pl.ds(0, size)],
            send_sem=block_send.at[m], recv_sem=block_recv.at[slot],
            device_id=(m * stride, n), device_id_type=MESH,
        )

    def own_copy(p, slot):
        return pltpu.make_async_remote_copy(
            src_ref=small_held[levels].at[0, p], dst_ref=small_landed.at[slot],
            send_sem=own_send.at[p], recv_sem=own_recv.at[slot], device_id=(p, n),
            device_id_type=MESH,
        )

    for m in range(4 * L):
        @pl.when(w != m * stride)
        def _():
            block_copy(m, w).start()

    over_peers(w, wide, lambda p: own_copy(p, w).start())

    over_peers(me, count, lambda p: slot_copy(p, p).wait_recv())
    eye = lax.broadcasted_iota(jnp.int32, (CAP, TOKS), 0) == lax.broadcasted_iota(
        jnp.int32, (CAP, TOKS), 1
    )
    spots = lax.broadcasted_iota(jnp.int32, (CAP, local), 1)
    out_table[...] = jnp.zeros_like(out_table)

    def gather_terms(c, carry):
        hits, terms = [], []
        for j in range(chunk):
            q = c * chunk + j
            row = jnp.concatenate([requests_ref[q]] * (CAP // 8), 0)
            column = jnp.sum(jnp.where(eye, row, 0.0), 1, keepdims=True).astype(jnp.int32)
            hits.append(jnp.where(spots == column, 1.0, 0.0).astype(BF16))
            part = landed[q]
            tail = part[CAP:]
            spread = jnp.concatenate([tail, pltpu.roll(tail, D - TOKS, 1)], 0)
            terms.append(jnp.concatenate([part[:CAP], spread], 1))
        term = jnp.transpose(jnp.concatenate(terms, 0))[:D]
        high, low = split_two(term)
        hit = jnp.concatenate(hits, 0)
        out_table[...] += mm(high, hit) + mm(low, hit)
        return carry

    lax.fori_loop(0, count // chunk, gather_terms, 0)

    over_peers(w, wide, lambda p: own_copy(p, p).wait_recv())
    summed = small_held[levels][0, w]

    def add_small(k, value):
        return value + small_landed[lax.rem(w + k, wide)]

    out_small[...] = lax.fori_loop(1, wide, add_small, summed)
    out_grad[...] = jnp.zeros_like(out_grad)
    for m in range(4 * L):
        start, size = block_of(m)

        @pl.when(w == m * stride)
        def _():
            out_grad[:size, :D] = mats_held[levels][0, start : start + size]

            def add_block(k, carry):
                p = lax.rem(w + k, wide)
                block_copy(m, p).wait_recv()
                out_grad[:size, :D] += mats_landed[p, :size]
                return carry

            lax.fori_loop(1, wide, add_block, 0)

    for s in range(levels):
        for copy in level_copies(s)[1]:
            copy.wait_send()
    over_peers(me, count, lambda p: slot_copy(p, me).wait_send())
    over_peers(w, wide, lambda p: own_copy(p, w).wait_send())
    for m in range(4 * L):
        @pl.when(w != m * stride)
        def _():
            block_copy(m, w).wait_send()


def reduce_call(dmats, dsmall, dslots, requests, local, wide, narrow):
    count = wide * narrow
    levels = levels_of(narrow)
    shape = jax.ShapeDtypeStruct
    outs = [
        shape((2 * TOKS, 2 * TOKS), F32),
        shape(dsmall.shape[2:], F32),
        shape((D, local), F32),
    ]
    vm = pltpu.VMEM
    dma = pltpu.SemaphoreType.DMA

    def level_shapes(array):
        return [vm((narrow >> (s + 1),) + array.shape[1:], F32) for s in range(levels)]

    largest = max(ROWS_OF) // narrow
    spec = pl.BlockSpec(memory_space=pltpu.VMEM)
    return pl.pallas_call(
        functools.partial(reduce_kernel, wide=wide, narrow=narrow, chunk=8),
        out_shape=outs,
        in_specs=[spec] * 4,
        out_specs=[spec] * len(outs),
        scratch_shapes=level_shapes(dmats) * 2 + level_shapes(dsmall) * 2
        + [
            vm(dslots.shape, F32),
            vm((wide, largest, D), F32),
            vm((wide,) + dsmall.shape[2:], F32),
            dma((count,)), dma((count,)),
            dma((levels, narrow // 2)), dma((levels, narrow // 2)),
            dma((levels, narrow // 2)), dma((levels, narrow // 2)),
            dma((4 * L,)), dma((wide,)), dma((wide,)), dma((wide,)),
        ],
        compiler_params=pltpu.CompilerParams(
            collective_id=1, has_side_effects=True, vmem_limit_bytes=58 << 20
        ),
        name="reduce",
    )(dmats, dsmall, dslots, requests)


def adam_step(weight, gradient, first, second):
    first = BETA_ONE * first + (1.0 - BETA_ONE) * gradient
    second = BETA_TWO * second + (1.0 - BETA_TWO) * gradient * gradient
    ratio = first / (1.0 - BETA_ONE**STEP) / (jnp.sqrt(second / (1.0 - BETA_TWO**STEP)) + ADAM_EPS)
    return (weight - ADAM_RATE * (ratio + DECAY * weight), first, second)


def exact(left, right, left_dim=1, right_dim=0):
    return lax.dot_general(
        left, right, (((left_dim,), (right_dim,)), ((), ())), preferred_element_type=F32,
        precision=lax.Precision.HIGHEST,
    )


def update_kernel(*refs, wide, narrow):
    refs = list(refs)

    def take(number):
        head = refs[:number]
        del refs[:number]
        return head

    grad_ref, gsmall_ref, tgrad_ref, loss_ref = take(4)
    weights, moments = take(4), take(4)
    small_ref, small_one_ref, small_two_ref = take(3)
    (out_stats,) = take(1)
    out_weights, out_moments = take(4), take(4)
    out_small, out_one, out_two = take(3)
    norm_all, = take(1)
    mom_came, mom_sent, x_sent, x_came = take(4), take(4), take(4), take(4)
    x_start, x_end, gram_held, gram_came = take(4)
    (
        norm_send, norm_recv, get_send, get_recv, put_send, put_recv, new_send, new_recv,
        gram_send, gram_recv,
    ) = refs
    count = wide * narrow
    levels = levels_of(narrow)
    w, n, me = place(wide, narrow)
    barrier = greet_all(me, count, narrow)
    stride = wide // (4 * L)
    columns = D // wide

    def over_peers(origin, size, body):
        def run(k, carry):
            body(lax.rem(origin + k, size))
            return carry

        lax.fori_loop(1, size, run, 0)

    def total_of(value):
        return jnp.sum(jnp.sum(value, 0, keepdims=True), 1, keepdims=True)

    table_grad = tgrad_ref[...]
    squares = total_of(table_grad * table_grad)
    squares = squares + total_of(grad_ref[...] * grad_ref[...])
    squares = squares + total_of(gsmall_ref[...] * gsmall_ref[...])
    loss_here = jnp.sum(loss_ref[...], 1, keepdims=True)
    lane = lax.broadcasted_iota(jnp.int32, (8, TOKS), 1)
    norm_all[me] = jnp.where(lane == 0, squares, jnp.where(lane == 1, loss_here, 0.0))

    def norm_copy(p, slot):
        return pltpu.make_async_remote_copy(
            src_ref=norm_all.at[me], dst_ref=norm_all.at[slot], send_sem=norm_send.at[p],
            recv_sem=norm_recv.at[slot], device_id=(p // narrow, lax.rem(p, narrow)),
            device_id_type=MESH,
        )

    def get_copy(m, slot):
        return pltpu.make_async_remote_copy(
            src_ref=moments[m % 4].at[m // 4], dst_ref=mom_came[m % 4].at[slot],
            send_sem=get_send.at[m], recv_sem=get_recv.at[slot], device_id=(m * stride, n),
            device_id_type=MESH,
        )

    def put_copy(m, p):
        return pltpu.make_async_remote_copy(
            src_ref=mom_sent[m % 4].at[p], dst_ref=out_moments[m % 4].at[m // 4],
            send_sem=put_send.at[p], recv_sem=put_recv.at[m], device_id=(p, n),
            device_id_type=MESH,
        )

    def new_copy(m, p):
        return pltpu.make_async_remote_copy(
            src_ref=x_sent[m % 4].at[p], dst_ref=x_came[m % 4].at[m // 4],
            send_sem=new_send.at[p], recv_sem=new_recv.at[m], device_id=(p, n),
            device_id_type=MESH,
        )

    def gram_copy(s):
        bit = lax.rem(n // (1 << s), 2)
        partner = n + (1 - 2 * bit) * (1 << s)
        return pltpu.make_async_remote_copy(
            src_ref=gram_held.at[s], dst_ref=gram_came.at[s], send_sem=gram_send.at[s],
            recv_sem=gram_recv.at[s], device_id=(w, partner), device_id_type=MESH,
        )

    pl.semaphore_wait(barrier, count - 1)
    over_peers(me, count, lambda p: norm_copy(p, me).start())
    for m in range(4 * L):
        @pl.when(w != m * stride)
        def _():
            get_copy(m, w).start()

        @pl.when(w == m * stride)
        def _():
            mom_came[m % 4][w] = moments[m % 4][m // 4]

    over_peers(me, count, lambda p: norm_copy(p, p).wait_recv())
    sums = jnp.sum(norm_all[...], 0)
    norm = jnp.sqrt(sums)
    out_stats[...] = jnp.where(lane == 0, norm, sums)
    factor = CLIP / jnp.maximum(norm[:1, :1], CLIP)

    x_start[...] = jnp.zeros_like(x_start)

    def gather_rows(ref):
        if columns % 8 == 0:
            return ref[...].reshape(D, ref.shape[2])
        return jnp.concatenate([ref[p] for p in range(wide)], 0)

    def spread_rows(ref, value):
        if columns % 8 == 0:
            ref[...] = value.reshape(ref.shape)
        else:
            for p in range(wide):
                ref[p] = value[p * columns : (p + 1) * columns]

    grad_t = jnp.transpose(grad_ref[...])[:D]
    for m in range(4 * L):
        @pl.when(w == m * stride)
        def _():
            over_peers(w, wide, lambda p: get_copy(m, p).wait_recv())
            size = ROWS_OF[m % 4] // narrow
            moment = MOMENTUM * gather_rows(mom_came[m % 4]) + factor * grad_t[:, :size]
            x_start[:, :size] = moment
            spread_rows(mom_sent[m % 4], moment)
            over_peers(w, wide, lambda p: put_copy(m, p).start())
            out_moments[m % 4][m // 4] = mom_sent[m % 4][w]

    x = x_start[...]
    gram_held[0] = exact(x, x, 1, 1)
    for s in range(levels):
        gram_copy(s).start()
        if s == 0:
            weight, first, second = adam_step(
                small_ref[...], factor * gsmall_ref[:columns, : small_ref.shape[1]],
                small_one_ref[...], small_two_ref[...],
            )
            out_small[...] = weight
            out_one[...] = first
            out_two[...] = second
        gram_copy(s).wait_recv()
        gram_held[s + 1] = gram_held[s] + gram_came[s]
    gram = gram_held[levels]
    eye = jnp.where(
        lax.broadcasted_iota(jnp.int32, (D, D), 0) == lax.broadcasted_iota(jnp.int32, (D, D), 1),
        1.0, 0.0,
    )
    inverse = lax.rsqrt(total_of(eye * gram) + ORTHO_EPS)
    square = gram * (inverse * inverse)
    product = None
    for step in range(5):
        polynomial = NS_ONE * eye + NS_TWO * square + NS_THREE * exact(square, square)
        product = polynomial if product is None else exact(product, polynomial)
        if step < 4:
            square = exact(polynomial, exact(square, polynomial))
    x_end[...] = exact(product, x * inverse)
    for m in range(4 * L):
        @pl.when(w == m * stride)
        def _():
            size = ROWS_OF[m % 4] // narrow
            spread_rows(x_sent[m % 4], x_end[:, :size])
            over_peers(w, wide, lambda p: new_copy(m, p).start())
            x_came[m % 4][m // 4] = x_sent[m % 4][w]

    for m in range(4 * L):
        @pl.when(w != m * stride)
        def _():
            new_copy(m, w).wait_recv()

        which, layer = m % 4, m // 4
        scale = math.sqrt(max(1.0, ROWS_OF[which] / D))
        out_weights[which][layer] = (
            weights[which][layer] * (1.0 - MUON_RATE * DECAY)
            - MUON_RATE * scale * x_came[which][layer]
        )

    for m in range(4 * L):
        @pl.when(w != m * stride)
        def _():
            put_copy(m, w).wait_recv()
            get_copy(m, w).wait_send()

        @pl.when(w == m * stride)
        def _():
            over_peers(w, wide, lambda p: put_copy(m, p).wait_send())
            over_peers(w, wide, lambda p: new_copy(m, p).wait_send())

    for s in range(levels):
        gram_copy(s).wait_send()
    over_peers(me, count, lambda p: norm_copy(p, me).wait_send())


def update_call(grad, gsmall, tgrad, loss, weights, moments, smalls, wide, narrow):
    count = wide * narrow
    levels = levels_of(narrow)
    columns = D // wide
    shape = jax.ShapeDtypeStruct
    outs = [shape((8, TOKS), F32)]
    outs += [shape(a.shape, F32) for a in weights + moments + smalls]
    vm = pltpu.VMEM
    dma = pltpu.SemaphoreType.DMA
    blocks = [vm((wide, columns, rows // narrow), F32) for rows in ROWS_OF]
    layers = [vm((L, columns, rows // narrow), F32) for rows in ROWS_OF]
    spec = pl.BlockSpec(memory_space=pltpu.VMEM)
    return pl.pallas_call(
        functools.partial(update_kernel, wide=wide, narrow=narrow),
        out_shape=outs,
        in_specs=[spec] * 15,
        out_specs=[spec] * len(outs),
        scratch_shapes=[vm((count, 8, TOKS), F32)]
        + blocks * 3 + layers
        + [
            vm((D, 2 * TOKS), F32), vm((D, 2 * TOKS), F32),
            vm((levels + 1, D, D), F32), vm((levels, D, D), F32),
            dma((count,)), dma((count,)), dma((4 * L,)), dma((wide,)), dma((wide,)), dma((4 * L,)),
            dma((wide,)), dma((4 * L,)), dma((levels,)), dma((levels,)),
        ],
        compiler_params=pltpu.CompilerParams(
            collective_id=2, has_side_effects=True, vmem_limit_bytes=58 << 20
        ),
        name="update",
    )(grad, gsmall, tgrad, loss, *weights, *moments, *smalls)


def per_device(
    cat_index, num_values, cell_mask, labels, table, table_first, table_second,
    small, small_first, small_second, w_qkv, w_proj, w_in, w_down,
    mom_qkv, mom_proj, mom_in, mom_down,
):
    wide = lax.axis_size("wide")
    narrow = lax.axis_size("narrow")
    count = wide * narrow
    data_rows = num_values.shape[0]
    pair = 4 if count * CAP <= 2048 else 2
    while data_rows % pair:
        pair //= 2
    flip = lambda v: jnp.swapaxes(v, -1, -2)
    weights = [flip(v) for v in (w_qkv, w_proj, w_in, w_down)]
    moments = [flip(v) for v in (mom_qkv, mom_proj, mom_in, mom_down)]
    smalls = [flip(v) for v in (small, small_first, small_second)]
    table_t = flip(table)
    flat_index = cat_index.reshape(-1)
    entries = flat_index.shape[0]
    qkv, proj, w_in_all, down, small_all, rows, slots, requests, stats = gather_call(
        flat_index[None], cell_mask, weights, smalls[0], table_t, wide, narrow
    )
    rows = rows.reshape(count * CAP, D)
    over = stats[0, CAP] > 0.5
    hidden_count = stats[:1, CAP + 1 : CAP + 2]

    def general_rows(rows, slots):
        whole = lax.all_gather(table.astype(BF16), ("wide", "narrow"), axis=0, tiled=True)
        looked = jnp.take(whole, flat_index, axis=0)
        spare = jnp.zeros((rows.shape[0] - entries, D), BF16)
        return jnp.concatenate([looked, spare], 0), lax.iota(jnp.int32, entries)[None]

    rows, slots = lax.cond(over, general_rows, lambda r, s: (r, s), rows, slots)

    def spread(value, fill=0):
        value = jnp.pad(value, ((0, 0), (1, TOKS - 1 - NUMF)), constant_values=fill)
        return value.reshape(data_rows // pair, 1, pair * TOKS)

    masked = cell_mask.astype(F32)
    slot_rows = jnp.pad(
        slots.reshape(data_rows, CATF), ((0, 0), (TOKS - CATF, 0)), constant_values=-1
    ).reshape(data_rows // pair, 1, pair * TOKS)
    label_rows = jnp.broadcast_to(labels[:, None], (data_rows, TOKS)).reshape(
        data_rows // pair, 1, pair * TOKS
    )
    loss, dmats, dsmall, dslots = model_call(
        hidden_count, rows, slot_rows, spread((1.0 - masked) * num_values), spread(num_values),
        spread(masked), label_rows, (qkv, proj, w_in_all, down), small_all, pair, wide, narrow,
    )
    grad, gsmall, tgrad = reduce_call(dmats, dsmall, dslots, requests, table.shape[0], wide, narrow)

    def general_terms(tgrad, dslots):
        tail = dslots[:, CAP:]
        tail = jnp.concatenate([tail[:, :, : D - TOKS], tail[:, :, D - TOKS :]], 1)
        terms = jnp.concatenate([dslots[:, :CAP], tail], 2).reshape(count * CAP, D)[:entries]
        whole = count * table.shape[0]
        hits = (flat_index[:, None] == lax.iota(jnp.int32, whole)[None, :]).astype(BF16)
        sums = lax.psum_scatter(
            mm(hits, terms.astype(BF16), 0, 0), ("wide", "narrow"), scatter_dimension=0, tiled=True
        )
        return flip(sums)

    tgrad = lax.cond(over, general_terms, lambda t, d: t, tgrad, dslots)
    outs = update_call(grad, gsmall, tgrad, loss, weights, moments, smalls, wide, narrow)
    stats_end = outs[0]
    norm = stats_end[0, 0]
    factor = CLIP / jnp.maximum(norm, CLIP)
    new_table, table_one, table_two = adam_step(
        table, factor * flip(tgrad), table_first, table_second
    )
    new_weights = [flip(v) for v in outs[1:5]]
    new_moments = [flip(v) for v in outs[5:9]]
    new_smalls = [flip(v) for v in outs[9:12]]
    return (
        stats_end[0, 1], hidden_count[0, 0], norm, new_table, table_one, table_two,
        *new_smalls, *new_weights, *new_moments,
    )


def solution(mesh):
    rows = P(("wide", "narrow"), None)
    square = P("narrow", "wide")
    cube = P(None, "narrow", "wide")
    return jax.shard_map(
        per_device,
        mesh=mesh,
        in_specs=(rows, rows, rows, P(("wide", "narrow")), rows, rows, rows)
        + (square,) * 3 + (cube,) * 8,
        out_specs=(P(), P(), P(), rows, rows, rows) + (square,) * 3 + (cube,) * 8,
        check_vma=False,
    )
```

```python
import functools
import math

import jax
import jax.numpy as jnp
import numpy as np
from jax import lax
from jax.experimental import pallas as pl
from jax.experimental.pallas import tpu as pltpu
from jax.sharding import PartitionSpec as P

D = 192
HEADS = 8
HD = 24
FF = 256
L = 2
NUMF = 95
CATF = 32
NCLASS = 7
STEP = 10
TOKS = 128

NORM_EPS = 1e-05
CLIP = 0.002
BETA_ONE = 0.9
BETA_TWO = 0.95
ADAM_EPS = 1e-08
ADAM_RATE = 0.2
MUON_RATE = 1.0
MOMENTUM = 0.95
DECAY = 0.01
ORTHO_EPS = 1e-20
NS_ONE = 3.4445
NS_TWO = -4.775
NS_THREE = 2.0315
GELU_A = math.sqrt(2.0 / math.pi)
GELU_B = 0.044715
SCALE = HD ** (-0.5)

F32 = jnp.float32
BF16 = jnp.bfloat16
MESH = pl.DeviceIdType.MESH

ROWS_OF = (3 * D, D, 2 * FF, FF)
ORDER = (2, 0, 1, 3)
NSR = 8 * L + TOKS + NUMF + 1 + 2 + NCLASS + NUMF
OFF_SCALE = 8 * L + TOKS
OFF_FIN = OFF_SCALE + NUMF + 1
CAP = 32
PACK = CAP + CAP // 2


def mm(left, right, left_dim=1, right_dim=0):
    return lax.dot_general(
        left, right, (((left_dim,), (right_dim,)), ((), ())), preferred_element_type=F32
    )


def up_to(value, unit):
    return -(-value // unit) * unit


def split_two(value):
    high = value.astype(BF16)
    return high, (value - high.astype(F32)).astype(BF16)


def split_three(value):
    high = value.astype(BF16)
    rest = value - high.astype(F32)
    middle = rest.astype(BF16)
    return high, middle, (rest - middle.astype(F32)).astype(BF16)


def place(wide, narrow):
    w = lax.axis_index("wide")
    n = lax.axis_index("narrow")
    return w, n, w * narrow + n


def greet_all(me, count, narrow):
    barrier = pltpu.get_barrier_semaphore()

    def signal(k, carry):
        p = lax.rem(me + k, count)
        pl.semaphore_signal(
            barrier, inc=1, device_id=(p // narrow, lax.rem(p, narrow)), device_id_type=MESH
        )
        return carry

    lax.fori_loop(1, count, signal, 0)
    return barrier


def quarter_offsets(narrow):
    offsets, total = {}, 0
    for which in ORDER:
        offsets[which] = total
        total += ROWS_OF[which] // narrow
    return offsets, total


def gather_kernel(
    index_ref, mask_ref, qkv_ref, proj_ref, in_ref, down_ref, small_ref, table_ref, pick_ref,
    out_qkv, out_proj, out_in, out_down, out_small, out_rows, out_slots, out_requests, out_stats,
    gat, ask, table_low, answers, landed,
    wide_send, wide_recv, narrow_send, narrow_recv, swide_send, swide_recv, snarrow_send, snarrow_recv,
    ask_send, ask_recv, row_send, row_recv,
    *, wide, narrow, chunk,
):
    count = wide * narrow
    w, n, me = place(wide, narrow)
    barrier = greet_all(me, count, narrow)

    def coords(p):
        return (p // narrow, lax.rem(p, narrow))

    offsets, total = quarter_offsets(narrow)
    width = qkv_ref.shape[1]
    rows_pad = gat.shape[2]
    shards = (qkv_ref, proj_ref, in_ref, down_ref)
    pieces = [
        jnp.concatenate([shards[which][l] for which in ORDER], 1) for l in range(L)
    ]
    if rows_pad > L * width:
        pieces.append(jnp.zeros((rows_pad - L * width, total), F32))
    gat[n, w] = jnp.concatenate(pieces, 0).astype(BF16)
    small = small_ref[...]
    own_rows = small.shape[1]
    pieces = [small]
    if out_small.shape[2] > width:
        pieces = [jnp.concatenate([small, jnp.zeros((out_small.shape[2] - width, own_rows), F32)], 0)]
    out_small[n, w] = jnp.concatenate(
        pieces + [jnp.zeros((out_small.shape[2], TOKS - own_rows), F32)], 1
    )

    entries = index_ref.shape[1]
    local = table_ref.shape[1]
    index_row = index_ref[...]
    owner_row = jnp.zeros_like(index_row)
    for k in range(1, count):
        owner_row = owner_row + (index_row >= k * local).astype(jnp.int32)
    base_row = owner_row * local
    index_col = jnp.transpose(jnp.broadcast_to(index_row, (8, entries)))[:, :1]
    before = lax.broadcasted_iota(jnp.int32, (entries, entries), 0)
    after = lax.broadcasted_iota(jnp.int32, (entries, entries), 1)
    same = index_col == index_row
    first_col = 1.0 - jnp.max(jnp.where(same & (after < before), 1.0, 0.0), 1, keepdims=True)
    first_row = 1.0 - jnp.max(jnp.where(same & (before < after), 1.0, 0.0), 0, keepdims=True)
    lower = (index_col >= base_row) & (index_col < index_row)
    rank_row = jnp.sum(jnp.where(lower, first_col, 0.0), 0, keepdims=True).astype(jnp.int32)
    out_slots[...] = owner_row * CAP + rank_row
    over = jnp.max(jnp.where(rank_row >= CAP, 1.0, 0.0), 1, keepdims=True)
    hidden_cells = jnp.sum(jnp.sum(mask_ref[...].astype(F32), 0, keepdims=True), 1, keepdims=True)
    place_row = index_row - base_row
    owners = lax.broadcasted_iota(jnp.int32, (count, entries), 0)
    mine = jnp.where(owners == owner_row, first_row, 0.0)
    high = lax.shift_right_logical(place_row, 6)
    low = place_row - high * 64
    at_rank = jnp.where(
        lax.broadcasted_iota(jnp.int32, (TOKS, entries), 0) == rank_row, 1.0, 0.0
    ).astype(BF16)
    wanted = 64.0 * mm((mine * high.astype(F32)).astype(BF16), at_rank, 1, 1) + mm(
        (mine * low.astype(F32)).astype(BF16), at_rank, 1, 1
    )
    lane = lax.broadcasted_iota(jnp.int32, (count, TOKS), 1)
    wanted = jnp.where(lane < CAP, wanted, 0.0)
    wanted = jnp.where(lane == CAP, over, wanted)
    wanted = jnp.where(lane == CAP + 1, hidden_cells, wanted)
    for k in range(count):
        ask[k] = jnp.broadcast_to(wanted[k : k + 1], (8, TOKS))

    pl.semaphore_wait(barrier, count - 1)

    def wide_copy(p, slot):
        return (
            pltpu.make_async_remote_copy(
                src_ref=gat.at[n, w], dst_ref=gat.at[n, slot], send_sem=wide_send.at[p],
                recv_sem=wide_recv.at[slot], device_id=(p, n), device_id_type=MESH,
            ),
            pltpu.make_async_remote_copy(
                src_ref=out_small.at[n, w], dst_ref=out_small.at[n, slot], send_sem=swide_send.at[p],
                recv_sem=swide_recv.at[slot], device_id=(p, n), device_id_type=MESH,
            ),
        )

    def ask_copy(p, slot):
        return pltpu.make_async_remote_copy(
            src_ref=ask.at[p], dst_ref=out_requests.at[slot], send_sem=ask_send.at[p],
            recv_sem=ask_recv.at[slot], device_id=coords(p), device_id_type=MESH,
        )

    def narrow_copy(p, slot):
        return (
            pltpu.make_async_remote_copy(
                src_ref=gat.at[n], dst_ref=gat.at[slot], send_sem=narrow_send.at[p],
                recv_sem=narrow_recv.at[slot], device_id=(w, p), device_id_type=MESH,
            ),
            pltpu.make_async_remote_copy(
                src_ref=out_small.at[n], dst_ref=out_small.at[slot], send_sem=snarrow_send.at[p],
                recv_sem=snarrow_recv.at[slot], device_id=(w, p), device_id_type=MESH,
            ),
        )

    def row_copy(p, slot):
        return pltpu.make_async_remote_copy(
            src_ref=answers.at[p], dst_ref=landed.at[slot], send_sem=row_send.at[p],
            recv_sem=row_recv.at[slot], device_id=coords(p), device_id_type=MESH,
        )

    def over_peers(origin, size, body):
        def run(k, carry):
            body(lax.rem(origin + k, size))
            return carry

        lax.fori_loop(1, size, run, 0)

    def start_wide(p):
        for copy in wide_copy(p, w):
            copy.start()

    def end_wide(p):
        for copy in wide_copy(p, p):
            copy.wait_recv()

    def start_narrow(p):
        for copy in narrow_copy(p, n):
            copy.start()

    def end_narrow(p):
        for copy in narrow_copy(p, p):
            copy.wait_recv()

    over_peers(me, count, lambda p: ask_copy(p, me).start())
    over_peers(w, wide, start_wide)
    out_requests[me] = ask[me]
    table_low[...] = table_ref[...].astype(BF16)
    over_peers(w, wide, end_wide)
    over_peers(n, narrow, start_narrow)
    over_peers(me, count, lambda p: ask_copy(p, p).wait_recv())

    eye = lax.broadcasted_iota(jnp.int32, (CAP, TOKS), 0) == lax.broadcasted_iota(
        jnp.int32, (CAP, TOKS), 1
    )
    spots = lax.broadcasted_iota(jnp.int32, (CAP, local), 1)

    def wanted_hits(q):
        row = jnp.concatenate([out_requests[q]] * (CAP // 8), 0)
        column = jnp.sum(jnp.where(eye, row, 0.0), 1, keepdims=True).astype(jnp.int32)
        return jnp.where(spots == column, 1.0, 0.0).astype(BF16)

    half_lane = lax.broadcasted_iota(jnp.int32, (CAP // 2, TOKS), 1) < D - TOKS

    def answer(c, carry):
        found = [wanted_hits(c * chunk + j) for j in range(chunk)]
        got = mm(jnp.concatenate(found, 0), table_low[...], 1, 1)
        got = jnp.concatenate([got, jnp.zeros((got.shape[0], 2 * TOKS - D), F32)], 1)
        for j in range(chunk):
            q = c * chunk + j
            part = got[j * CAP : (j + 1) * CAP]
            tail = part[:, TOKS:]
            rolled = pltpu.roll(tail[CAP // 2 :], D - TOKS, 1)
            packed = jnp.where(half_lane, tail[: CAP // 2], rolled)
            answers[q] = jnp.concatenate([part[:, :TOKS], packed], 0).astype(BF16)

            @pl.when(q != me)
            def _():
                row_copy(q, me).start()

        return carry

    lax.fori_loop(0, count // chunk, answer, 0)
    landed[me] = answers[me]

    over_peers(n, narrow, end_narrow)
    outs = (out_qkv, out_proj, out_in, out_down)
    for q in range(narrow):
        held = gat[q].reshape(wide * rows_pad, total)
        for l in range(L):
            matrix = mm(held, pick_ref[l], 0, 0).astype(BF16)
            for which in ORDER:
                size = ROWS_OF[which] // narrow
                outs[which][l, q * size : (q + 1) * size] = matrix[
                    offsets[which] : offsets[which] + size
                ]

    requests = out_requests[...]
    reached = jnp.max(requests, 0)
    summed = jnp.sum(requests, 0)
    lane = lax.broadcasted_iota(jnp.int32, (8, TOKS), 1)
    out_stats[...] = jnp.where(lane == CAP, reached, summed)

    over_peers(me, count, lambda p: row_copy(p, p).wait_recv())

    def unpack(q, carry):
        part = landed[q].astype(F32)
        out_rows[q, :, :TOKS] = part[:CAP].astype(BF16)
        tail = part[CAP:]
        spread = jnp.concatenate([tail, pltpu.roll(tail, D - TOKS, 1)], 0)
        out_rows[q, :, TOKS:] = spread[:, : D - TOKS].astype(BF16)
        return carry

    lax.fori_loop(0, count, unpack, 0)

    def drain_wide(p):
        for copy in wide_copy(p, w):
            copy.wait_send()

    def drain_narrow(p):
        for copy in narrow_copy(p, n):
            copy.wait_send()

    over_peers(w, wide, drain_wide)
    over_peers(n, narrow, drain_narrow)
    over_peers(me, count, lambda p: ask_copy(p, me).wait_send())
    over_peers(me, count, lambda p: row_copy(p, me).wait_send())


def gather_call(index_row, cell_mask, shards_t, small_t, table_t, wide, narrow):
    count = wide * narrow
    width = small_t.shape[0]
    rows_pad = up_to(L * width, 16)
    small_pad = up_to(width, 8)
    _, total = quarter_offsets(narrow)
    pick = np.zeros((L, wide * rows_pad, D), np.float32)
    for l in range(L):
        for block in range(wide):
            for c in range(width):
                pick[l, block * rows_pad + l * width + c, block * width + c] = 1.0
    local = table_t.shape[1]
    entries = index_row.shape[1]
    shape = jax.ShapeDtypeStruct
    outs = [shape((L, rows, D), BF16) for rows in ROWS_OF] + [
        shape((narrow, wide, small_pad, TOKS), F32),
        shape((count, CAP, D), BF16),
        shape((1, entries), jnp.int32),
        shape((count, 8, TOKS), F32),
        shape((8, TOKS), F32),
    ]
    vmem = pl.BlockSpec(memory_space=pltpu.VMEM)
    dma = pltpu.SemaphoreType.DMA
    return pl.pallas_call(
        functools.partial(gather_kernel, wide=wide, narrow=narrow, chunk=8),
        out_shape=outs,
        in_specs=[vmem] * 9,
        out_specs=[vmem] * len(outs),
        scratch_shapes=[
            pltpu.VMEM((narrow, wide, rows_pad, total), BF16),
            pltpu.VMEM((count, 8, TOKS), F32),
            pltpu.VMEM((D, local), BF16),
            pltpu.VMEM((count, PACK, TOKS), BF16),
            pltpu.VMEM((count, PACK, TOKS), BF16),
            dma((wide,)), dma((wide,)), dma((narrow,)), dma((narrow,)),
            dma((wide,)), dma((wide,)), dma((narrow,)), dma((narrow,)),
            dma((count,)), dma((count,)), dma((count,)), dma((count,)),
        ],
        compiler_params=pltpu.CompilerParams(
            collective_id=0, has_side_effects=True, vmem_limit_bytes=56 << 20
        ),
        name="gather",
    )(index_row, cell_mask, *shards_t, small_t, table_t, jnp.asarray(pick, BF16))


def lanes(vector, width):
    return jnp.concatenate([vector] * (width // vector.shape[1]), 1)


def fold(value):
    total = value[:, :TOKS]
    for start in range(TOKS, value.shape[1], TOKS):
        total = total + value[:, start : start + TOKS]
    return total


def norm_forward(value, gain, shift):
    center = value - jnp.sum(value, 0, keepdims=True) * (1.0 / D)
    spread = jnp.sum(center * center, 0, keepdims=True) * (1.0 / D)
    inverse = lax.rsqrt(spread + NORM_EPS)
    unit = center * inverse
    return unit, inverse, unit * gain + shift


def norm_backward(unit, inverse, grad_unit):
    mean_one = jnp.sum(grad_unit, 0, keepdims=True) * (1.0 / D)
    mean_two = jnp.sum(grad_unit * unit, 0, keepdims=True) * (1.0 / D)
    return inverse * (grad_unit - mean_one - unit * mean_two)


NVEC = 8 * L + 3


def model_kernel(
    count_ref, rows_ref, slots_ref, coef_ref, num_ref, mask_ref, labels_ref,
    qkv_ref, proj_ref, in_ref, down_ref, small_ref,
    loss_ref, dmats_ref, dsmall_ref, dslots_ref,
    rows_t, qkv_t, proj_t, in_t, down_t, tok_s, scale_s, rec_s, class_s, class_t_s,
    dtok_s, dscale_s, drec_s, dclass_s, slots_acc,
    vecb, probs_s, unit_one_s, inv_one_s, normed_s, q_s, k_s, v_s, mixed_s,
    unit_two_s, inv_two_s, normed_two_s, gate_s, hidden_s, acc_s, hits_s, vt_s, wide_s, low_s, ds_s,
    qkv_acc, proj_acc, in_acc, down_acc,
    *, pair, wide, narrow,
):
    width = pair * TOKS
    blocks = slots_ref.shape[0]
    columns = D // wide
    own_rows = NSR // narrow
    slots = rows_ref.shape[0]
    offsets, _ = packed_offsets(narrow)
    mats_acc = (qkv_acc, proj_acc, in_acc, down_acc)
    inv_count = 1.0 / count_ref[0, 0]

    rows_t[...] = jnp.transpose(rows_ref[...].astype(F32)).astype(BF16)
    for l in range(L):
        qkv_t[l] = jnp.transpose(qkv_ref[l].astype(F32)).astype(BF16)
        proj_t[l] = jnp.transpose(proj_ref[l].astype(F32)).astype(BF16)
        in_t[l] = jnp.transpose(in_ref[l].astype(F32)).astype(BF16)
        down_t[l] = jnp.transpose(down_ref[l].astype(F32)).astype(BF16)
    pieces = []
    for n in range(narrow):
        if small_ref.shape[2] == columns:
            piece = small_ref[n].reshape(D, TOKS)
        else:
            piece = jnp.concatenate([small_ref[n, w, :columns] for w in range(wide)], 0)
        pieces.append(piece[:, :own_rows])
    small = jnp.concatenate(pieces, 1)
    for i in range(NVEC):
        at = i if i < 8 * L else (OFF_FIN + i - 8 * L if i < 8 * L + 2 else OFF_SCALE + NUMF)
        vecb[i] = jnp.broadcast_to(small[:, at : at + 1], (D, TOKS))
    gap_one = jnp.zeros((D, 1), F32)
    gap_end = jnp.zeros((D, TOKS - 1 - NUMF), F32)
    tok_s[...] = small[:, 8 * L : OFF_SCALE]
    scale_s[...] = jnp.concatenate([gap_one, small[:, OFF_SCALE : OFF_SCALE + NUMF], gap_end], 1)
    rec_s[...] = jnp.concatenate([gap_one, small[:, OFF_FIN + 2 + NCLASS :], gap_end], 1)
    class_t = jnp.concatenate(
        [small[:, OFF_FIN + 2 : OFF_FIN + 2 + NCLASS], jnp.zeros((D, TOKS - NCLASS), F32)], 1
    )
    class_s[...] = jnp.transpose(class_t)[:16].astype(BF16)
    class_t_s[...] = jnp.concatenate([class_t[:, :16]] * 3, 1).astype(BF16)
    for ref in (loss_ref, *mats_acc, dtok_s, dscale_s, drec_s, dclass_s, acc_s, slots_acc):
        ref[...] = jnp.zeros_like(ref)

    def vec(i):
        return lanes(vecb[i], width)

    def head_rows(value, h, b):
        return value[h * HD : h * HD + HD, b * TOKS : b * TOKS + TOKS]

    def head_mask(h):
        lane = lax.broadcasted_iota(jnp.int32, (1, D), 1)
        return jnp.where((lane >= h * HD) & (lane < h * HD + HD), 1.0, 0.0).astype(BF16)

    def add_mats(l, which, value):
        mats_acc[which][l] += value

    def add_vec(i, value):
        acc_s[i] += fold(value)

    def forward(l, x):
        base = 8 * l
        unit, inverse, normed = norm_forward(x, vec(base), vec(base + 1))
        normed = normed.astype(BF16)
        unit_one_s[l] = unit
        inv_one_s[l] = inverse
        normed_s[l] = normed
        joined = mm(qkv_ref[l], normed)
        q_f = joined[:D] + vec(base + 4)
        k_f = joined[D : 2 * D]
        v_f = joined[2 * D :] + vec(base + 5)
        k_t = jnp.transpose(k_f).astype(BF16)
        vt_s[l] = jnp.transpose(v_f).astype(BF16)
        q_low = q_f.astype(BF16)
        mixed_cols = []
        for b in range(pair):
            for h in range(HEADS):
                qh = head_rows(q_f, h, b).astype(BF16)
                kh = head_rows(k_f, h, b).astype(BF16)
                vh = head_rows(v_f, h, b).astype(BF16)
                u = b * HEADS + h
                q_s[l, u] = qh
                k_s[l, u] = kh
                v_s[l, u] = vh
                wide_s[u] = mm(k_t[b * TOKS : (b + 1) * TOKS] * head_mask(h), q_low[:, b * TOKS : (b + 1) * TOKS])
        for b in range(pair):
            for h in range(HEADS):
                u = b * HEADS + h
                scores = wide_s[u]
                top = jnp.max(scores, 0, keepdims=True)
                weight = jnp.exp((scores - top) * SCALE)
                probs = weight * (1.0 / jnp.sum(weight, 0, keepdims=True))
                probs_s[l, u] = probs
                low_s[l, u] = probs.astype(BF16)
        for b in range(pair):
            rows = []
            for h in range(HEADS):
                u = b * HEADS + h
                rows.append(mm(v_s[l, u], low_s[l, u]))
            mixed_cols.append(jnp.concatenate(rows, 0))
        mixed = jnp.concatenate(mixed_cols, 1).astype(BF16)
        mixed_s[l] = mixed
        after = x + mm(proj_ref[l], mixed) + vec(base + 6)
        unit, inverse, normed = norm_forward(after, vec(base + 2), vec(base + 3))
        normed = normed.astype(BF16)
        unit_two_s[l] = unit
        inv_two_s[l] = inverse
        normed_two_s[l] = normed
        gate_up = mm(in_ref[l], normed)
        gate_s[l] = gate_up
        gate, up = gate_up[:FF], gate_up[FF:]
        inner = GELU_A * (gate + GELU_B * gate * gate * gate)
        hidden = (0.5 * gate * (1.0 + jnp.tanh(inner)) * up).astype(BF16)
        hidden_s[l] = hidden
        return after + mm(down_t[l], hidden) + vec(base + 7)

    def backward(l, dout):
        base = 8 * l
        add_vec(base + 7, dout)
        up_low = dout.astype(BF16)
        add_mats(l, 3, mm(hidden_s[l], up_low, 1, 1))
        dhidden = mm(down_ref[l], up_low)
        gate, up = gate_s[l, :FF], gate_s[l, FF:]
        square = gate * gate
        tanh = jnp.tanh(GELU_A * (gate + GELU_B * square * gate))
        half = 0.5 * (1.0 + tanh)
        slope = half + 0.5 * gate * (1.0 - tanh * tanh) * (GELU_A * (1.0 + 3.0 * GELU_B * square))
        dgate = dhidden * up * slope
        dup = dhidden * (gate * half)
        dgl = jnp.concatenate([dgate, dup], 0).astype(BF16)
        add_mats(l, 2, mm(dgl, normed_two_s[l], 1, 1))
        dnormed = mm(in_t[l], dgl)
        unit = unit_two_s[l]
        add_vec(base + 2, dnormed * unit)
        add_vec(base + 3, dnormed)
        dafter = dout + norm_backward(unit, inv_two_s[l], dnormed * vec(base + 2))
        add_vec(base + 6, dafter)
        after_low = dafter.astype(BF16)
        add_mats(l, 1, mm(after_low, mixed_s[l], 1, 1))
        dmixed = mm(proj_t[l], after_low)
        dmixed_low = dmixed.astype(BF16)
        q_cols, k_cols, v_cols = [], [], []
        for b in range(pair):
            for h in range(HEADS):
                u = b * HEADS + h
                wide_s[u] = mm(vt_s[l, b * TOKS : (b + 1) * TOKS] * head_mask(h), dmixed_low[:, b * TOKS : (b + 1) * TOKS])
        for b in range(pair):
            for h in range(HEADS):
                u = b * HEADS + h
                probs = probs_s[l, u]
                dprobs = wide_s[u]
                inner = jnp.sum(dprobs * probs, 0, keepdims=True)
                ds_s[u] = (probs * (dprobs - inner) * SCALE).astype(BF16)
        for b in range(pair):
            q_rows, k_rows, v_rows = [], [], []
            for h in range(HEADS):
                u = b * HEADS + h
                dm = head_rows(dmixed, h, b).astype(BF16)
                v_rows.append(mm(dm, low_s[l, u], 1, 1))
                dscores = ds_s[u]
                q_rows.append(mm(k_s[l, u], dscores))
                k_rows.append(mm(q_s[l, u], dscores, 1, 1))
            q_cols.append(jnp.concatenate(q_rows, 0))
            k_cols.append(jnp.concatenate(k_rows, 0))
            v_cols.append(jnp.concatenate(v_rows, 0))
        dq = jnp.concatenate(q_cols, 1)
        dk = jnp.concatenate(k_cols, 1)
        dv = jnp.concatenate(v_cols, 1)
        add_vec(base + 4, dq)
        add_vec(base + 5, dv)
        dj = jnp.concatenate([dq, dk, dv], 0).astype(BF16)
        add_mats(l, 0, mm(dj, normed_s[l], 1, 1))
        dnormed = mm(qkv_t[l], dj)
        unit = unit_one_s[l]
        add_vec(base, dnormed * unit)
        add_vec(base + 1, dnormed)
        return dafter + norm_backward(unit, inv_one_s[l], dnormed * vec(base))

    def step(i, carry):
        coef = coef_ref[i]
        num = num_ref[i]
        mask = mask_ref[i]
        slot = lax.broadcasted_iota(jnp.int32, (slots, width), 0)
        hits_s[...] = jnp.where(slot == slots_ref[i], 1.0, 0.0).astype(BF16)
        x = mm(rows_t[...], hits_s[...]) + lanes(tok_s[...], width)
        x = x + coef * lanes(scale_s[...], width) + mask * vec(8 * L + 2)
        for l in range(L):
            x = forward(l, x)
        unit, inverse, final = norm_forward(x, vec(8 * L), vec(8 * L + 1))
        rec = lanes(rec_s[...], width)
        error = jnp.sum(final * rec, 0, keepdims=True) - num
        final_low = final.astype(BF16)
        logits = mm(class_s[...], final_low)
        row = lax.broadcasted_iota(jnp.int32, logits.shape, 0)
        lane = lax.broadcasted_iota(jnp.int32, logits.shape, 1)
        live = row < NCLASS
        logits = jnp.where(live, logits, -1e30)
        top = jnp.max(logits, 0, keepdims=True)
        weight = jnp.where(live, jnp.exp(logits - top), 0.0)
        sums = jnp.sum(weight, 0, keepdims=True)
        first = (lane % TOKS) == 0
        hit = jnp.where(first & (row == labels_ref[i]), 1.0, 0.0)
        firsts = jnp.where(first[:1], 1.0, 0.0)
        picked = jnp.sum(jnp.where(hit > 0, logits, 0.0), 0, keepdims=True)
        loss_ref[...] += fold(mask * error * error + firsts * (top + jnp.log(sums)) - picked)
        dlogits = (firsts * weight / sums - hit) * inv_count
        dpredict = (2.0 * inv_count) * mask * error
        parts = jnp.concatenate([p.astype(F32) for p in split_three(dlogits)], 0).astype(BF16)
        dclass_s[...] += mm(final_low, parts, 1, 1)
        drec_s[...] += fold(final * dpredict)
        dfinal = rec * dpredict + mm(class_t_s[...], parts)
        add_vec(8 * L, dfinal * unit)
        add_vec(8 * L + 1, dfinal)
        dx = norm_backward(unit, inverse, dfinal * vec(8 * L))
        for l in reversed(range(L)):
            dx = backward(l, dx)
        dtok_s[...] += fold(dx)
        dscale_s[...] += fold(coef * dx)
        acc_s[8 * L + 2] += fold(mask * dx)
        slots_acc[...] += mm(hits_s[...], dx.astype(BF16), 1, 1)
        return carry

    lax.fori_loop(0, blocks, step, 0)

    dvec = [jnp.sum(acc_s[i], 1, keepdims=True) for i in range(NVEC)]
    dclass = dclass_s[...]
    dclass = dclass[:, :16] + dclass[:, 16:32] + dclass[:, 32:]
    dsmall = jnp.concatenate(
        dvec[: 8 * L]
        + [dtok_s[...], dscale_s[:, 1 : 1 + NUMF], dvec[8 * L + 2]]
        + dvec[8 * L : 8 * L + 2]
        + [dclass[:, :NCLASS], drec_s[:, 1 : 1 + NUMF]],
        1,
    )
    blank = jnp.zeros((D, TOKS - own_rows), F32)
    for n in range(narrow):
        piece = jnp.concatenate([dsmall[:, n * own_rows : (n + 1) * own_rows], blank], 1)
        if dsmall_ref.shape[2] == columns:
            dsmall_ref[n] = piece.reshape(wide, columns, TOKS)
        else:
            dsmall_ref[n] = jnp.zeros(dsmall_ref.shape[1:], F32)
            for w in range(wide):
                dsmall_ref[n, w, :columns] = piece[w * columns : (w + 1) * columns]

    def beside(tail):
        rows = tail.shape[0]
        tail = jnp.concatenate([tail, jnp.zeros((rows, 2 * TOKS - D), F32)], 1)
        lane = lax.broadcasted_iota(jnp.int32, (rows // 2, TOKS), 1)
        return jnp.where(
            lane < D - TOKS, tail[: rows // 2], pltpu.roll(tail[rows // 2 :], D - TOKS, 1)
        )

    for which in range(4):
        size = ROWS_OF[which] // narrow
        for l in range(L):
            for n in range(narrow):
                part = mats_acc[which][l, n * size : (n + 1) * size]
                at = offsets[which]
                dmats_ref[l, n, at : at + size] = part[:, :TOKS]
                dmats_ref[l, n, at + size : at + size + size // 2] = beside(part[:, TOKS:])

    def pack(q, carry):
        at = pl.multiple_of(q * CAP, CAP)
        part = slots_acc[pl.ds(at, CAP), :]
        dslots_ref[q] = jnp.concatenate([part[:, :TOKS], beside(part[:, TOKS:])], 0).astype(BF16)
        return carry

    lax.fori_loop(0, slots // CAP, pack, 0)


def model_call(count, rows, slots, coef, num, mask, labels, mats, small, pair, wide, narrow):
    blocks, _, width = slots.shape
    used = rows.shape[0]
    _, total = packed_offsets(narrow)
    shape = jax.ShapeDtypeStruct
    outs = [
        shape((1, TOKS), F32),
        shape((L, narrow, total, TOKS), F32),
        shape(small.shape, F32),
        shape((used // CAP, PACK, TOKS), BF16),
    ]
    units = pair * HEADS
    vm = pltpu.VMEM
    scratch = [
        vm((D, used), BF16),
        vm((L, D, 3 * D), BF16), vm((L, D, D), BF16), vm((L, D, 2 * FF), BF16), vm((L, D, FF), BF16),
        vm((D, TOKS), F32), vm((D, TOKS), F32), vm((D, TOKS), F32), vm((16, D), BF16), vm((D, 48), BF16),
        vm((D, TOKS), F32), vm((D, TOKS), F32), vm((D, TOKS), F32), vm((D, 48), F32), vm((used, D), F32),
        vm((NVEC, D, TOKS), F32), vm((L, units, TOKS, TOKS), F32),
        vm((L, D, width), F32), vm((L, 1, width), F32), vm((L, D, width), BF16),
        vm((L, units, HD, TOKS), BF16), vm((L, units, HD, TOKS), BF16), vm((L, units, HD, TOKS), BF16),
        vm((L, D, width), BF16),
        vm((L, D, width), F32), vm((L, 1, width), F32), vm((L, D, width), BF16),
        vm((L, 2 * FF, width), F32), vm((L, FF, width), BF16),
        vm((NVEC, D, TOKS), F32), vm((used, width), BF16), vm((L, width, D), BF16), vm((units, TOKS, TOKS), F32), vm((L, units, TOKS, TOKS), BF16), vm((units, TOKS, TOKS), BF16),
        *[vm((L, rows, D), F32) for rows in ROWS_OF],
    ]
    spec = pl.BlockSpec(memory_space=pltpu.VMEM)
    return pl.pallas_call(
        functools.partial(model_kernel, pair=pair, wide=wide, narrow=narrow),
        out_shape=outs,
        in_specs=[pl.BlockSpec(memory_space=pltpu.SMEM)] + [spec] * 11,
        out_specs=[spec] * len(outs),
        scratch_shapes=scratch,
        compiler_params=pltpu.CompilerParams(vmem_limit_bytes=58 << 20),
        name="model",
    )(count, rows, slots, coef, num, mask, labels, *mats, small)


def levels_of(size):
    return size.bit_length() - 1


def packed_rows(which, narrow):
    size = ROWS_OF[which] // narrow
    return size + size // 2


def packed_offsets(narrow):
    offsets, total = [], 0
    for which in range(4):
        offsets.append(total)
        total += packed_rows(which, narrow)
    return offsets, total


def worker_of(m, wide):
    layer, kind = m // 4, m % 4
    return (layer * 2 + kind % 2) * (wide // 8) * 2 + kind // 2


def adam_step(weight, gradient, first, second):
    first = BETA_ONE * first + (1.0 - BETA_ONE) * gradient
    second = BETA_TWO * second + (1.0 - BETA_TWO) * gradient * gradient
    ratio = first / (1.0 - BETA_ONE**STEP) / (jnp.sqrt(second / (1.0 - BETA_TWO**STEP)) + ADAM_EPS)
    return (weight - ADAM_RATE * (ratio + DECAY * weight), first, second)


def exact(left, right, left_dim=1, right_dim=0):
    return lax.dot_general(
        left, right, (((left_dim,), (right_dim,)), ((), ())), preferred_element_type=F32,
        precision=lax.Precision.HIGHEST,
    )


def finish_kernel(*refs, wide, narrow):
    refs = list(refs)

    def take(number):
        head = refs[:number]
        del refs[:number]
        return head

    levels = levels_of(narrow)
    count = wide * narrow
    columns = D // wide
    dmats_ref, dsmall_ref, dslots_ref, requests_ref, extra_ref, loss_ref = take(6)
    weights, moments = take(4), take(4)
    small_ref, small_one_ref, small_two_ref = take(3)
    out_stats, out_table = take(2)
    out_weights, out_moments = take(4), take(4)
    out_small, out_one, out_two = take(3)
    steps = levels + 1
    mats_held = [take(steps) for _ in range(L)]
    mats_came = [take(steps) for _ in range(L)]
    small_held, small_came = take(levels), take(levels)
    landed, hits, mats_landed, small_landed, grad_s, extra_s = take(6)
    norm_all, = take(1)
    mom_came, mom_sent, x_sent, x_came = take(4), take(4), take(4), take(4)
    x_start, x_end, gram_held, gram_came = take(4)
    (
        slot_send, slot_recv, mats_send, mats_recv, small_send, small_recv,
        block_send, block_recv, own_send, own_recv,
        norm_send, norm_recv, get_send, get_recv, put_send, put_recv, new_send, new_recv,
        gram_send, gram_recv, extra_sem,
    ) = refs
    w, n, me = place(wide, narrow)
    barrier = greet_all(me, count, narrow)
    offsets, total = packed_offsets(narrow)
    half_rows = total // 2
    local = out_table.shape[1]
    side = lax.rem(w, 2)

    def over_peers(origin, size, body):
        def run(k, carry):
            body(lax.rem(origin + k, size))
            return carry

        lax.fori_loop(1, size, run, 0)

    def coords(p):
        return (p // narrow, lax.rem(p, narrow))

    def narrow_partner(s):
        bit = lax.rem(n // (1 << s), 2)
        return bit, n + (1 - 2 * bit) * (1 << s)

    def plan(l):
        if l % 2:
            return list(range(levels)) + ["side"]
        return [0, "side"] + list(range(1, levels)) if levels else ["side"]

    def before(l, t):
        return dmats_ref.at[l] if t == 0 else mats_held[l][t - 1]

    def step_copies(l, t):
        move = plan(l)[t]
        source = before(l, t)
        copies = []
        if move == "side":
            for j in range(source.shape[0]):
                copies.append(
                    pltpu.make_async_remote_copy(
                        src_ref=source.at[j, pl.ds((1 - side) * half_rows, half_rows)],
                        dst_ref=mats_came[l][t].at[j],
                        send_sem=mats_send.at[l, t, j], recv_sem=mats_recv.at[l, t, j],
                        device_id=(w + 1 - 2 * side, n), device_id_type=MESH,
                    )
                )
        else:
            bit, partner = narrow_partner(move)
            for j in range(source.shape[0] // 2):
                copies.append(
                    pltpu.make_async_remote_copy(
                        src_ref=source.at[2 * j + 1 - bit], dst_ref=mats_came[l][t].at[j],
                        send_sem=mats_send.at[l, t, j], recv_sem=mats_recv.at[l, t, j],
                        device_id=(w, partner), device_id_type=MESH,
                    )
                )
        return copies

    def step_add(l, t):
        move = plan(l)[t]
        source = before(l, t)
        for j in range(mats_held[l][t].shape[0]):
            if move == "side":
                mine = source[j, pl.ds(side * half_rows, half_rows)]
            else:
                mine = source[2 * j + narrow_partner(move)[0]]
            mats_held[l][t][j] = mine + mats_came[l][t][j]

    def small_before(s):
        return dsmall_ref if s == 0 else small_held[s - 1]

    def small_copies(s):
        bit, partner = narrow_partner(s)
        return [
            pltpu.make_async_remote_copy(
                src_ref=small_before(s).at[2 * j + 1 - bit], dst_ref=small_came[s].at[j],
                send_sem=small_send.at[s, j], recv_sem=small_recv.at[s, j],
                device_id=(w, partner), device_id_type=MESH,
            )
            for j in range(narrow >> (s + 1))
        ]

    def small_add(s):
        bit, _ = narrow_partner(s)
        for j in range(narrow >> (s + 1)):
            small_held[s][j] = small_before(s)[2 * j + bit] + small_came[s][j]

    def slot_copy(p, slot):
        return pltpu.make_async_remote_copy(
            src_ref=dslots_ref.at[p], dst_ref=landed.at[slot], send_sem=slot_send.at[p],
            recv_sem=slot_recv.at[slot], device_id=coords(p), device_id_type=MESH,
        )

    def block_copy(m, slot):
        layer, kind = m // 4, m % 4
        start = offsets[kind] - half_rows * (kind // 2)
        size = packed_rows(kind, narrow)
        return pltpu.make_async_remote_copy(
            src_ref=mats_held[layer][steps - 1].at[0, pl.ds(start, size)],
            dst_ref=mats_landed.at[slot, pl.ds(0, size)],
            send_sem=block_send.at[m], recv_sem=block_recv.at[slot],
            device_id=(worker_of(m, wide), n), device_id_type=MESH,
        )

    def own_copy(p, slot):
        return pltpu.make_async_remote_copy(
            src_ref=small_held[levels - 1].at[0, p], dst_ref=small_landed.at[slot],
            send_sem=own_send.at[p], recv_sem=own_recv.at[slot], device_id=(p, n),
            device_id_type=MESH,
        )

    def norm_copy(p, slot):
        return pltpu.make_async_remote_copy(
            src_ref=norm_all.at[me], dst_ref=norm_all.at[slot], send_sem=norm_send.at[p],
            recv_sem=norm_recv.at[slot], device_id=coords(p), device_id_type=MESH,
        )

    def get_copy(m, slot):
        return pltpu.make_async_remote_copy(
            src_ref=moments[m % 4].at[m // 4], dst_ref=mom_came[m % 4].at[slot],
            send_sem=get_send.at[m], recv_sem=get_recv.at[slot],
            device_id=(worker_of(m, wide), n), device_id_type=MESH,
        )

    def put_copy(m, p):
        return pltpu.make_async_remote_copy(
            src_ref=mom_sent[m % 4].at[p], dst_ref=out_moments[m % 4].at[m // 4],
            send_sem=put_send.at[p], recv_sem=put_recv.at[m], device_id=(p, n),
            device_id_type=MESH,
        )

    def new_copy(m, p):
        return pltpu.make_async_remote_copy(
            src_ref=x_sent[m % 4].at[p], dst_ref=x_came[m % 4].at[m // 4],
            send_sem=new_send.at[p], recv_sem=new_recv.at[m], device_id=(p, n),
            device_id_type=MESH,
        )

    def gram_copy(s):
        _, partner = narrow_partner(s)
        return pltpu.make_async_remote_copy(
            src_ref=gram_held.at[s], dst_ref=gram_came.at[s], send_sem=gram_send.at[s],
            recv_sem=gram_recv.at[s], device_id=(w, partner), device_id_type=MESH,
        )

    extra_copy = pltpu.make_async_copy(extra_ref, extra_s, extra_sem)
    extra_copy.start()

    pl.semaphore_wait(barrier, count - 1)
    for l in range(L):
        for copy in step_copies(l, 0):
            copy.start()
    for copy in small_copies(0):
        copy.start()
    over_peers(me, count, lambda p: slot_copy(p, me).start())
    landed[me] = dslots_ref[me]
    for m in range(4 * L):
        @pl.when(w != worker_of(m, wide))
        def _():
            get_copy(m, w).start()

        @pl.when(w == worker_of(m, wide))
        def _():
            mom_came[m % 4][w] = moments[m % 4][m // 4]

    eye = lax.broadcasted_iota(jnp.int32, (CAP, TOKS), 0) == lax.broadcasted_iota(
        jnp.int32, (CAP, TOKS), 1
    )
    spots = lax.broadcasted_iota(jnp.int32, (CAP, local), 1)

    def find(q, carry):
        row = jnp.broadcast_to(requests_ref[q][:1], (CAP, TOKS))
        column = jnp.sum(jnp.where(eye, row, 0.0), 1, keepdims=True).astype(jnp.int32)
        at = pl.multiple_of(q * CAP, CAP)
        hits[pl.ds(at, CAP), :] = jnp.where(spots == column, 1.0, 0.0).astype(BF16)
        return carry

    lax.fori_loop(0, count, find, 0)

    def finish_step(t):
        for l in range(L):
            for copy in step_copies(l, t):
                copy.wait_recv()
            step_add(l, t)
        if t < levels:
            for copy in small_copies(t):
                copy.wait_recv()
            small_add(t)
        if t + 1 < steps:
            for l in range(L):
                for copy in step_copies(l, t + 1):
                    copy.start()
        if t + 1 < levels:
            for copy in small_copies(t + 1):
                copy.start()

    finish_step(0)

    over_peers(me, count, lambda p: slot_copy(p, p).wait_recv())
    terms = landed[...].astype(F32)
    tail = terms[:, CAP:].reshape(count * (CAP // 2), TOKS)
    moved = pltpu.roll(tail, D - TOKS, 1).reshape(count, CAP // 2, TOKS)
    tail = jnp.concatenate([tail.reshape(count, CAP // 2, TOKS), moved], 1)
    head = terms[:, :CAP].reshape(count * CAP, TOKS)
    tail = tail.reshape(count * CAP, TOKS)
    terms_t = jnp.concatenate([jnp.transpose(head), jnp.transpose(tail)[: D - TOKS]], 0)
    if steps > 2:
        finish_step(1)
    extra_copy.wait()
    out_table[...] = extra_s[...] + mm(terms_t.astype(BF16), hits[...])
    for t in range(2 if steps > 2 else 1, steps):
        finish_step(t)

    over_peers(w, wide, lambda p: own_copy(p, w).start())
    for m in range(4 * L):
        kind = m % 4

        @pl.when((side == kind // 2) & (w != worker_of(m, wide)))
        def _():
            block_copy(m, w).start()

    table_grad = out_table[...]

    def total_of(value):
        return jnp.sum(jnp.sum(value, 0, keepdims=True), 1, keepdims=True)

    squares = total_of(table_grad * table_grad)
    loss_here = jnp.sum(loss_ref[...], 1, keepdims=True)
    x_start[...] = jnp.zeros_like(x_start)
    grad_s[...] = jnp.zeros_like(grad_s)

    over_peers(w, wide, lambda p: own_copy(p, p).wait_recv())

    def add_small(k, value):
        return value + small_landed[lax.rem(w + k, wide)]

    own_small = lax.fori_loop(1, wide, add_small, small_held[levels - 1][0, w])
    squares = squares + total_of(own_small * own_small)
    for m in range(4 * L):
        layer, kind = m // 4, m % 4

        @pl.when(w == worker_of(m, wide))
        def _():
            start = offsets[kind] - half_rows * (kind // 2)
            size = packed_rows(kind, narrow)
            whole = ROWS_OF[kind] // narrow

            def add_block(k, value):
                p = lax.rem(w // 2 + k, wide // 2) * 2 + side
                block_copy(m, p).wait_recv()
                return value + mats_landed[p, :size]

            packed = lax.fori_loop(
                1, wide // 2, add_block,
                mats_held[layer][steps - 1][0, start : start + size],
            )
            tail = packed[whole:]
            grad_s[:whole, :TOKS] = packed[:whole]
            grad_s[: whole // 2, TOKS : D] = tail[:, : D - TOKS]
            grad_s[whole // 2 : whole, TOKS : D] = tail[:, D - TOKS :]

    grad = grad_s[...]
    squares = squares + total_of(grad * grad)
    lane = lax.broadcasted_iota(jnp.int32, (1, TOKS), 1)
    norm_all[me] = jnp.where(lane == 0, squares, jnp.where(lane == 1, loss_here, 0.0))
    over_peers(me, count, lambda p: norm_copy(p, me).start())
    grad_t = jnp.transpose(grad)[:D]
    over_peers(me, count, lambda p: norm_copy(p, p).wait_recv())
    sums = jnp.sum(norm_all[...], 0)
    norm = jnp.sqrt(sums)
    out_stats[...] = jnp.where(lane == 0, norm, sums)
    factor = CLIP / jnp.maximum(norm[:, :1], CLIP)

    def gather_rows(ref):
        if columns % 8 == 0:
            return ref[...].reshape(D, ref.shape[2])
        return jnp.concatenate([ref[p] for p in range(wide)], 0)

    def spread_rows(ref, value):
        if columns % 8 == 0:
            ref[...] = value.reshape(ref.shape)
        else:
            for p in range(wide):
                ref[p] = value[p * columns : (p + 1) * columns]

    for m in range(4 * L):
        @pl.when(w == worker_of(m, wide))
        def _():
            over_peers(w, wide, lambda p: get_copy(m, p).wait_recv())
            size = ROWS_OF[m % 4] // narrow
            moment = MOMENTUM * gather_rows(mom_came[m % 4]) + factor * grad_t[:, :size]
            x_start[:, :size] = moment
            spread_rows(mom_sent[m % 4], moment)
            over_peers(w, wide, lambda p: put_copy(m, p).start())
            out_moments[m % 4][m // 4] = mom_sent[m % 4][w]

    x = x_start[...]
    gram = exact(x, x, 1, 1)
    rest = D - TOKS
    gram_held[0, :D] = gram[:, :TOKS]
    gram_held[0, D : D + rest] = jnp.concatenate(
        [gram[TOKS:, TOKS:], jnp.zeros((rest, TOKS - rest), F32)], 1
    )
    for s in range(levels):
        gram_copy(s).start()
        if s == 0:
            weight, first, second = adam_step(
                small_ref[...], factor * own_small[:columns, : small_ref.shape[1]],
                small_one_ref[...], small_two_ref[...],
            )
            out_small[...] = weight
            out_one[...] = first
            out_two[...] = second
        gram_copy(s).wait_recv()
        gram_held[s + 1] = gram_held[s] + gram_came[s]
    left = gram_held[levels, :D]
    corner = gram_held[levels, D : D + rest][:, :rest]
    above = jnp.transpose(
        jnp.concatenate([left[TOKS:], jnp.zeros((TOKS - rest, TOKS), F32)], 0)
    )[:, :rest]
    gram = jnp.concatenate([left, jnp.concatenate([above, corner], 0)], 1)
    eye = jnp.where(
        lax.broadcasted_iota(jnp.int32, (D, D), 0) == lax.broadcasted_iota(jnp.int32, (D, D), 1),
        1.0, 0.0,
    )
    inverse = lax.rsqrt(total_of(eye * gram) + ORTHO_EPS)
    square = gram * (inverse * inverse)
    product = None
    for step in range(5):
        polynomial = NS_ONE * eye + NS_TWO * square + NS_THREE * exact(square, square)
        product = polynomial if product is None else exact(product, polynomial)
        if step < 4:
            square = exact(polynomial, exact(square, polynomial))
    x_end[...] = exact(product, x * inverse)
    for m in range(4 * L):
        @pl.when(w == worker_of(m, wide))
        def _():
            size = ROWS_OF[m % 4] // narrow
            spread_rows(x_sent[m % 4], x_end[:, :size])
            over_peers(w, wide, lambda p: new_copy(m, p).start())
            x_came[m % 4][m // 4] = x_sent[m % 4][w]

    for m in range(4 * L):
        @pl.when(w != worker_of(m, wide))
        def _():
            new_copy(m, w).wait_recv()

        which, layer = m % 4, m // 4
        scale = math.sqrt(max(1.0, ROWS_OF[which] / D))
        out_weights[which][layer] = (
            weights[which][layer] * (1.0 - MUON_RATE * DECAY)
            - MUON_RATE * scale * x_came[which][layer]
        )

    for m in range(4 * L):
        @pl.when(w != worker_of(m, wide))
        def _():
            put_copy(m, w).wait_recv()
            get_copy(m, w).wait_send()

        @pl.when((side == (m % 4) // 2) & (w != worker_of(m, wide)))
        def _():
            block_copy(m, w).wait_send()

        @pl.when(w == worker_of(m, wide))
        def _():
            over_peers(w, wide, lambda p: put_copy(m, p).wait_send())
            over_peers(w, wide, lambda p: new_copy(m, p).wait_send())

    for s in range(levels):
        gram_copy(s).wait_send()
        for copy in small_copies(s):
            copy.wait_send()
    for l in range(L):
        for t in range(steps):
            for copy in step_copies(l, t):
                copy.wait_send()
    over_peers(me, count, lambda p: norm_copy(p, me).wait_send())
    over_peers(me, count, lambda p: slot_copy(p, me).wait_send())
    over_peers(w, wide, lambda p: own_copy(p, w).wait_send())


def finish_call(dmats, dsmall, dslots, requests, extra, loss, weights, moments, smalls, wide, narrow):
    count = wide * narrow
    levels = levels_of(narrow)
    columns = D // wide
    local = extra.shape[1]
    _, total = packed_offsets(narrow)
    shape = jax.ShapeDtypeStruct
    outs = [shape((1, TOKS), F32), shape(extra.shape, F32)]
    outs += [shape(a.shape, F32) for a in weights + moments + smalls]
    vm = pltpu.VMEM
    dma = pltpu.SemaphoreType.DMA
    steps = levels + 1

    def mats_shapes(l):
        sizes, quarters, rows = [], narrow, total
        plan = list(range(levels)) + ["side"] if l % 2 else [0, "side"] + list(range(1, levels))
        for move in plan:
            if move == "side":
                rows //= 2
            else:
                quarters //= 2
            sizes.append(vm((quarters, rows, TOKS), F32))
        return sizes

    mats = [v for l in range(L) for v in mats_shapes(l)]
    small_shapes = [vm((narrow >> (s + 1),) + dsmall.shape[1:], F32) for s in range(levels)]
    largest = max(packed_rows(which, narrow) for which in range(4))
    blocks = [vm((wide, columns, rows // narrow), F32) for rows in ROWS_OF]
    layers = [vm((L, columns, rows // narrow), F32) for rows in ROWS_OF]
    spec = pl.BlockSpec(memory_space=pltpu.VMEM)
    anywhere = pl.BlockSpec(memory_space=pl.ANY)
    return pl.pallas_call(
        functools.partial(finish_kernel, wide=wide, narrow=narrow),
        out_shape=outs,
        in_specs=[spec] * 4 + [anywhere] + [spec] * 12,
        out_specs=[spec] * len(outs),
        scratch_shapes=mats * 2 + small_shapes * 2
        + [
            vm(dslots.shape, BF16),
            vm((count * CAP, local), BF16),
            vm((wide, largest, TOKS), F32),
            vm((wide,) + dsmall.shape[2:], F32),
            vm((2 * TOKS, 2 * TOKS), F32),
            vm((D, local), F32),
            vm((count, 1, TOKS), F32),
        ]
        + blocks * 3 + layers
        + [
            vm((D, 2 * TOKS), F32), vm((D, 2 * TOKS), F32),
            vm((levels + 1, 2 * TOKS, TOKS), F32), vm((levels, 2 * TOKS, TOKS), F32),
            dma((count,)), dma((count,)),
            dma((L, steps, narrow)), dma((L, steps, narrow)),
            dma((levels, narrow // 2)), dma((levels, narrow // 2)),
            dma((4 * L,)), dma((wide,)), dma((wide,)), dma((wide,)),
            dma((count,)), dma((count,)), dma((4 * L,)), dma((wide,)), dma((wide,)), dma((4 * L,)),
            dma((wide,)), dma((4 * L,)), dma((levels,)), dma((levels,)), dma(()),
        ],
        compiler_params=pltpu.CompilerParams(
            collective_id=1, has_side_effects=True, vmem_limit_bytes=58 << 20
        ),
        name="finish",
    )(dmats, dsmall, dslots, requests, extra, loss, *weights, *moments, *smalls)


def per_device(
    cat_index, num_values, cell_mask, labels, table, table_first, table_second,
    small, small_first, small_second, w_qkv, w_proj, w_in, w_down,
    mom_qkv, mom_proj, mom_in, mom_down,
):
    wide = lax.axis_size("wide")
    narrow = lax.axis_size("narrow")
    count = wide * narrow
    data_rows = num_values.shape[0]
    pair = 4 if count * CAP <= 2048 else 2
    while data_rows % pair:
        pair //= 2
    flip = lambda v: jnp.swapaxes(v, -1, -2)
    weights = [flip(v) for v in (w_qkv, w_proj, w_in, w_down)]
    moments = [flip(v) for v in (mom_qkv, mom_proj, mom_in, mom_down)]
    smalls = [flip(v) for v in (small, small_first, small_second)]
    table_t = flip(table)
    flat_index = cat_index.reshape(-1)
    entries = flat_index.shape[0]
    qkv, proj, w_in_all, down, small_all, rows, slots, requests, stats = gather_call(
        flat_index[None], cell_mask, weights, smalls[0], table_t, wide, narrow
    )
    rows = rows.reshape(count * CAP, D)
    over = stats[0, CAP] > 0.5
    hidden_count = stats[:1, CAP + 1 : CAP + 2]

    def general_rows(rows, slots):
        whole = lax.all_gather(table.astype(BF16), ("wide", "narrow"), axis=0, tiled=True)
        looked = jnp.take(whole, flat_index, axis=0)
        spare = jnp.zeros((rows.shape[0] - entries, D), BF16)
        return jnp.concatenate([looked, spare], 0), lax.iota(jnp.int32, entries)[None]

    rows, slots = lax.cond(over, general_rows, lambda r, s: (r, s), rows, slots)

    def spread(value, fill=0):
        value = jnp.pad(value, ((0, 0), (1, TOKS - 1 - NUMF)), constant_values=fill)
        return value.reshape(data_rows // pair, 1, pair * TOKS)

    masked = cell_mask.astype(F32)
    slot_rows = jnp.pad(
        slots.reshape(data_rows, CATF), ((0, 0), (TOKS - CATF, 0)), constant_values=-1
    ).reshape(data_rows // pair, 1, pair * TOKS)
    label_rows = jnp.broadcast_to(labels[:, None], (data_rows, TOKS)).reshape(
        data_rows // pair, 1, pair * TOKS
    )
    loss, dmats, dsmall, dslots = model_call(
        hidden_count, rows, slot_rows, spread((1.0 - masked) * num_values), spread(num_values),
        spread(masked), label_rows, (qkv, proj, w_in_all, down), small_all, pair, wide, narrow,
    )

    def general_terms(dslots):
        tail = dslots[:, CAP:]
        tail = jnp.concatenate([tail[:, :, : D - TOKS], tail[:, :, D - TOKS :]], 1)
        terms = jnp.concatenate([dslots[:, :CAP], tail], 2).reshape(count * CAP, D)[:entries]
        whole = count * table.shape[0]
        hits = (flat_index[:, None] == lax.iota(jnp.int32, whole)[None, :]).astype(BF16)
        sums = lax.psum_scatter(
            mm(hits, terms, 0, 0), ("wide", "narrow"), scatter_dimension=0, tiled=True
        )
        return flip(sums), jnp.zeros_like(dslots)

    extra, dslots = lax.cond(
        over, general_terms, lambda d: (jnp.zeros(table_t.shape, F32), d), dslots
    )
    outs = finish_call(
        dmats, dsmall, dslots, requests, extra, loss, weights, moments, smalls, wide, narrow
    )
    stats_end, tgrad = outs[:2]
    norm = stats_end[0, 0]
    factor = CLIP / jnp.maximum(norm, CLIP)
    new_table, table_one, table_two = adam_step(
        table, factor * flip(tgrad), table_first, table_second
    )
    new_weights = [flip(v) for v in outs[2:6]]
    new_moments = [flip(v) for v in outs[6:10]]
    new_smalls = [flip(v) for v in outs[10:13]]
    return (
        stats_end[0, 1], hidden_count[0, 0], norm, new_table, table_one, table_two,
        *new_smalls, *new_weights, *new_moments,
    )


def solution(mesh):
    rows = P(("wide", "narrow"), None)
    square = P("narrow", "wide")
    cube = P(None, "narrow", "wide")
    return jax.shard_map(
        per_device,
        mesh=mesh,
        in_specs=(rows, rows, rows, P(("wide", "narrow")), rows, rows, rows)
        + (square,) * 3 + (cube,) * 8,
        out_specs=(P(), P(), P(), rows, rows, rows) + (square,) * 3 + (cube,) * 8,
        check_vma=False,
    )
```

```python
import functools
import math

import jax
import jax.numpy as jnp
import numpy as np
from jax import lax
from jax.experimental import pallas as pl
from jax.experimental.pallas import tpu as pltpu
from jax.sharding import PartitionSpec as P

D = 192
HEADS = 8
HD = 24
FF = 256
L = 2
NUMF = 95
CATF = 32
NCLASS = 7
STEP = 10
TOKS = 128

NORM_EPS = 1e-05
CLIP = 0.002
BETA_ONE = 0.9
BETA_TWO = 0.95
ADAM_EPS = 1e-08
ADAM_RATE = 0.2
MUON_RATE = 1.0
MOMENTUM = 0.95
DECAY = 0.01
ORTHO_EPS = 1e-20
NS_ONE = 3.4445
NS_TWO = -4.775
NS_THREE = 2.0315
GELU_A = math.sqrt(2.0 / math.pi)
GELU_B = 0.044715
SCALE = HD ** (-0.5)

F32 = jnp.float32
BF16 = jnp.bfloat16
MESH = pl.DeviceIdType.MESH

ROWS_OF = (3 * D, D, 2 * FF, FF)
ORDER = (2, 0, 1, 3)
NSR = 8 * L + TOKS + NUMF + 1 + 2 + NCLASS + NUMF
OFF_SCALE = 8 * L + TOKS
OFF_FIN = OFF_SCALE + NUMF + 1
CAP = 32
PACK = CAP + CAP // 2


def mm(left, right, left_dim=1, right_dim=0):
    return lax.dot_general(
        left, right, (((left_dim,), (right_dim,)), ((), ())), preferred_element_type=F32
    )


def up_to(value, unit):
    return -(-value // unit) * unit


def split_two(value):
    high = value.astype(BF16)
    return high, (value - high.astype(F32)).astype(BF16)


def split_three(value):
    high = value.astype(BF16)
    rest = value - high.astype(F32)
    middle = rest.astype(BF16)
    return high, middle, (rest - middle.astype(F32)).astype(BF16)


def place(wide, narrow):
    w = lax.axis_index("wide")
    n = lax.axis_index("narrow")
    return w, n, w * narrow + n


def greet_all(me, count, narrow):
    barrier = pltpu.get_barrier_semaphore()

    def signal(k, carry):
        p = lax.rem(me + k, count)
        pl.semaphore_signal(
            barrier, inc=1, device_id=(p // narrow, lax.rem(p, narrow)), device_id_type=MESH
        )
        return carry

    lax.fori_loop(1, count, signal, 0)
    return barrier


def quarter_offsets(narrow):
    offsets, total = {}, 0
    for which in ORDER:
        offsets[which] = total
        total += ROWS_OF[which] // narrow
    return offsets, total


def gather_kernel(
    cat_ref, mask_ref, qkv_ref, proj_ref, in_ref, down_ref, small_ref, table_ref, pick_ref,
    out_qkv, out_proj, out_in, out_down, out_small, out_rows, out_slots, out_requests, out_stats,
    gat_one, gat_two, ask, table_s, table_low, answers, landed,
    far_send, far_recv, step_send, step_recv, ask_send, ask_recv, row_send, row_recv, table_sem,
    *, wide, narrow, chunk,
):
    count = wide * narrow
    levels = levels_of(narrow)
    w, n, me = place(wide, narrow)
    side, far = lax.rem(w, 2), w // 2
    fars = wide // 2
    table_copy = pltpu.make_async_copy(table_ref, table_s, table_sem)
    table_copy.start()
    barrier = greet_all(me, count, narrow)

    def coords(p):
        return (p // narrow, lax.rem(p, narrow))

    offsets, total = quarter_offsets(narrow)
    width = qkv_ref.shape[1]
    rows_pad = gat_one.shape[3]
    cut = gat_one.shape[4]
    shards = (qkv_ref, proj_ref, in_ref, down_ref)
    pieces = [
        jnp.concatenate([shards[which][l] for which in ORDER], 1) for l in range(L)
    ]
    if rows_pad > L * width:
        pieces.append(jnp.zeros((rows_pad - L * width, total), F32))
    packed = jnp.concatenate(pieces, 0).astype(BF16)
    gat_one[n, side, far] = packed[:, :cut]
    gat_two[n, side, far] = packed[:, cut:]
    small = small_ref[...]
    own_rows = small.shape[1]
    small_pad = out_small.shape[3]
    if small_pad > width:
        small = jnp.concatenate([small, jnp.zeros((small_pad - width, own_rows), F32)], 0)
    out_small[n, side, far] = jnp.concatenate(
        [small, jnp.zeros((small_pad, TOKS - own_rows), F32)], 1
    )

    data_rows, per_row = cat_ref.shape
    entries = data_rows * per_row
    local = table_s.shape[1]
    index_row = jnp.concatenate([cat_ref[r : r + 1, :] for r in range(data_rows)], 1)
    owner_row = jnp.zeros_like(index_row)
    for k in range(1, count):
        owner_row = owner_row + (index_row >= k * local).astype(jnp.int32)
    base_row = owner_row * local
    index_col = jnp.transpose(jnp.broadcast_to(index_row, (8, entries)))[:, :1]
    before = lax.broadcasted_iota(jnp.int32, (entries, entries), 0)
    after = lax.broadcasted_iota(jnp.int32, (entries, entries), 1)
    same = index_col == index_row
    first_col = 1.0 - jnp.max(jnp.where(same & (after < before), 1.0, 0.0), 1, keepdims=True)
    first_row = 1.0 - jnp.max(jnp.where(same & (before < after), 1.0, 0.0), 0, keepdims=True)
    lower = (index_col >= base_row) & (index_col < index_row)
    rank_row = jnp.sum(jnp.where(lower, first_col, 0.0), 0, keepdims=True).astype(jnp.int32)
    slot_row = owner_row * CAP + rank_row
    none = jnp.full((1, TOKS - per_row), -1, jnp.int32)
    for r in range(data_rows):
        out_slots[r : r + 1, :] = jnp.concatenate(
            [none, slot_row[:, r * per_row : (r + 1) * per_row]], 1
        )
    over = jnp.max(jnp.where(rank_row >= CAP, 1.0, 0.0), 1, keepdims=True)
    hidden_cells = jnp.sum(jnp.sum(mask_ref[...].astype(F32), 0, keepdims=True), 1, keepdims=True)
    place_row = index_row - base_row
    owners = lax.broadcasted_iota(jnp.int32, (count, entries), 0)
    mine = jnp.where(owners == owner_row, first_row, 0.0)
    high = lax.shift_right_logical(place_row, 6)
    low = place_row - high * 64
    at_rank = jnp.where(
        lax.broadcasted_iota(jnp.int32, (TOKS, entries), 0) == rank_row, 1.0, 0.0
    ).astype(BF16)
    wanted = 64.0 * mm((mine * high.astype(F32)).astype(BF16), at_rank, 1, 1) + mm(
        (mine * low.astype(F32)).astype(BF16), at_rank, 1, 1
    )
    lane = lax.broadcasted_iota(jnp.int32, (count, TOKS), 1)
    wanted = jnp.where(lane < CAP, wanted, 0.0)
    wanted = jnp.where(lane == CAP, over, wanted)
    wanted = jnp.where(lane == CAP + 1, hidden_cells, wanted)
    for k in range(count):
        ask[k] = wanted[k : k + 1]

    pl.semaphore_wait(barrier, count - 1)

    def over_peers(origin, size, body):
        def run(k, carry):
            body(lax.rem(origin + k, size))
            return carry

        lax.fori_loop(1, size, run, 0)

    def ask_copy(p, slot):
        return pltpu.make_async_remote_copy(
            src_ref=ask.at[p], dst_ref=out_requests.at[slot], send_sem=ask_send.at[p],
            recv_sem=ask_recv.at[slot], device_id=coords(p), device_id_type=MESH,
        )

    def row_copy(p, slot):
        return pltpu.make_async_remote_copy(
            src_ref=answers.at[p], dst_ref=landed.at[slot], send_sem=row_send.at[p],
            recv_sem=row_recv.at[slot], device_id=coords(p), device_id_type=MESH,
        )

    arrays = (gat_one, gat_two, out_small)

    def far_copies(p, slot):
        return [
            pltpu.make_async_remote_copy(
                src_ref=array.at[n, side, far], dst_ref=array.at[n, side, slot],
                send_sem=far_send.at[a, p], recv_sem=far_recv.at[a, slot],
                device_id=(p * 2 + side, n), device_id_type=MESH,
            )
            for a, array in enumerate(arrays)
        ]

    high_levels = list(range(levels - 1, 0, -1))
    plans = (
        high_levels + ["side"] + [0] * (levels > 0),
        ["side"] + high_levels + [0] * (levels > 0),
    )
    steps = len(plans[0])

    def step_copies(t):
        copies = []
        for a, array in enumerate(arrays):
            plan = plans[min(a, 1)]
            move = plan[t]
            done = plan[:t]
            lowest = min([v for v in done if v != "side"], default=levels)
            for j in range(1 << (levels - lowest)):
                block = lax.rem(n, 1 << lowest) + (j << lowest)
                if move == "side":
                    target = (w + 1 - 2 * side, n)
                else:
                    bit = lax.rem(n // (1 << move), 2)
                    target = (w, n + (1 - 2 * bit) * (1 << move))
                ref = array.at[block] if "side" in done else array.at[block, side]
                copies.append(
                    pltpu.make_async_remote_copy(
                        src_ref=ref, dst_ref=ref, send_sem=step_send.at[t, a, j],
                        recv_sem=step_recv.at[t, a, j], device_id=target, device_id_type=MESH,
                    )
                )
        return copies

    def step_arrivals(t):
        copies = []
        for a, array in enumerate(arrays):
            plan = plans[min(a, 1)]
            move = plan[t]
            done = plan[:t]
            lowest = min([v for v in done if v != "side"], default=levels)
            for j in range(1 << (levels - lowest)):
                if move == "side":
                    there, whose, target = n, 1 - side, (w + 1 - 2 * side, n)
                else:
                    bit = lax.rem(n // (1 << move), 2)
                    there, whose = n + (1 - 2 * bit) * (1 << move), side
                    target = (w, there)
                block = lax.rem(there, 1 << lowest) + (j << lowest)
                ref = array.at[block] if "side" in done else array.at[block, whose]
                copies.append(
                    pltpu.make_async_remote_copy(
                        src_ref=ref, dst_ref=ref, send_sem=step_send.at[t, a, j],
                        recv_sem=step_recv.at[t, a, j], device_id=target, device_id_type=MESH,
                    )
                )
        return copies

    def start_far(p):
        for copy in far_copies(p, far):
            copy.start()

    def end_far(p):
        for copy in far_copies(p, p):
            copy.wait_recv()

    over_peers(me, count, lambda p: ask_copy(p, me).start())
    over_peers(far, fars, start_far)
    out_requests[me] = ask[me]
    table_copy.wait()
    table_low[...] = table_s[...].astype(BF16)
    over_peers(far, fars, end_far)
    for copy in step_copies(0):
        copy.start()
    over_peers(me, count, lambda p: ask_copy(p, p).wait_recv())

    eye = lax.broadcasted_iota(jnp.int32, (CAP, TOKS), 0) == lax.broadcasted_iota(
        jnp.int32, (CAP, TOKS), 1
    )
    spots = lax.broadcasted_iota(jnp.int32, (CAP, local), 1)

    def wanted_hits(q):
        row = jnp.broadcast_to(out_requests[q], (CAP, TOKS))
        column = jnp.sum(jnp.where(eye, row, 0.0), 1, keepdims=True).astype(jnp.int32)
        return jnp.where(spots == column, 1.0, 0.0).astype(BF16)

    half_lane = lax.broadcasted_iota(jnp.int32, (CAP // 2, TOKS), 1) < D - TOKS

    def answer(c, carry):
        found = [wanted_hits(c * chunk + j) for j in range(chunk)]
        got = mm(jnp.concatenate(found, 0), table_low[...], 1, 1)
        got = jnp.concatenate([got, jnp.zeros((got.shape[0], 2 * TOKS - D), F32)], 1)
        for j in range(chunk):
            q = c * chunk + j
            part = got[j * CAP : (j + 1) * CAP]
            tail = part[:, TOKS:]
            rolled = pltpu.roll(tail[CAP // 2 :], D - TOKS, 1)
            packed = jnp.where(half_lane, tail[: CAP // 2], rolled)
            answers[q] = jnp.concatenate([part[:, :TOKS], packed], 0).astype(BF16)

            @pl.when(q != me)
            def _():
                row_copy(q, me).start()

        return carry

    def next_step(t):
        for copy in step_arrivals(t):
            copy.wait_recv()
        if t + 1 < steps:
            for copy in step_copies(t + 1):
                copy.start()

    lax.fori_loop(0, count // chunk // 2, answer, 0)
    next_step(0)
    lax.fori_loop(count // chunk // 2, count // chunk, answer, 0)
    landed[me] = answers[me]
    for t in range(1, steps):
        next_step(t)

    outs = (out_qkv, out_proj, out_in, out_down)
    for q in range(narrow):
        held = jnp.concatenate(
            [
                gat_one[q].reshape(wide * rows_pad, cut),
                gat_two[q].reshape(wide * rows_pad, total - cut),
            ],
            1,
        )
        for l in range(L):
            matrix = mm(held, pick_ref[l], 0, 0).astype(BF16)
            for which in ORDER:
                size = ROWS_OF[which] // narrow
                outs[which][l, q * size : (q + 1) * size] = matrix[
                    offsets[which] : offsets[which] + size
                ]

    requests = out_requests[...]
    reached = jnp.max(requests, 0)
    summed = jnp.sum(requests, 0)
    lane = lax.broadcasted_iota(jnp.int32, (1, TOKS), 1)
    out_stats[...] = jnp.where(lane == CAP, reached, summed)

    over_peers(me, count, lambda p: row_copy(p, p).wait_recv())
    out_rows[...] = spread_slots(landed[...].astype(F32)).astype(BF16)

    def drain_far(p):
        for copy in far_copies(p, far):
            copy.wait_send()

    over_peers(far, fars, drain_far)
    for t in range(steps):
        for copy in step_copies(t):
            copy.wait_send()
    over_peers(me, count, lambda p: ask_copy(p, me).wait_send())
    over_peers(me, count, lambda p: row_copy(p, me).wait_send())


def levels_of(size):
    return size.bit_length() - 1


def spread_slots(packed):
    owners = packed.shape[0]
    head = packed[:, :CAP].reshape(owners * CAP, TOKS)
    tail = packed[:, CAP:].reshape(owners * (CAP // 2), TOKS)
    moved = pltpu.roll(tail, D - TOKS, 1).reshape(owners, CAP // 2, TOKS)
    tail = jnp.concatenate([tail.reshape(owners, CAP // 2, TOKS), moved], 1)
    return jnp.concatenate([head, tail.reshape(owners * CAP, TOKS)[:, : D - TOKS]], 1)


def gather_call(cat_index, cell_mask, shards_t, small_t, table_t, wide, narrow):
    count = wide * narrow
    levels = levels_of(narrow)
    width = small_t.shape[0]
    rows_pad = up_to(L * width, 16)
    small_pad = up_to(width, 8)
    _, total = quarter_offsets(narrow)
    cut = up_to(total // 2, TOKS)
    pick = np.zeros((L, wide * rows_pad, D), np.float32)
    for l in range(L):
        for block in range(wide):
            at = (block % 2) * (wide // 2) + block // 2
            for c in range(width):
                pick[l, at * rows_pad + l * width + c, block * width + c] = 1.0
    local = table_t.shape[1]
    shape = jax.ShapeDtypeStruct
    outs = [shape((L, rows, D), BF16) for rows in ROWS_OF] + [
        shape((narrow, 2, wide // 2, small_pad, TOKS), F32),
        shape((count * CAP, D), BF16),
        shape((cat_index.shape[0], TOKS), jnp.int32),
        shape((count, 1, TOKS), F32),
        shape((1, TOKS), F32),
    ]
    vmem = pl.BlockSpec(memory_space=pltpu.VMEM)
    vm = pltpu.VMEM
    dma = pltpu.SemaphoreType.DMA
    return pl.pallas_call(
        functools.partial(gather_kernel, wide=wide, narrow=narrow, chunk=8),
        out_shape=outs,
        in_specs=[vmem] * 7 + [pl.BlockSpec(memory_space=pl.ANY), vmem],
        out_specs=[vmem] * len(outs),
        scratch_shapes=[
            vm((narrow, 2, wide // 2, rows_pad, cut), BF16),
            vm((narrow, 2, wide // 2, rows_pad, total - cut), BF16),
            vm((count, 1, TOKS), F32),
            vm((D, local), F32),
            vm((D, local), BF16),
            vm((count, PACK, TOKS), BF16),
            vm((count, PACK, TOKS), BF16),
            dma((3, wide // 2)), dma((3, wide // 2)),
            dma((levels + 1, 3, narrow)), dma((levels + 1, 3, narrow)),
            dma((count,)), dma((count,)), dma((count,)), dma((count,)), dma(()),
        ],
        compiler_params=pltpu.CompilerParams(
            collective_id=0, has_side_effects=True, vmem_limit_bytes=56 << 20
        ),
        name="gather",
    )(cat_index, cell_mask, *shards_t, small_t, table_t, jnp.asarray(pick, BF16))


def lanes(vector, width):
    return jnp.concatenate([vector] * (width // vector.shape[1]), 1)


def fold(value):
    total = value[:, :TOKS]
    for start in range(TOKS, value.shape[1], TOKS):
        total = total + value[:, start : start + TOKS]
    return total


def norm_forward(value, gain, shift):
    center = value - jnp.sum(value, 0, keepdims=True) * (1.0 / D)
    spread = jnp.sum(center * center, 0, keepdims=True) * (1.0 / D)
    inverse = lax.rsqrt(spread + NORM_EPS)
    unit = center * inverse
    return unit, inverse, unit * gain + shift


def norm_backward(unit, inverse, grad_unit):
    mean_one = jnp.sum(grad_unit, 0, keepdims=True) * (1.0 / D)
    mean_two = jnp.sum(grad_unit * unit, 0, keepdims=True) * (1.0 / D)
    return inverse * (grad_unit - mean_one - unit * mean_two)


NVEC = 8 * L + 3
ROOM = TOKS // CATF


def model_kernel(
    stats_ref, labels_ref, rows_ref, slots_ref, num_ref, mask_ref,
    qkv_ref, proj_ref, in_ref, down_ref, small_ref,
    loss_ref, dmats_ref, dsmall_ref, dslots_ref,
    rows_t, qkv_t, proj_t, in_t, down_t, tok_s, scale_s, rec_s, class_s, class_t_s,
    dtok_s, dscale_s, drec_s, dclass_s, slots_acc,
    vecb, probs_s, unit_one_s, inv_one_s, normed_s, q_s, k_s, v_s, mixed_s,
    unit_two_s, inv_two_s, normed_two_s, gate_s, hidden_s, acc_s, looked_s, vt_s, wide_s, low_s, ds_s, qt_s,
    qkv_acc, proj_acc, in_acc, down_acc, num_s, mask_s, coef_s,
    *, pair, wide, narrow,
):
    width = pair * TOKS
    blocks = slots_ref.shape[0] // pair
    columns = D // wide
    own_rows = NSR // narrow
    slots = rows_ref.shape[0]
    offsets, _ = packed_offsets(narrow)
    mats_acc = (qkv_acc, proj_acc, in_acc, down_acc)
    inv_count = 1.0 / jnp.full((1, 1), stats_ref[0, CAP + 1], F32)
    data_rows = slots_ref.shape[0]
    gap = jnp.zeros((data_rows, 1), F32)
    gap_tail = jnp.zeros((data_rows, TOKS - 1 - NUMF), F32)
    masked = mask_ref[...].astype(F32)
    num_s[...] = jnp.concatenate([gap, num_ref[...], gap_tail], 1)
    mask_s[...] = jnp.concatenate([gap, masked, gap_tail], 1)
    coef_s[...] = jnp.concatenate([gap, (1.0 - masked) * num_ref[...], gap_tail], 1)

    rows_t[...] = jnp.transpose(rows_ref[...].astype(F32)).astype(BF16)
    for l in range(L):
        qkv_t[l] = jnp.transpose(qkv_ref[l].astype(F32)).astype(BF16)
        proj_t[l] = jnp.transpose(proj_ref[l].astype(F32)).astype(BF16)
        in_t[l] = jnp.transpose(in_ref[l].astype(F32)).astype(BF16)
        down_t[l] = jnp.transpose(down_ref[l].astype(F32)).astype(BF16)
    pieces = []
    for n in range(narrow):
        piece = jnp.concatenate([small_ref[n, w % 2, w // 2, :columns] for w in range(wide)], 0)
        pieces.append(piece[:, :own_rows])
    small = jnp.concatenate(pieces, 1)
    for i in range(NVEC):
        at = i if i < 8 * L else (OFF_FIN + i - 8 * L if i < 8 * L + 2 else OFF_SCALE + NUMF)
        vecb[i] = jnp.broadcast_to(small[:, at : at + 1], (D, TOKS))
    gap_one = jnp.zeros((D, 1), F32)
    gap_end = jnp.zeros((D, TOKS - 1 - NUMF), F32)
    tok_s[...] = small[:, 8 * L : OFF_SCALE]
    scale_s[...] = jnp.concatenate([gap_one, small[:, OFF_SCALE : OFF_SCALE + NUMF], gap_end], 1)
    rec_s[...] = jnp.concatenate([gap_one, small[:, OFF_FIN + 2 + NCLASS :], gap_end], 1)
    class_t = jnp.concatenate(
        [small[:, OFF_FIN + 2 : OFF_FIN + 2 + NCLASS], jnp.zeros((D, TOKS - NCLASS), F32)], 1
    )
    class_s[...] = jnp.transpose(class_t)[:16].astype(BF16)
    class_t_s[...] = jnp.concatenate([class_t[:, :16]] * 3, 1).astype(BF16)
    for ref in (loss_ref, *mats_acc, dtok_s, dscale_s, drec_s, dclass_s, acc_s):
        ref[...] = jnp.zeros_like(ref)

    def vec(i):
        return lanes(vecb[i], width)

    def head_rows(value, h, b):
        return value[h * HD : h * HD + HD, b * TOKS : b * TOKS + TOKS]

    def head_mask(h):
        lane = lax.broadcasted_iota(jnp.int32, (1, D), 1)
        return jnp.where((lane >= h * HD) & (lane < h * HD + HD), 1.0, 0.0).astype(BF16)

    def by_head(value):
        return jnp.concatenate([value * head_mask(h) for h in range(HEADS)], 0)

    def by_rows(value):
        row = lax.broadcasted_iota(jnp.int32, value.shape, 0)
        return jnp.concatenate([value * jnp.where((row >= h * HD) & (row < h * HD + HD), 1.0, 0.0).astype(BF16) for h in range(HEADS)], 1)

    def add_mats(l, which, value):
        mats_acc[which][l] += value

    def add_vec(i, value):
        acc_s[i] += fold(value)

    def forward(l, x):
        base = 8 * l
        unit, inverse, normed = norm_forward(x, vec(base), vec(base + 1))
        normed = normed.astype(BF16)
        unit_one_s[l] = unit
        inv_one_s[l] = inverse
        normed_s[l] = normed
        joined = mm(qkv_ref[l], normed)
        q_f = joined[:D] + vec(base + 4)
        k_f = joined[D : 2 * D]
        v_f = joined[2 * D :] + vec(base + 5)
        k_t = jnp.transpose(k_f).astype(BF16)
        vt_s[l] = jnp.transpose(v_f).astype(BF16)
        q_low = q_f.astype(BF16)
        qt_s[l] = jnp.transpose(q_f).astype(BF16)
        mixed_cols = []
        for b in range(pair):
            for h in range(HEADS):
                qh = head_rows(q_f, h, b).astype(BF16)
                kh = head_rows(k_f, h, b).astype(BF16)
                vh = head_rows(v_f, h, b).astype(BF16)
                u = b * HEADS + h
                q_s[l, u] = qh
                k_s[l, u] = kh
                v_s[l, u] = vh
        for b in range(pair):
            span = slice(b * TOKS, (b + 1) * TOKS)
            wide_s[b] = mm(k_t[span], by_rows(q_low[:, span]))
        for b in range(pair):
            for h in range(HEADS):
                u = b * HEADS + h
                scores = wide_s[b, :, h * TOKS : (h + 1) * TOKS]
                top = jnp.max(scores, 0, keepdims=True)
                weight = jnp.exp((scores - top) * SCALE)
                probs = weight * (1.0 / jnp.sum(weight, 0, keepdims=True))
                probs_s[l, u] = probs
                low_s[l, b, :, h * TOKS : (h + 1) * TOKS] = probs.astype(BF16)
        for b in range(pair):
            rows = []
            for h in range(HEADS):
                u = b * HEADS + h
                rows.append(mm(v_s[l, u], low_s[l, b, :, h * TOKS : (h + 1) * TOKS]))
            mixed_cols.append(jnp.concatenate(rows, 0))
        mixed = jnp.concatenate(mixed_cols, 1).astype(BF16)
        mixed_s[l] = mixed
        after = x + mm(proj_ref[l], mixed) + vec(base + 6)
        unit, inverse, normed = norm_forward(after, vec(base + 2), vec(base + 3))
        normed = normed.astype(BF16)
        unit_two_s[l] = unit
        inv_two_s[l] = inverse
        normed_two_s[l] = normed
        gate_up = mm(in_ref[l], normed)
        gate_s[l] = gate_up
        gate, up = gate_up[:FF], gate_up[FF:]
        inner = GELU_A * (gate + GELU_B * gate * gate * gate)
        hidden = (0.5 * gate * (1.0 + jnp.tanh(inner)) * up).astype(BF16)
        hidden_s[l] = hidden
        return after + mm(down_t[l], hidden) + vec(base + 7)

    def backward(l, dout):
        base = 8 * l
        add_vec(base + 7, dout)
        up_low = dout.astype(BF16)
        add_mats(l, 3, mm(hidden_s[l], up_low, 1, 1))
        dhidden = mm(down_ref[l], up_low)
        gate, up = gate_s[l, :FF], gate_s[l, FF:]
        square = gate * gate
        tanh = jnp.tanh(GELU_A * (gate + GELU_B * square * gate))
        half = 0.5 * (1.0 + tanh)
        slope = half + 0.5 * gate * (1.0 - tanh * tanh) * (GELU_A * (1.0 + 3.0 * GELU_B * square))
        dgate = dhidden * up * slope
        dup = dhidden * (gate * half)
        dgl = jnp.concatenate([dgate, dup], 0).astype(BF16)
        add_mats(l, 2, mm(dgl, normed_two_s[l], 1, 1))
        dnormed = mm(in_t[l], dgl)
        unit = unit_two_s[l]
        add_vec(base + 2, dnormed * unit)
        add_vec(base + 3, dnormed)
        dafter = dout + norm_backward(unit, inv_two_s[l], dnormed * vec(base + 2))
        add_vec(base + 6, dafter)
        after_low = dafter.astype(BF16)
        add_mats(l, 1, mm(after_low, mixed_s[l], 1, 1))
        dmixed = mm(proj_t[l], after_low)
        dmixed_low = dmixed.astype(BF16)
        dm_t = jnp.transpose(dmixed).astype(BF16)
        q_cols, k_cols, v_cols = [], [], []
        for b in range(pair):
            span = slice(b * TOKS, (b + 1) * TOKS)
            wide_s[b] = mm(vt_s[l, span], by_rows(dmixed_low[:, span]))
        for b in range(pair):
            for h in range(HEADS):
                u = b * HEADS + h
                probs = probs_s[l, u]
                dprobs = wide_s[b, :, h * TOKS : (h + 1) * TOKS]
                inner = jnp.sum(dprobs * probs, 0, keepdims=True)
                ds_s[b, :, h * TOKS : (h + 1) * TOKS] = (probs * (dprobs - inner) * SCALE).astype(BF16)
        for b in range(pair):
            q_rows = []
            for h in range(HEADS):
                u = b * HEADS + h
                q_rows.append(mm(k_s[l, u], ds_s[b, :, h * TOKS : (h + 1) * TOKS]))
            q_cols.append(jnp.concatenate(q_rows, 0))
            span = slice(b * TOKS, (b + 1) * TOKS)
            v_cols.append(mm(low_s[l, b], by_head(dm_t[span])))
            k_cols.append(mm(ds_s[b], by_head(qt_s[l, span])))
        dq = jnp.concatenate(q_cols, 1)
        dk = jnp.transpose(jnp.concatenate(k_cols, 0))
        dv = jnp.transpose(jnp.concatenate(v_cols, 0))
        add_vec(base + 4, dq)
        add_vec(base + 5, dv)
        dj = jnp.concatenate([dq, dk, dv], 0).astype(BF16)
        add_mats(l, 0, mm(dj, normed_s[l], 1, 1))
        dnormed = mm(qkv_t[l], dj)
        unit = unit_one_s[l]
        add_vec(base, dnormed * unit)
        add_vec(base + 1, dnormed)
        return dafter + norm_backward(unit, inv_one_s[l], dnormed * vec(base))

    def step(i, carry):
        def row_of(ref):
            return jnp.concatenate([ref[pl.ds(i * pair + b, 1), :] for b in range(pair)], 1)

        coef = row_of(coef_s)
        num = row_of(num_s)
        mask = row_of(mask_s)
        lane = lax.broadcasted_iota(jnp.int32, (D, TOKS), 1)
        placed = []
        for b in range(pair):
            found = looked_s[i, :, (b // ROOM) * TOKS : (b // ROOM + 1) * TOKS]
            shift = (TOKS - CATF - b * CATF) % TOKS
            moved = pltpu.roll(found, shift, 1) if shift else found
            placed.append(jnp.where(lane < TOKS - CATF, 0.0, moved))
        x = jnp.concatenate(placed, 1) + lanes(tok_s[...], width)
        x = x + coef * lanes(scale_s[...], width) + mask * vec(8 * L + 2)
        for l in range(L):
            x = forward(l, x)
        unit, inverse, final = norm_forward(x, vec(8 * L), vec(8 * L + 1))
        rec = lanes(rec_s[...], width)
        error = jnp.sum(final * rec, 0, keepdims=True) - num
        final_low = final.astype(BF16)
        logits = mm(class_s[...], final_low)
        row = lax.broadcasted_iota(jnp.int32, logits.shape, 0)
        lane = lax.broadcasted_iota(jnp.int32, logits.shape, 1)
        live = row < NCLASS
        logits = jnp.where(live, logits, -1e30)
        top = jnp.max(logits, 0, keepdims=True)
        weight = jnp.where(live, jnp.exp(logits - top), 0.0)
        sums = jnp.sum(weight, 0, keepdims=True)
        first = (lane % TOKS) == 0
        label = jnp.concatenate(
            [jnp.full((1, TOKS), labels_ref[i * pair + b], jnp.int32) for b in range(pair)], 1
        )
        hit = jnp.where(first & (row == label), 1.0, 0.0)
        firsts = jnp.where(first[:1], 1.0, 0.0)
        picked = jnp.sum(jnp.where(hit > 0, logits, 0.0), 0, keepdims=True)
        loss_ref[...] += fold(mask * error * error + firsts * (top + jnp.log(sums)) - picked)
        dlogits = (firsts * weight / sums - hit) * inv_count
        dpredict = (2.0 * inv_count) * mask * error
        parts = jnp.concatenate([p.astype(F32) for p in split_three(dlogits)], 0).astype(BF16)
        dclass_s[...] += mm(final_low, parts, 1, 1)
        drec_s[...] += fold(final * dpredict)
        dfinal = rec * dpredict + mm(class_t_s[...], parts)
        add_vec(8 * L, dfinal * unit)
        add_vec(8 * L + 1, dfinal)
        dx = norm_backward(unit, inverse, dfinal * vec(8 * L))
        for l in reversed(range(L)):
            dx = backward(l, dx)
        dtok_s[...] += fold(dx)
        dscale_s[...] += fold(coef * dx)
        acc_s[8 * L + 2] += fold(mask * dx)
        packed = [jnp.zeros((D, TOKS), F32) for _ in range(groups)]
        group = lax.broadcasted_iota(jnp.int32, (D, TOKS), 1) // CATF
        for b in range(pair):
            part = dx[:, b * TOKS : (b + 1) * TOKS]
            shift = (b * CATF + CATF) % TOKS
            if shift:
                part = pltpu.roll(part, shift, 1)
            packed[b // ROOM] = jnp.where(group == b % ROOM, part, packed[b // ROOM])
        for at in range(groups):
            looked_s[i, :, at * TOKS : (at + 1) * TOKS] = packed[at]
        return carry

    groups = -(-pair // ROOM)
    spare = groups * TOKS - pair * CATF

    def hits_of(i):
        pieces = [
            slots_ref[i * pair + b : i * pair + b + 1, TOKS - CATF :] for b in range(pair)
        ]
        if spare:
            pieces.append(jnp.full((1, spare), -1, jnp.int32))
        slot = lax.broadcasted_iota(jnp.int32, (slots, groups * TOKS), 0)
        return jnp.where(slot == jnp.concatenate(pieces, 1), 1.0, 0.0).astype(BF16)

    for i in range(blocks):
        looked_s[i] = mm(rows_t[...], hits_of(i))
    lax.fori_loop(0, blocks, step, 0)
    slots_acc[...] = jnp.zeros_like(slots_acc)
    for i in range(blocks):
        slots_acc[...] += mm(hits_of(i), looked_s[i].astype(BF16), 1, 1)

    dvec = [jnp.sum(acc_s[i], 1, keepdims=True) for i in range(NVEC)]
    dclass = dclass_s[...]
    dclass = dclass[:, :16] + dclass[:, 16:32] + dclass[:, 32:]
    dsmall = jnp.concatenate(
        dvec[: 8 * L]
        + [dtok_s[...], dscale_s[:, 1 : 1 + NUMF], dvec[8 * L + 2]]
        + dvec[8 * L : 8 * L + 2]
        + [dclass[:, :NCLASS], drec_s[:, 1 : 1 + NUMF]],
        1,
    )
    blank = jnp.zeros((D, TOKS - own_rows), F32)
    for n in range(narrow):
        piece = jnp.concatenate([dsmall[:, n * own_rows : (n + 1) * own_rows], blank], 1)
        if dsmall_ref.shape[2] == columns:
            dsmall_ref[n] = piece.reshape(wide, columns, TOKS)
        else:
            dsmall_ref[n] = jnp.zeros(dsmall_ref.shape[1:], F32)
            for w in range(wide):
                dsmall_ref[n, w, :columns] = piece[w * columns : (w + 1) * columns]

    def beside(tail):
        rows = tail.shape[0]
        tail = jnp.concatenate([tail, jnp.zeros((rows, 2 * TOKS - D), F32)], 1)
        lane = lax.broadcasted_iota(jnp.int32, (rows // 2, TOKS), 1)
        return jnp.where(
            lane < D - TOKS, tail[: rows // 2], pltpu.roll(tail[rows // 2 :], D - TOKS, 1)
        )

    for which in range(4):
        size = ROWS_OF[which] // narrow
        for l in range(L):
            for n in range(narrow):
                part = mats_acc[which][l, n * size : (n + 1) * size]
                at = offsets[which]
                dmats_ref[l, n, at : at + size] = part[:, :TOKS]
                dmats_ref[l, n, at + size : at + size + size // 2] = beside(part[:, TOKS:])

    terms = slots_acc[...]
    dslots_ref[:, :CAP] = terms[:, :TOKS].reshape(slots // CAP, CAP, TOKS).astype(BF16)
    tail = jnp.concatenate([terms[:, TOKS:], jnp.zeros((slots, 2 * TOKS - D), F32)], 1)
    tail = tail.reshape(slots // CAP, CAP, TOKS)
    low = tail[:, : CAP // 2].reshape(slots // 2, TOKS)
    high = pltpu.roll(tail[:, CAP // 2 :].reshape(slots // 2, TOKS), D - TOKS, 1)
    lane = lax.broadcasted_iota(jnp.int32, (slots // 2, TOKS), 1)
    dslots_ref[:, CAP:] = (
        jnp.where(lane < D - TOKS, low, high).reshape(slots // CAP, CAP // 2, TOKS).astype(BF16)
    )


def model_call(stats, labels, rows, slots, num, mask, mats, small, pair, wide, narrow):
    width = pair * TOKS
    used = rows.shape[0]
    _, total = packed_offsets(narrow)
    shape = jax.ShapeDtypeStruct
    outs = [
        shape((1, TOKS), F32),
        shape((L, narrow, total, TOKS), F32),
        shape((narrow, wide, small.shape[3], TOKS), F32),
        shape((used // CAP, PACK, TOKS), BF16),
    ]
    units = pair * HEADS
    vm = pltpu.VMEM
    scratch = [
        vm((D, used), BF16),
        vm((L, D, 3 * D), BF16), vm((L, D, D), BF16), vm((L, D, 2 * FF), BF16), vm((L, D, FF), BF16),
        vm((D, TOKS), F32), vm((D, TOKS), F32), vm((D, TOKS), F32), vm((16, D), BF16), vm((D, 48), BF16),
        vm((D, TOKS), F32), vm((D, TOKS), F32), vm((D, TOKS), F32), vm((D, 48), F32), vm((used, D), F32),
        vm((NVEC, D, TOKS), F32), vm((L, units, TOKS, TOKS), F32),
        vm((L, D, width), F32), vm((L, 1, width), F32), vm((L, D, width), BF16),
        vm((L, units, HD, TOKS), BF16), vm((L, units, HD, TOKS), BF16), vm((L, units, HD, TOKS), BF16),
        vm((L, D, width), BF16),
        vm((L, D, width), F32), vm((L, 1, width), F32), vm((L, D, width), BF16),
        vm((L, 2 * FF, width), F32), vm((L, FF, width), BF16),
        vm((NVEC, D, TOKS), F32), vm((slots.shape[0] // pair, D, -(-pair // ROOM) * TOKS), F32), vm((L, width, D), BF16), vm((pair, TOKS, HEADS * TOKS), F32), vm((L, pair, TOKS, HEADS * TOKS), BF16), vm((pair, TOKS, HEADS * TOKS), BF16), vm((L, width, D), BF16),
        *[vm((L, rows, D), F32) for rows in ROWS_OF],
        *[vm((slots.shape[0], TOKS), F32)] * 3,
    ]
    spec = pl.BlockSpec(memory_space=pltpu.VMEM)
    return pl.pallas_call(
        functools.partial(model_kernel, pair=pair, wide=wide, narrow=narrow),
        out_shape=outs,
        in_specs=[pl.BlockSpec(memory_space=pltpu.SMEM)] * 2 + [spec] * 9,
        out_specs=[spec] * len(outs),
        scratch_shapes=scratch,
        compiler_params=pltpu.CompilerParams(vmem_limit_bytes=62 << 20),
        name="model",
    )(stats, labels, rows, slots, num, mask, *mats, small)


def packed_rows(which, narrow):
    size = ROWS_OF[which] // narrow
    return size + size // 2


def packed_offsets(narrow):
    offsets, total = [], 0
    for which in range(4):
        offsets.append(total)
        total += packed_rows(which, narrow)
    return offsets, total


def worker_of(m, wide):
    layer, kind = m // 4, m % 4
    return (layer * 2 + kind % 2) * (wide // 8) * 2 + kind // 2


def adam_step(weight, gradient, first, second):
    first = BETA_ONE * first + (1.0 - BETA_ONE) * gradient
    second = BETA_TWO * second + (1.0 - BETA_TWO) * gradient * gradient
    ratio = first / (1.0 - BETA_ONE**STEP) / (jnp.sqrt(second / (1.0 - BETA_TWO**STEP)) + ADAM_EPS)
    return (weight - ADAM_RATE * (ratio + DECAY * weight), first, second)


def exact(left, right, left_dim=1, right_dim=0):
    return lax.dot_general(
        left, right, (((left_dim,), (right_dim,)), ((), ())), preferred_element_type=F32,
        precision=lax.Precision.HIGHEST,
    )


def finish_kernel(*refs, wide, narrow):
    refs = list(refs)

    def take(number):
        head = refs[:number]
        del refs[:number]
        return head

    levels = levels_of(narrow)
    count = wide * narrow
    columns = D // wide
    dmats_ref, dsmall_ref, dslots_ref, requests_ref, loss_ref = take(5)
    moments = take(4)
    out_stats, out_table, out_small = take(3)
    x_came, out_moments = take(4), take(4)
    steps = levels + 1
    mats_held = [take(steps) for _ in range(L)]
    mats_came = [take(steps) for _ in range(L)]
    small_held, small_came = take(levels), take(levels)
    landed, hits, mats_landed, small_landed, grad_s = take(5)
    norm_near, norm_all = take(2)
    mom_came, mom_sent, x_sent = take(4), take(4), take(4)
    x_start, x_end, gram_held, gram_came = take(4)
    (
        slot_send, slot_recv, mats_send, mats_recv, small_send, small_recv,
        block_send, block_recv, own_send, own_recv,
        near_send, near_recv, norm_send, norm_recv, get_send, get_recv, put_send, put_recv, new_send, new_recv,
        gram_send, gram_recv,
    ) = refs
    w, n, me = place(wide, narrow)
    barrier = greet_all(me, count, narrow)
    offsets, total = packed_offsets(narrow)
    half_rows = total // 2
    local = out_table.shape[1]
    side = lax.rem(w, 2)

    def over_peers(origin, size, body):
        def run(k, carry):
            body(lax.rem(origin + k, size))
            return carry

        lax.fori_loop(1, size, run, 0)

    def coords(p):
        return (p // narrow, lax.rem(p, narrow))

    def narrow_partner(s):
        bit = lax.rem(n // (1 << s), 2)
        return bit, n + (1 - 2 * bit) * (1 << s)

    def plan(l):
        if l % 2:
            return list(range(levels)) + ["side"]
        return [0, "side"] + list(range(1, levels)) if levels else ["side"]

    def before(l, t):
        return dmats_ref.at[l] if t == 0 else mats_held[l][t - 1]

    def step_copies(l, t):
        move = plan(l)[t]
        source = before(l, t)
        copies = []
        if move == "side":
            for j in range(source.shape[0]):
                copies.append(
                    pltpu.make_async_remote_copy(
                        src_ref=source.at[j, pl.ds((1 - side) * half_rows, half_rows)],
                        dst_ref=mats_came[l][t].at[j],
                        send_sem=mats_send.at[l, t, j], recv_sem=mats_recv.at[l, t, j],
                        device_id=(w + 1 - 2 * side, n), device_id_type=MESH,
                    )
                )
        else:
            bit, partner = narrow_partner(move)
            for j in range(source.shape[0] // 2):
                copies.append(
                    pltpu.make_async_remote_copy(
                        src_ref=source.at[2 * j + 1 - bit], dst_ref=mats_came[l][t].at[j],
                        send_sem=mats_send.at[l, t, j], recv_sem=mats_recv.at[l, t, j],
                        device_id=(w, partner), device_id_type=MESH,
                    )
                )
        return copies

    def step_add(l, t):
        move = plan(l)[t]
        source = before(l, t)
        for j in range(mats_held[l][t].shape[0]):
            if move == "side":
                mine = source[j, pl.ds(side * half_rows, half_rows)]
            else:
                mine = source[2 * j + narrow_partner(move)[0]]
            mats_held[l][t][j] = mine + mats_came[l][t][j]

    def small_before(s):
        return dsmall_ref if s == 0 else small_held[s - 1]

    def small_copies(s):
        bit, partner = narrow_partner(s)
        return [
            pltpu.make_async_remote_copy(
                src_ref=small_before(s).at[2 * j + 1 - bit], dst_ref=small_came[s].at[j],
                send_sem=small_send.at[s, j], recv_sem=small_recv.at[s, j],
                device_id=(w, partner), device_id_type=MESH,
            )
            for j in range(narrow >> (s + 1))
        ]

    def small_add(s):
        bit, _ = narrow_partner(s)
        for j in range(narrow >> (s + 1)):
            small_held[s][j] = small_before(s)[2 * j + bit] + small_came[s][j]

    def slot_copy(p, slot):
        return pltpu.make_async_remote_copy(
            src_ref=dslots_ref.at[p], dst_ref=landed.at[slot], send_sem=slot_send.at[p],
            recv_sem=slot_recv.at[slot], device_id=coords(p), device_id_type=MESH,
        )

    def block_copy(m, slot):
        layer, kind = m // 4, m % 4
        start = offsets[kind] - half_rows * (kind // 2)
        size = packed_rows(kind, narrow)
        return pltpu.make_async_remote_copy(
            src_ref=mats_held[layer][steps - 1].at[0, pl.ds(start, size)],
            dst_ref=mats_landed.at[slot, pl.ds(0, size)],
            send_sem=block_send.at[m], recv_sem=block_recv.at[slot],
            device_id=(worker_of(m, wide), n), device_id_type=MESH,
        )

    def own_copy(p, slot):
        return pltpu.make_async_remote_copy(
            src_ref=small_held[levels - 1].at[0, p], dst_ref=small_landed.at[slot],
            send_sem=own_send.at[p], recv_sem=own_recv.at[slot], device_id=(p, n),
            device_id_type=MESH,
        )

    def near_copy(p, slot):
        return pltpu.make_async_remote_copy(
            src_ref=norm_near.at[n], dst_ref=norm_near.at[slot], send_sem=near_send.at[p],
            recv_sem=near_recv.at[slot], device_id=(w, p), device_id_type=MESH,
        )

    def norm_copy(p, slot):
        return pltpu.make_async_remote_copy(
            src_ref=norm_all.at[w], dst_ref=norm_all.at[slot], send_sem=norm_send.at[p],
            recv_sem=norm_recv.at[slot], device_id=(p, n), device_id_type=MESH,
        )

    def get_copy(m, slot):
        return pltpu.make_async_remote_copy(
            src_ref=moments[m % 4].at[m // 4], dst_ref=mom_came[m % 4].at[slot],
            send_sem=get_send.at[m], recv_sem=get_recv.at[slot],
            device_id=(worker_of(m, wide), n), device_id_type=MESH,
        )

    def put_copy(m, p):
        return pltpu.make_async_remote_copy(
            src_ref=mom_sent[m % 4].at[p], dst_ref=out_moments[m % 4].at[m // 4],
            send_sem=put_send.at[p], recv_sem=put_recv.at[m], device_id=(p, n),
            device_id_type=MESH,
        )

    def new_copy(m, p):
        return pltpu.make_async_remote_copy(
            src_ref=x_sent[m % 4].at[p], dst_ref=x_came[m % 4].at[m // 4],
            send_sem=new_send.at[p], recv_sem=new_recv.at[m], device_id=(p, n),
            device_id_type=MESH,
        )

    def gram_copy(s):
        _, partner = narrow_partner(s)
        return pltpu.make_async_remote_copy(
            src_ref=gram_held.at[s], dst_ref=gram_came.at[s], send_sem=gram_send.at[s],
            recv_sem=gram_recv.at[s], device_id=(w, partner), device_id_type=MESH,
        )

    pl.semaphore_wait(barrier, count - 1)
    for l in range(L):
        for copy in step_copies(l, 0):
            copy.start()
    for copy in small_copies(0):
        copy.start()
    over_peers(me, count, lambda p: slot_copy(p, me).start())
    landed[me] = dslots_ref[me]
    for m in range(4 * L):
        @pl.when(w != worker_of(m, wide))
        def _():
            get_copy(m, w).start()

        @pl.when(w == worker_of(m, wide))
        def _():
            mom_came[m % 4][w] = moments[m % 4][m // 4]

    eye = lax.broadcasted_iota(jnp.int32, (CAP, TOKS), 0) == lax.broadcasted_iota(
        jnp.int32, (CAP, TOKS), 1
    )
    spots = lax.broadcasted_iota(jnp.int32, (CAP, local), 1)

    def find(c, carry):
        for j in range(8):
            q = c * 8 + j
            row = jnp.broadcast_to(requests_ref[q], (CAP, TOKS))
            column = jnp.sum(jnp.where(eye, row, 0.0), 1, keepdims=True).astype(jnp.int32)
            at = pl.multiple_of(q * CAP, CAP)
            hits[pl.ds(at, CAP), :] = jnp.where(spots == column, 1.0, 0.0).astype(BF16)
        return carry

    lax.fori_loop(0, count // 8, find, 0)

    def finish_step(t):
        for l in range(L):
            for copy in step_copies(l, t):
                copy.wait_recv()
            step_add(l, t)
        if t < levels:
            for copy in small_copies(t):
                copy.wait_recv()
            small_add(t)
        if t + 1 < steps:
            for l in range(L):
                for copy in step_copies(l, t + 1):
                    copy.start()
        if t + 1 < levels:
            for copy in small_copies(t + 1):
                copy.start()

    finish_step(0)

    over_peers(me, count, lambda p: slot_copy(p, p).wait_recv())
    terms_t = jnp.transpose(spread_slots(landed[...].astype(F32)))
    if steps > 2:
        finish_step(1)
    out_table[...] = mm(terms_t.astype(BF16), hits[...])
    for t in range(2 if steps > 2 else 1, steps):
        finish_step(t)

    over_peers(w, wide, lambda p: own_copy(p, w).start())
    for m in range(4 * L):
        kind = m % 4

        @pl.when((side == kind // 2) & (w != worker_of(m, wide)))
        def _():
            block_copy(m, w).start()

    table_grad = out_table[...]

    def total_of(value):
        return jnp.sum(jnp.sum(value, 0, keepdims=True), 1, keepdims=True)

    squares = total_of(table_grad * table_grad)
    loss_here = jnp.sum(loss_ref[...], 1, keepdims=True)
    x_start[...] = jnp.zeros_like(x_start)
    grad_s[...] = jnp.zeros_like(grad_s)

    over_peers(w, wide, lambda p: own_copy(p, p).wait_recv())

    def add_small(k, value):
        return value + small_landed[lax.rem(w + k, wide)]

    own_small = lax.fori_loop(1, wide, add_small, small_held[levels - 1][0, w])
    squares = squares + total_of(own_small * own_small)
    out_small[...] = own_small
    for m in range(4 * L):
        layer, kind = m // 4, m % 4

        @pl.when(w == worker_of(m, wide))
        def _():
            start = offsets[kind] - half_rows * (kind // 2)
            size = packed_rows(kind, narrow)
            whole = ROWS_OF[kind] // narrow

            def add_block(k, value):
                p = lax.rem(w // 2 + k, wide // 2) * 2 + side
                block_copy(m, p).wait_recv()
                return value + mats_landed[p, :size]

            packed = lax.fori_loop(
                1, wide // 2, add_block,
                mats_held[layer][steps - 1][0, start : start + size],
            )
            tail = packed[whole:]
            grad_s[:whole, :TOKS] = packed[:whole]
            grad_s[: whole // 2, TOKS : D] = tail[:, : D - TOKS]
            grad_s[whole // 2 : whole, TOKS : D] = tail[:, D - TOKS :]

    grad = grad_s[...]
    squares = squares + total_of(grad * grad)
    lane = lax.broadcasted_iota(jnp.int32, (1, TOKS), 1)
    norm_near[n] = jnp.where(lane == 0, squares, jnp.where(lane == 1, loss_here, 0.0))
    over_peers(n, narrow, lambda p: near_copy(p, n).start())
    grad_t = jnp.transpose(grad)[:D]
    over_peers(n, narrow, lambda p: near_copy(p, p).wait_recv())
    norm_all[w] = jnp.sum(norm_near[...], 0)
    over_peers(w, wide, lambda p: norm_copy(p, w).start())
    over_peers(w, wide, lambda p: norm_copy(p, p).wait_recv())
    sums = jnp.sum(norm_all[...], 0)
    norm = jnp.sqrt(sums)
    factor = CLIP / jnp.maximum(norm[:, :1], CLIP)
    out_stats[...] = jnp.where(lane == 0, norm, jnp.where(lane == 2, factor, sums))

    def gather_rows(ref):
        if columns % 8 == 0:
            return ref[...].reshape(D, ref.shape[2])
        return jnp.concatenate([ref[p] for p in range(wide)], 0)

    def spread_rows(ref, value):
        if columns % 8 == 0:
            ref[...] = value.reshape(ref.shape)
        else:
            for p in range(wide):
                ref[p] = value[p * columns : (p + 1) * columns]

    for m in range(4 * L):
        @pl.when(w == worker_of(m, wide))
        def _():
            over_peers(w, wide, lambda p: get_copy(m, p).wait_recv())
            size = ROWS_OF[m % 4] // narrow
            moment = MOMENTUM * gather_rows(mom_came[m % 4]) + factor * grad_t[:, :size]
            x_start[:, :size] = moment
            spread_rows(mom_sent[m % 4], moment)
            over_peers(w, wide, lambda p: put_copy(m, p).start())
            out_moments[m % 4][m // 4] = mom_sent[m % 4][w]

    x = x_start[...]
    gram = exact(x, x, 1, 1)
    rest = D - TOKS
    gram_held[0, :D] = gram[:, :TOKS]
    gram_held[0, D : D + rest] = jnp.concatenate(
        [gram[TOKS:, TOKS:], jnp.zeros((rest, TOKS - rest), F32)], 1
    )
    for s in range(levels):
        gram_copy(s).start()
        gram_copy(s).wait_recv()
        gram_held[s + 1] = gram_held[s] + gram_came[s]
    left = gram_held[levels, :D]
    corner = gram_held[levels, D : D + rest][:, :rest]
    above = jnp.transpose(
        jnp.concatenate([left[TOKS:], jnp.zeros((TOKS - rest, TOKS), F32)], 0)
    )[:, :rest]
    gram = jnp.concatenate([left, jnp.concatenate([above, corner], 0)], 1)
    eye = jnp.where(
        lax.broadcasted_iota(jnp.int32, (D, D), 0) == lax.broadcasted_iota(jnp.int32, (D, D), 1),
        1.0, 0.0,
    )
    inverse = lax.rsqrt(total_of(eye * gram) + ORTHO_EPS)
    square = gram * (inverse * inverse)
    product = None
    for step in range(5):
        polynomial = NS_ONE * eye + NS_TWO * square + NS_THREE * exact(square, square)
        product = polynomial if product is None else exact(product, polynomial)
        if step < 4:
            square = exact(polynomial, exact(square, polynomial))
    x_end[...] = exact(product, x * inverse)
    for m in range(4 * L):
        @pl.when(w == worker_of(m, wide))
        def _():
            size = ROWS_OF[m % 4] // narrow
            spread_rows(x_sent[m % 4], x_end[:, :size])
            over_peers(w, wide, lambda p: new_copy(m, p).start())
            x_came[m % 4][m // 4] = x_sent[m % 4][w]

    for m in range(4 * L):
        @pl.when(w != worker_of(m, wide))
        def _():
            new_copy(m, w).wait_recv()

    for m in range(4 * L):
        @pl.when(w != worker_of(m, wide))
        def _():
            put_copy(m, w).wait_recv()
            get_copy(m, w).wait_send()

        @pl.when((side == (m % 4) // 2) & (w != worker_of(m, wide)))
        def _():
            block_copy(m, w).wait_send()

        @pl.when(w == worker_of(m, wide))
        def _():
            over_peers(w, wide, lambda p: put_copy(m, p).wait_send())
            over_peers(w, wide, lambda p: new_copy(m, p).wait_send())

    for s in range(levels):
        gram_copy(s).wait_send()
        for copy in small_copies(s):
            copy.wait_send()
    for l in range(L):
        for t in range(steps):
            for copy in step_copies(l, t):
                copy.wait_send()
    over_peers(n, narrow, lambda p: near_copy(p, n).wait_send())
    over_peers(w, wide, lambda p: norm_copy(p, w).wait_send())
    over_peers(me, count, lambda p: slot_copy(p, me).wait_send())
    over_peers(w, wide, lambda p: own_copy(p, w).wait_send())


def finish_call(dmats, dsmall, dslots, requests, loss, moments, local, wide, narrow):
    count = wide * narrow
    levels = levels_of(narrow)
    columns = D // wide
    _, total = packed_offsets(narrow)
    shape = jax.ShapeDtypeStruct
    outs = [shape((1, TOKS), F32), shape((D, local), F32), shape(dsmall.shape[2:], F32)]
    outs += [shape(a.shape, F32) for a in moments + moments]
    vm = pltpu.VMEM
    dma = pltpu.SemaphoreType.DMA
    steps = levels + 1

    def mats_shapes(l):
        sizes, quarters, rows = [], narrow, total
        plan = list(range(levels)) + ["side"] if l % 2 else [0, "side"] + list(range(1, levels))
        for move in plan:
            if move == "side":
                rows //= 2
            else:
                quarters //= 2
            sizes.append(vm((quarters, rows, TOKS), F32))
        return sizes

    mats = [v for l in range(L) for v in mats_shapes(l)]
    small_shapes = [vm((narrow >> (s + 1),) + dsmall.shape[1:], F32) for s in range(levels)]
    largest = max(packed_rows(which, narrow) for which in range(4))
    blocks = [vm((wide, columns, rows // narrow), F32) for rows in ROWS_OF]
    spec = pl.BlockSpec(memory_space=pltpu.VMEM)
    return pl.pallas_call(
        functools.partial(finish_kernel, wide=wide, narrow=narrow),
        out_shape=outs,
        in_specs=[spec] * 9,
        out_specs=[spec] * len(outs),
        scratch_shapes=mats * 2 + small_shapes * 2
        + [
            vm(dslots.shape, BF16),
            vm((count * CAP, local), BF16),
            vm((wide, largest, TOKS), F32),
            vm((wide,) + dsmall.shape[2:], F32),
            vm((2 * TOKS, 2 * TOKS), F32),
            vm((narrow, 1, TOKS), F32),
            vm((wide, 1, TOKS), F32),
        ]
        + blocks * 3
        + [
            vm((D, 2 * TOKS), F32), vm((D, 2 * TOKS), F32),
            vm((levels + 1, 2 * TOKS, TOKS), F32), vm((levels, 2 * TOKS, TOKS), F32),
            dma((count,)), dma((count,)),
            dma((L, steps, narrow)), dma((L, steps, narrow)),
            dma((levels, narrow // 2)), dma((levels, narrow // 2)),
            dma((4 * L,)), dma((wide,)), dma((wide,)), dma((wide,)),
            dma((narrow,)), dma((narrow,)), dma((wide,)), dma((wide,)),
            dma((4 * L,)), dma((wide,)), dma((wide,)), dma((4 * L,)),
            dma((wide,)), dma((4 * L,)), dma((levels,)), dma((levels,)),
        ],
        compiler_params=pltpu.CompilerParams(
            collective_id=1, has_side_effects=True, vmem_limit_bytes=58 << 20
        ),
        name="finish",
    )(dmats, dsmall, dslots, requests, loss, *moments)


def apply_kernel(*refs):
    refs = list(refs)

    def take(number):
        head = refs[:number]
        del refs[:number]
        return head

    stats_ref, start_ref = take(2)
    tables, (gsmall_ref,), smalls = take(4), take(1), take(3)
    weights, ortho, moments = take(4), take(4), take(4)
    out_scalars, out_tables, out_smalls = take(3), take(3), take(3)
    out_weights, out_moments = take(4), take(4)
    factor = jnp.full((1, 1), stats_ref[0, 2], F32)
    table, grad, first, second = (ref[...] for ref in tables)
    for ref, value in zip(out_tables, adam_step(table, factor * grad, first, second)):
        ref[...] = value

    @pl.when(pl.program_id(0) == 0)
    def _():
        out_scalars[0][0, 0] = stats_ref[0, 1]
        out_scalars[1][0, 0] = start_ref[0, CAP + 1]
        out_scalars[2][0, 0] = stats_ref[0, 0]
        small, first, second = (ref[...] for ref in smalls)
        grad = gsmall_ref[: small.shape[0], : small.shape[1]]
        for ref, value in zip(out_smalls, adam_step(small, factor * grad, first, second)):
            ref[...] = value
        for which in range(4):
            scale = math.sqrt(max(1.0, ROWS_OF[which] / D))
            out_weights[which][...] = (
                weights[which][...] * (1.0 - MUON_RATE * DECAY)
                - MUON_RATE * scale * ortho[which][...]
            )
            out_moments[which][...] = moments[which][...]


def apply_call(stats, start_stats, tables, gsmall, smalls, weights, ortho, moments):
    shape = jax.ShapeDtypeStruct
    smem = pl.BlockSpec(memory_space=pltpu.SMEM)
    local = tables[0].shape[1]
    rows = 24
    block = pl.BlockSpec((rows, local), lambda i: (i, 0))

    def whole(array):
        return pl.BlockSpec(array.shape, lambda i, nd=array.ndim: (0,) * nd)

    beside = smalls + weights + ortho + moments
    outs = smalls + weights + moments
    return pl.pallas_call(
        apply_kernel,
        grid=(D // rows,),
        out_shape=[shape((1, 1), F32)] * 3
        + [shape(tables[0].shape, F32)] * 3
        + [shape(a.shape, F32) for a in outs],
        in_specs=[smem, smem] + [block] * 4 + [whole(gsmall)] + [whole(a) for a in beside],
        out_specs=[smem] * 3 + [block] * 3 + [whole(a) for a in outs],
        compiler_params=pltpu.CompilerParams(vmem_limit_bytes=48 << 20),
        name="apply",
    )(stats, start_stats, *tables, gsmall, *beside)


def per_device(
    cat_index, num_values, cell_mask, labels, table, table_first, table_second,
    small, small_first, small_second, w_qkv, w_proj, w_in, w_down,
    mom_qkv, mom_proj, mom_in, mom_down,
):
    wide = lax.axis_size("wide")
    narrow = lax.axis_size("narrow")
    count = wide * narrow
    data_rows = num_values.shape[0]
    pair = 8 if count * CAP <= 2048 else 4
    while data_rows % pair:
        pair //= 2
    flip = lambda v: jnp.swapaxes(v, -1, -2)
    weights = [flip(v) for v in (w_qkv, w_proj, w_in, w_down)]
    moments = [flip(v) for v in (mom_qkv, mom_proj, mom_in, mom_down)]
    smalls = [flip(v) for v in (small, small_first, small_second)]
    tables = [flip(v) for v in (table, table_first, table_second)]
    qkv, proj, w_in_all, down, small_all, rows, slots, requests, stats = gather_call(
        cat_index, cell_mask, weights, smalls[0], tables[0], wide, narrow
    )
    loss, dmats, dsmall, dslots = model_call(
        stats, labels, rows, slots, num_values, cell_mask,
        (qkv, proj, w_in_all, down), small_all, pair, wide, narrow,
    )
    outs = finish_call(
        dmats, dsmall, dslots, requests, loss, moments, table.shape[0], wide, narrow
    )

    def sparse():
        done = apply_call(
            outs[0], stats, [tables[0], outs[1], *tables[1:]], outs[2], smalls, weights,
            list(outs[3:7]), list(outs[7:11]),
        )
        return tuple(v.reshape(()) for v in done[:3]) + tuple(flip(v) for v in done[3:])

    def general():
        return general_step(
            cat_index, num_values, cell_mask, labels, table, table_first, table_second,
            small, small_first, small_second, w_qkv, w_proj, w_in, w_down,
            mom_qkv, mom_proj, mom_in, mom_down,
        )

    return lax.cond(stats[0, CAP] > 0.5, general, sparse)


def normalize(value, gain, shift):
    center = value - jnp.mean(value, -1, keepdims=True)
    spread = jnp.mean(center * center, -1, keepdims=True)
    return center * lax.rsqrt(spread + NORM_EPS) * gain + shift


def gated(gate, upward):
    return jax.nn.gelu(gate, approximate=True) * upward


def rounded(value):
    return value + lax.stop_gradient(value.astype(jnp.bfloat16).astype(jnp.float32) - value)


def contract(left, right, left_dim, right_dim):
    return lax.dot_general(
        left, right, (((left_dim,), (right_dim,)), ((), ())), preferred_element_type=jnp.float32
    )


def split_heads(value, count_rows):
    return value.reshape(count_rows, TOKS, HEADS, HD)


def layer_forward(state, matrices, vector):
    w_qkv, w_proj, w_in, w_down = matrices
    count_rows = state.shape[0]
    flat = state.reshape(-1, D)
    normed = normalize(flat, vector[0], vector[1]).astype(jnp.bfloat16)
    joined = contract(normed, w_qkv, 1, 1)
    query = (joined[:, :D] + vector[4]).astype(jnp.bfloat16)
    keys = joined[:, D : 2 * D].astype(jnp.bfloat16)
    values = (joined[:, 2 * D :] + vector[5]).astype(jnp.bfloat16)
    scores = jnp.einsum(
        "bqhd,bkhd->bhqk",
        split_heads(query, count_rows),
        split_heads(keys, count_rows),
        preferred_element_type=jnp.float32,
    )
    probs = jax.nn.softmax(scores * HD ** (-0.5), axis=-1)
    weights = probs.astype(jnp.bfloat16)
    mixed = jnp.einsum(
        "bhqk,bkhd->bqhd",
        weights,
        split_heads(values, count_rows),
        preferred_element_type=jnp.float32,
    )
    mixed = mixed.reshape(-1, D).astype(jnp.bfloat16)
    after = flat + contract(mixed, w_proj, 1, 1) + vector[6]
    normed_two = normalize(after, vector[2], vector[3]).astype(jnp.bfloat16)
    gate_up = contract(normed_two, w_in, 1, 1)
    hidden = gated(gate_up[:, :FF], gate_up[:, FF:]).astype(jnp.bfloat16)
    output = after + jnp.dot(hidden, w_down, preferred_element_type=jnp.float32) + vector[7]
    return (
        normed,
        query,
        keys,
        values,
        probs,
        weights,
        mixed,
        after,
        normed_two,
        gate_up,
        hidden,
        output.reshape(state.shape),
    )


def layer_backward(state, matrices, vector, grad_out):
    w_qkv, w_proj, w_in, w_down = matrices
    count_rows = state.shape[0]
    flat = state.reshape(-1, D)
    (
        normed,
        query,
        keys,
        values,
        probs,
        weights,
        mixed,
        after,
        normed_two,
        gate_up,
        hidden,
        output,
    ) = layer_forward(state, matrices, vector)
    upstream = grad_out.reshape(-1, D)
    grad_bdown = jnp.sum(upstream, 0)
    up_low = upstream.astype(jnp.bfloat16)
    grad_wdown = contract(hidden, up_low, 0, 0)
    grad_hidden = contract(up_low, w_down, 1, 1)
    _, pull_gate = jax.vjp(gated, gate_up[:, :FF], gate_up[:, FF:])
    grad_gate, grad_up = pull_gate(grad_hidden)
    gate_low = jnp.concatenate([grad_gate, grad_up], 1).astype(jnp.bfloat16)
    grad_win = contract(gate_low, normed_two, 0, 0)
    grad_normed_two = contract(gate_low, w_in, 1, 0)
    _, pull_second = jax.vjp(normalize, after, vector[2], vector[3])
    grad_after_norm, grad_gain_two, grad_shift_two = pull_second(grad_normed_two)
    grad_after = upstream + grad_after_norm
    grad_bproj = jnp.sum(grad_after, 0)
    after_low = grad_after.astype(jnp.bfloat16)
    grad_wproj = contract(after_low, mixed, 0, 0)
    grad_mixed = contract(after_low, w_proj, 1, 0).astype(jnp.bfloat16)
    mixed_heads = split_heads(grad_mixed, count_rows)
    grad_probs = jnp.einsum(
        "bqhd,bkhd->bhqk",
        mixed_heads,
        split_heads(values, count_rows),
        preferred_element_type=jnp.float32,
    )
    grad_values = jnp.einsum(
        "bhqk,bqhd->bkhd", weights, mixed_heads, preferred_element_type=jnp.float32
    ).reshape(-1, D)
    grad_scores = probs * (grad_probs - jnp.sum(grad_probs * probs, -1, keepdims=True))
    scores_low = (grad_scores * HD ** (-0.5)).astype(jnp.bfloat16)
    grad_query = jnp.einsum(
        "bhqk,bkhd->bqhd",
        scores_low,
        split_heads(keys, count_rows),
        preferred_element_type=jnp.float32,
    ).reshape(-1, D)
    grad_keys = jnp.einsum(
        "bhqk,bqhd->bkhd",
        scores_low,
        split_heads(query, count_rows),
        preferred_element_type=jnp.float32,
    ).reshape(-1, D)
    joined_low = jnp.concatenate([grad_query, grad_keys, grad_values], 1).astype(jnp.bfloat16)
    grad_wqkv = contract(joined_low, normed, 0, 0)
    grad_normed = contract(joined_low, w_qkv, 1, 0)
    _, pull_first = jax.vjp(normalize, flat, vector[0], vector[1])
    grad_flat, grad_gain_one, grad_shift_one = pull_first(grad_normed)
    grad_state = (grad_after + grad_flat).reshape(state.shape)
    grad_vector = jnp.stack(
        [
            grad_gain_one,
            grad_shift_one,
            grad_gain_two,
            grad_shift_two,
            jnp.sum(grad_query, 0),
            jnp.sum(grad_values, 0),
            grad_bproj,
            grad_bdown,
        ]
    )
    return (grad_state, (grad_wqkv, grad_wproj, grad_win, grad_wdown), grad_vector)


def head_loss(final, head_rows, num_values, cell_mask, labels):
    normed = normalize(final, head_rows[0], head_rows[1])
    logits = jnp.dot(
        rounded(normed[:, 0]), rounded(head_rows[2 : 2 + NCLASS]).T, precision=lax.Precision.HIGHEST
    )
    hits = labels[:, None] == jnp.arange(NCLASS)[None, :]
    picked = jnp.sum(jnp.where(hits, logits, 0.0), -1)
    predict = jnp.sum(normed[:, 1 : 1 + NUMF] * head_rows[2 + NCLASS :], -1)
    error = predict - num_values
    return jnp.sum(cell_mask.astype(jnp.float32) * error * error) + jnp.sum(
        jax.nn.logsumexp(logits, -1) - picked
    )


def gram_of(matrix):
    return jnp.einsum("lrc,lrd->lcd", matrix, matrix, precision=lax.Precision.HIGHEST)


def gram_sums(first, second, third, fourth):
    return lax.psum((gram_of(first), gram_of(second), gram_of(third), gram_of(fourth)), "narrow")


def orthogonalize(first, second, third, fourth):
    current = [first, second, third, fourth]
    grams = gram_sums(first, second, third, fourth)
    squares = []
    for index_no in range(4):
        inverse = lax.rsqrt(jnp.trace(grams[index_no], axis1=1, axis2=2) + ORTHO_EPS)[:, None, None]
        current[index_no] = current[index_no] * inverse
        squares.append(grams[index_no] * inverse * inverse)
    for step in range(5):
        if step > 0:
            squares = gram_sums(current[0], current[1], current[2], current[3])
        updated = []
        for block, square in zip(current, squares):
            polynomial = NS_TWO * square + NS_THREE * jnp.einsum(
                "lcd,lde->lce", square, square, precision=lax.Precision.HIGHEST
            )
            updated.append(
                NS_ONE * block
                + jnp.einsum("lrc,lcd->lrd", block, polynomial, precision=lax.Precision.HIGHEST)
            )
        current = updated
    return current


def general_step(
    cat_index,
    num_values,
    cell_mask,
    labels,
    table,
    table_first,
    table_second,
    small,
    small_first,
    small_second,
    w_qkv,
    w_proj,
    w_in,
    w_down,
    mom_qkv,
    mom_proj,
    mom_in,
    mom_down,
):
    count_rows = num_values.shape[0]
    keep = 1.0 - cell_mask.astype(jnp.float32)
    masked = jnp.sum(1.0 - keep)
    widened = (
        lax.all_gather(w_qkv, "wide", axis=2, tiled=True),
        lax.all_gather(w_proj, "wide", axis=2, tiled=True),
        lax.all_gather(w_in, "wide", axis=2, tiled=True),
        lax.all_gather(w_down, "wide", axis=2, tiled=True),
        lax.all_gather(small, "wide", axis=1, tiled=True),
    )
    gathered = (
        lax.all_gather(widened[0], "narrow", axis=1, tiled=True),
        lax.all_gather(widened[1], "narrow", axis=1, tiled=True),
        lax.all_gather(widened[2], "narrow", axis=1, tiled=True),
        lax.all_gather(widened[3], "narrow", axis=1, tiled=True),
        lax.all_gather(widened[4], "narrow", axis=0, tiled=True),
    )
    matrices = tuple((part.astype(jnp.bfloat16) for part in gathered[:4]))
    params = gathered[4]
    flat_index = cat_index.reshape(-1)
    piece = lax.all_gather(table.astype(jnp.bfloat16), ("wide", "narrow"), axis=0, tiled=True)
    hits = (flat_index[:, None] == lax.iota(jnp.int32, piece.shape[0])[None, :]).astype(
        jnp.bfloat16
    )
    looked = jnp.dot(hits, piece, preferred_element_type=jnp.float32)
    off_scale = 8 * L + TOKS
    off_fin = off_scale + NUMF + 1
    numeric = (keep * num_values)[:, :, None] * params[off_scale : off_scale + NUMF] + (1.0 - keep)[
        :, :, None
    ] * params[off_scale + NUMF]
    state = (
        jnp.concatenate(
            [
                jnp.zeros((count_rows, 1, D), jnp.float32),
                numeric,
                looked.reshape(count_rows, CATF, D),
            ],
            1,
        )
        + params[8 * L : off_scale]
    )
    inputs = []
    for depth in range(L):
        inputs.append(state)
        state = layer_forward(
            state, tuple((part[depth] for part in matrices)), params[8 * depth : 8 * depth + 8]
        )[-1]

    def head_part(final, head_rows):
        return head_loss(final, head_rows, num_values, cell_mask, labels)

    loss_here, pull_head = jax.vjp(head_part, state, params[off_fin:])
    loss_sum, count = lax.psum((loss_here, masked), ("wide", "narrow"))
    grad_state, grad_head = pull_head(1.0 / count)
    layer_grads = []
    vector_grads = []
    for depth in reversed(range(L)):
        grad_state, grad_mats, grad_vector = layer_backward(
            inputs[depth],
            tuple((part[depth] for part in matrices)),
            params[8 * depth : 8 * depth + 8],
            grad_state,
        )
        layer_grads.insert(0, grad_mats)
        vector_grads.insert(0, grad_vector)
    numeric_grad = grad_state[:, 1 : 1 + NUMF]
    grad_scale = jnp.sum((keep * num_values)[:, :, None] * numeric_grad, 0)
    grad_mask_row = jnp.sum((1.0 - keep)[:, :, None] * numeric_grad, (0, 1))[None]
    small_grad = jnp.concatenate(
        vector_grads + [jnp.sum(grad_state, 0), grad_scale, grad_mask_row, grad_head], 0
    )
    cat_grad = grad_state[:, 1 + NUMF :].reshape(-1, D).astype(jnp.bfloat16)
    rows_here = table.shape[0]
    hits = (
        flat_index[:, None]
        == lax.iota(jnp.int32, lax.axis_size(("wide", "narrow")) * rows_here)[None, :]
    ).astype(jnp.bfloat16)
    table_grad = lax.psum_scatter(
        contract(hits, cat_grad, 0, 0), ("wide", "narrow"), scatter_dimension=0, tiled=True
    )
    stacked = [jnp.stack([grads[which] for grads in layer_grads]) for which in range(4)]
    by_cols = (
        lax.psum_scatter(stacked[0], "wide", scatter_dimension=2, tiled=True),
        lax.psum_scatter(stacked[1], "wide", scatter_dimension=2, tiled=True),
        lax.psum_scatter(stacked[2], "wide", scatter_dimension=2, tiled=True),
        lax.psum_scatter(stacked[3], "wide", scatter_dimension=2, tiled=True),
        lax.psum_scatter(small_grad, "wide", scatter_dimension=1, tiled=True),
    )
    owned = (
        lax.psum_scatter(by_cols[0], "narrow", scatter_dimension=1, tiled=True),
        lax.psum_scatter(by_cols[1], "narrow", scatter_dimension=1, tiled=True),
        lax.psum_scatter(by_cols[2], "narrow", scatter_dimension=1, tiled=True),
        lax.psum_scatter(by_cols[3], "narrow", scatter_dimension=1, tiled=True),
        lax.psum_scatter(by_cols[4], "narrow", scatter_dimension=0, tiled=True),
    )
    squares = jnp.sum(table_grad * table_grad) + sum((jnp.sum(part * part) for part in owned))
    squared = lax.psum(squares, ("wide", "narrow"))
    grad_norm = jnp.sqrt(squared)
    factor = CLIP / jnp.maximum(grad_norm, CLIP)
    new_table, table_one, table_two = adam_step(
        table, factor * table_grad, table_first, table_second
    )
    new_small, small_one, small_two = adam_step(small, factor * owned[4], small_first, small_second)
    weights_old = (w_qkv, w_proj, w_in, w_down)
    moments = (
        MOMENTUM * mom_qkv + factor * owned[0],
        MOMENTUM * mom_proj + factor * owned[1],
        MOMENTUM * mom_in + factor * owned[2],
        MOMENTUM * mom_down + factor * owned[3],
    )
    full_moments = (
        lax.all_gather(moments[0], "wide", axis=2, tiled=True),
        lax.all_gather(moments[1], "wide", axis=2, tiled=True),
        lax.all_gather(moments[2], "wide", axis=2, tiled=True),
        lax.all_gather(moments[3], "wide", axis=2, tiled=True),
    )
    width = w_qkv.shape[2]
    column = lax.axis_index("wide") * width
    ortho = orthogonalize(full_moments[0], full_moments[1], full_moments[2], full_moments[3])
    updated = []
    for weight, block in zip(weights_old, ortho):
        scale = math.sqrt(max(1.0, weight.shape[1] * lax.axis_size("narrow") / D))
        own = lax.dynamic_slice_in_dim(block, column, width, 2)
        updated.append(weight * (1.0 - MUON_RATE * DECAY) - MUON_RATE * scale * own)
    return (
        loss_sum,
        count,
        grad_norm,
        new_table,
        table_one,
        table_two,
        new_small,
        small_one,
        small_two,
        updated[0],
        updated[1],
        updated[2],
        updated[3],
        moments[0],
        moments[1],
        moments[2],
        moments[3],
    )


def solution(mesh):
    rows = P(("wide", "narrow"), None)
    square = P("narrow", "wide")
    cube = P(None, "narrow", "wide")
    return jax.shard_map(
        per_device,
        mesh=mesh,
        in_specs=(rows, rows, rows, P(("wide", "narrow")), rows, rows, rows)
        + (square,) * 3 + (cube,) * 8,
        out_specs=(P(), P(), P(), rows, rows, rows) + (square,) * 3 + (cube,) * 8,
        check_vma=False,
    )
```

```python
import functools
import math

import jax
import jax.numpy as jnp
import numpy as np
from jax import lax
from jax.experimental import pallas as pl
from jax.experimental.pallas import tpu as pltpu
from jax.sharding import PartitionSpec as P

D = 192
HEADS = 8
HD = 24
FF = 256
L = 2
NUMF = 95
CATF = 32
NCLASS = 7
STEP = 10
TOKS = 128

NORM_EPS = 1e-05
CLIP = 0.002
BETA_ONE = 0.9
BETA_TWO = 0.95
ADAM_EPS = 1e-08
ADAM_RATE = 0.2
MUON_RATE = 1.0
MOMENTUM = 0.95
DECAY = 0.01
ORTHO_EPS = 1e-20
NS_ONE = 3.4445
NS_TWO = -4.775
NS_THREE = 2.0315
GELU_A = math.sqrt(2.0 / math.pi)
GELU_B = 0.044715
SCALE = HD ** (-0.5)

F32 = jnp.float32
BF16 = jnp.bfloat16
MESH = pl.DeviceIdType.MESH

ROWS_OF = (3 * D, D, 2 * FF, FF)
ORDER = (2, 0, 1, 3)
NSR = 8 * L + TOKS + NUMF + 1 + 2 + NCLASS + NUMF
OFF_SCALE = 8 * L + TOKS
OFF_FIN = OFF_SCALE + NUMF + 1
CAP = 32
PACK = CAP + CAP // 2


def mm(left, right, left_dim=1, right_dim=0):
    return lax.dot_general(
        left, right, (((left_dim,), (right_dim,)), ((), ())), preferred_element_type=F32
    )


def up_to(value, unit):
    return -(-value // unit) * unit


def split_two(value):
    high = value.astype(BF16)
    return high, (value - high.astype(F32)).astype(BF16)


def split_three(value):
    high = value.astype(BF16)
    rest = value - high.astype(F32)
    middle = rest.astype(BF16)
    return high, middle, (rest - middle.astype(F32)).astype(BF16)


def place(wide, narrow):
    w = lax.axis_index("wide")
    n = lax.axis_index("narrow")
    return w, n, w * narrow + n


def greet_all(me, count, narrow):
    barrier = pltpu.get_barrier_semaphore()

    def signal(k, carry):
        p = lax.rem(me + k, count)
        pl.semaphore_signal(
            barrier, inc=1, device_id=(p // narrow, lax.rem(p, narrow)), device_id_type=MESH
        )
        return carry

    lax.fori_loop(1, count, signal, 0)
    return barrier


def quarter_offsets(narrow):
    offsets, total = {}, 0
    for which in ORDER:
        offsets[which] = total
        total += ROWS_OF[which] // narrow
    return offsets, total


def gather_kernel(
    cat_ref, mask_ref, qkv_ref, proj_ref, in_ref, down_ref, small_ref, table_ref, pick_ref,
    out_qkv, out_proj, out_in, out_down, out_small, out_rows, out_slots, out_requests, out_stats,
    gat_one, gat_two, ask, table_s, table_low, answers, landed,
    far_send, far_recv, step_send, step_recv, ask_send, ask_recv, row_send, row_recv, table_sem,
    *, wide, narrow, chunk,
):
    count = wide * narrow
    levels = levels_of(narrow)
    w, n, me = place(wide, narrow)
    side, far = lax.rem(w, 2), w // 2
    fars = wide // 2
    table_copy = pltpu.make_async_copy(table_ref, table_s, table_sem)
    table_copy.start()
    barrier = greet_all(me, count, narrow)

    def coords(p):
        return (p // narrow, lax.rem(p, narrow))

    offsets, total = quarter_offsets(narrow)
    width = qkv_ref.shape[1]
    rows_pad = gat_one.shape[3]
    cut = gat_one.shape[4]
    shards = (qkv_ref, proj_ref, in_ref, down_ref)
    pieces = [
        jnp.concatenate([shards[which][l] for which in ORDER], 1) for l in range(L)
    ]
    if rows_pad > L * width:
        pieces.append(jnp.zeros((rows_pad - L * width, total), F32))
    packed = jnp.concatenate(pieces, 0).astype(BF16)
    gat_one[n, side, far] = packed[:, :cut]
    gat_two[n, side, far] = packed[:, cut:]
    small = small_ref[...]
    own_rows = small.shape[1]
    small_pad = out_small.shape[3]
    if small_pad > width:
        small = jnp.concatenate([small, jnp.zeros((small_pad - width, own_rows), F32)], 0)
    out_small[n, side, far] = jnp.concatenate(
        [small, jnp.zeros((small_pad, TOKS - own_rows), F32)], 1
    )

    data_rows, per_row = cat_ref.shape
    entries = data_rows * per_row
    local = table_s.shape[1]
    index_row = jnp.concatenate([cat_ref[r : r + 1, :] for r in range(data_rows)], 1)
    owner_row = jnp.zeros_like(index_row)
    for k in range(1, count):
        owner_row = owner_row + (index_row >= k * local).astype(jnp.int32)
    base_row = owner_row * local
    index_col = jnp.transpose(jnp.broadcast_to(index_row, (8, entries)))[:, :1]
    before = lax.broadcasted_iota(jnp.int32, (entries, entries), 0)
    after = lax.broadcasted_iota(jnp.int32, (entries, entries), 1)
    same = index_col == index_row
    first_col = 1.0 - jnp.max(jnp.where(same & (after < before), 1.0, 0.0), 1, keepdims=True)
    first_row = 1.0 - jnp.max(jnp.where(same & (before < after), 1.0, 0.0), 0, keepdims=True)
    lower = (index_col >= base_row) & (index_col < index_row)
    rank_row = jnp.sum(jnp.where(lower, first_col, 0.0), 0, keepdims=True).astype(jnp.int32)
    slot_row = owner_row * CAP + rank_row
    none = jnp.full((1, TOKS - per_row), -1, jnp.int32)
    for r in range(data_rows):
        out_slots[r : r + 1, :] = jnp.concatenate(
            [none, slot_row[:, r * per_row : (r + 1) * per_row]], 1
        )
    over = jnp.max(jnp.where(rank_row >= CAP, 1.0, 0.0), 1, keepdims=True)
    hidden_cells = jnp.sum(jnp.sum(mask_ref[...].astype(F32), 0, keepdims=True), 1, keepdims=True)
    place_row = index_row - base_row
    owners = lax.broadcasted_iota(jnp.int32, (count, entries), 0)
    mine = jnp.where(owners == owner_row, first_row, 0.0)
    high = lax.shift_right_logical(place_row, 6)
    low = place_row - high * 64
    at_rank = jnp.where(
        lax.broadcasted_iota(jnp.int32, (TOKS, entries), 0) == rank_row, 1.0, 0.0
    ).astype(BF16)
    wanted = 64.0 * mm((mine * high.astype(F32)).astype(BF16), at_rank, 1, 1) + mm(
        (mine * low.astype(F32)).astype(BF16), at_rank, 1, 1
    )
    lane = lax.broadcasted_iota(jnp.int32, (count, TOKS), 1)
    wanted = jnp.where(lane < CAP, wanted, 0.0)
    wanted = jnp.where(lane == CAP, over, wanted)
    wanted = jnp.where(lane == CAP + 1, hidden_cells, wanted)
    for k in range(count):
        ask[k] = wanted[k : k + 1]

    pl.semaphore_wait(barrier, count - 1)

    def over_peers(origin, size, body):
        def run(k, carry):
            body(lax.rem(origin + k, size))
            return carry

        lax.fori_loop(1, size, run, 0)

    def ask_copy(p, slot):
        return pltpu.make_async_remote_copy(
            src_ref=ask.at[p], dst_ref=out_requests.at[slot], send_sem=ask_send.at[p],
            recv_sem=ask_recv.at[slot], device_id=coords(p), device_id_type=MESH,
        )

    def row_copy(p, slot):
        return pltpu.make_async_remote_copy(
            src_ref=answers.at[p], dst_ref=landed.at[slot], send_sem=row_send.at[p],
            recv_sem=row_recv.at[slot], device_id=coords(p), device_id_type=MESH,
        )

    arrays = (gat_one, gat_two, out_small)

    def far_copies(p, slot):
        return [
            pltpu.make_async_remote_copy(
                src_ref=array.at[n, side, far], dst_ref=array.at[n, side, slot],
                send_sem=far_send.at[a, p], recv_sem=far_recv.at[a, slot],
                device_id=(p * 2 + side, n), device_id_type=MESH,
            )
            for a, array in enumerate(arrays)
        ]

    high_levels = list(range(levels - 1, 0, -1))
    plans = (
        high_levels + ["side"] + [0] * (levels > 0),
        ["side"] + high_levels + [0] * (levels > 0),
    )
    steps = len(plans[0])

    def step_copies(t):
        copies = []
        for a, array in enumerate(arrays):
            plan = plans[min(a, 1)]
            move = plan[t]
            done = plan[:t]
            lowest = min([v for v in done if v != "side"], default=levels)
            for j in range(1 << (levels - lowest)):
                block = lax.rem(n, 1 << lowest) + (j << lowest)
                if move == "side":
                    target = (w + 1 - 2 * side, n)
                else:
                    bit = lax.rem(n // (1 << move), 2)
                    target = (w, n + (1 - 2 * bit) * (1 << move))
                ref = array.at[block] if "side" in done else array.at[block, side]
                copies.append(
                    pltpu.make_async_remote_copy(
                        src_ref=ref, dst_ref=ref, send_sem=step_send.at[t, a, j],
                        recv_sem=step_recv.at[t, a, j], device_id=target, device_id_type=MESH,
                    )
                )
        return copies

    def step_arrivals(t):
        copies = []
        for a, array in enumerate(arrays):
            plan = plans[min(a, 1)]
            move = plan[t]
            done = plan[:t]
            lowest = min([v for v in done if v != "side"], default=levels)
            for j in range(1 << (levels - lowest)):
                if move == "side":
                    there, whose, target = n, 1 - side, (w + 1 - 2 * side, n)
                else:
                    bit = lax.rem(n // (1 << move), 2)
                    there, whose = n + (1 - 2 * bit) * (1 << move), side
                    target = (w, there)
                block = lax.rem(there, 1 << lowest) + (j << lowest)
                ref = array.at[block] if "side" in done else array.at[block, whose]
                copies.append(
                    pltpu.make_async_remote_copy(
                        src_ref=ref, dst_ref=ref, send_sem=step_send.at[t, a, j],
                        recv_sem=step_recv.at[t, a, j], device_id=target, device_id_type=MESH,
                    )
                )
        return copies

    def start_far(p):
        for copy in far_copies(p, far):
            copy.start()

    def end_far(p):
        for copy in far_copies(p, p):
            copy.wait_recv()

    over_peers(me, count, lambda p: ask_copy(p, me).start())
    over_peers(far, fars, start_far)
    out_requests[me] = ask[me]
    table_copy.wait()
    table_low[...] = table_s[...].astype(BF16)
    over_peers(far, fars, end_far)
    for copy in step_copies(0):
        copy.start()
    over_peers(me, count, lambda p: ask_copy(p, p).wait_recv())

    eye = lax.broadcasted_iota(jnp.int32, (CAP, TOKS), 0) == lax.broadcasted_iota(
        jnp.int32, (CAP, TOKS), 1
    )
    spots = lax.broadcasted_iota(jnp.int32, (CAP, local), 1)

    def wanted_hits(q):
        row = jnp.broadcast_to(out_requests[q], (CAP, TOKS))
        column = jnp.sum(jnp.where(eye, row, 0.0), 1, keepdims=True).astype(jnp.int32)
        return jnp.where(spots == column, 1.0, 0.0).astype(BF16)

    half_lane = lax.broadcasted_iota(jnp.int32, (CAP // 2, TOKS), 1) < D - TOKS

    def answer(c, carry):
        found = [wanted_hits(c * chunk + j) for j in range(chunk)]
        got = mm(jnp.concatenate(found, 0), table_low[...], 1, 1)
        got = jnp.concatenate([got, jnp.zeros((got.shape[0], 2 * TOKS - D), F32)], 1)
        for j in range(chunk):
            q = c * chunk + j
            part = got[j * CAP : (j + 1) * CAP]
            tail = part[:, TOKS:]
            rolled = pltpu.roll(tail[CAP // 2 :], D - TOKS, 1)
            packed = jnp.where(half_lane, tail[: CAP // 2], rolled)
            answers[q] = jnp.concatenate([part[:, :TOKS], packed], 0).astype(BF16)

            @pl.when(q != me)
            def _():
                row_copy(q, me).start()

        return carry

    def next_step(t):
        for copy in step_arrivals(t):
            copy.wait_recv()
        if t + 1 < steps:
            for copy in step_copies(t + 1):
                copy.start()

    lax.fori_loop(0, count // chunk // 2, answer, 0)
    next_step(0)
    lax.fori_loop(count // chunk // 2, count // chunk, answer, 0)
    landed[me] = answers[me]
    for t in range(1, steps):
        next_step(t)

    outs = (out_qkv, out_proj, out_in, out_down)
    for q in range(narrow):
        held = jnp.concatenate(
            [
                gat_one[q].reshape(wide * rows_pad, cut),
                gat_two[q].reshape(wide * rows_pad, total - cut),
            ],
            1,
        )
        for l in range(L):
            matrix = mm(held, pick_ref[l], 0, 0).astype(BF16)
            for which in ORDER:
                size = ROWS_OF[which] // narrow
                outs[which][l, q * size : (q + 1) * size] = matrix[
                    offsets[which] : offsets[which] + size
                ]

    requests = out_requests[...]
    reached = jnp.max(requests, 0)
    summed = jnp.sum(requests, 0)
    lane = lax.broadcasted_iota(jnp.int32, (1, TOKS), 1)
    out_stats[...] = jnp.where(lane == CAP, reached, summed)

    over_peers(me, count, lambda p: row_copy(p, p).wait_recv())
    out_rows[...] = spread_slots(landed[...].astype(F32)).astype(BF16)

    def drain_far(p):
        for copy in far_copies(p, far):
            copy.wait_send()

    over_peers(far, fars, drain_far)
    for t in range(steps):
        for copy in step_copies(t):
            copy.wait_send()
    over_peers(me, count, lambda p: ask_copy(p, me).wait_send())
    over_peers(me, count, lambda p: row_copy(p, me).wait_send())


def levels_of(size):
    return size.bit_length() - 1


def spread_slots(packed):
    owners = packed.shape[0]
    head = packed[:, :CAP].reshape(owners * CAP, TOKS)
    tail = packed[:, CAP:].reshape(owners * (CAP // 2), TOKS)
    moved = pltpu.roll(tail, D - TOKS, 1).reshape(owners, CAP // 2, TOKS)
    tail = jnp.concatenate([tail.reshape(owners, CAP // 2, TOKS), moved], 1)
    return jnp.concatenate([head, tail.reshape(owners * CAP, TOKS)[:, : D - TOKS]], 1)


def gather_call(cat_index, cell_mask, shards_t, small_t, table_t, wide, narrow):
    count = wide * narrow
    levels = levels_of(narrow)
    width = small_t.shape[0]
    rows_pad = up_to(L * width, 16)
    small_pad = up_to(width, 8)
    _, total = quarter_offsets(narrow)
    cut = up_to(total // 2, TOKS)
    pick = np.zeros((L, wide * rows_pad, D), np.float32)
    for l in range(L):
        for block in range(wide):
            at = (block % 2) * (wide // 2) + block // 2
            for c in range(width):
                pick[l, at * rows_pad + l * width + c, block * width + c] = 1.0
    local = table_t.shape[1]
    shape = jax.ShapeDtypeStruct
    outs = [shape((L, rows, D), BF16) for rows in ROWS_OF] + [
        shape((narrow, 2, wide // 2, small_pad, TOKS), F32),
        shape((count * CAP, D), BF16),
        shape((cat_index.shape[0], TOKS), jnp.int32),
        shape((count, 1, TOKS), F32),
        shape((1, TOKS), F32),
    ]
    vmem = pl.BlockSpec(memory_space=pltpu.VMEM)
    vm = pltpu.VMEM
    dma = pltpu.SemaphoreType.DMA
    return pl.pallas_call(
        functools.partial(gather_kernel, wide=wide, narrow=narrow, chunk=8),
        out_shape=outs,
        in_specs=[vmem] * 7 + [pl.BlockSpec(memory_space=pl.ANY), vmem],
        out_specs=[vmem] * len(outs),
        scratch_shapes=[
            vm((narrow, 2, wide // 2, rows_pad, cut), BF16),
            vm((narrow, 2, wide // 2, rows_pad, total - cut), BF16),
            vm((count, 1, TOKS), F32),
            vm((D, local), F32),
            vm((D, local), BF16),
            vm((count, PACK, TOKS), BF16),
            vm((count, PACK, TOKS), BF16),
            dma((3, wide // 2)), dma((3, wide // 2)),
            dma((levels + 1, 3, narrow)), dma((levels + 1, 3, narrow)),
            dma((count,)), dma((count,)), dma((count,)), dma((count,)), dma(()),
        ],
        compiler_params=pltpu.CompilerParams(
            collective_id=0, has_side_effects=True, vmem_limit_bytes=62 << 20
        ),
        name="gather",
    )(cat_index, cell_mask, *shards_t, small_t, table_t, jnp.asarray(pick, BF16))


def lanes(vector, width):
    return jnp.concatenate([vector] * (width // vector.shape[1]), 1)


def fold(value):
    total = value[:, :TOKS]
    for start in range(TOKS, value.shape[1], TOKS):
        total = total + value[:, start : start + TOKS]
    return total


def norm_forward(value, gain, shift):
    center = value - jnp.sum(value, 0, keepdims=True) * (1.0 / D)
    spread = jnp.sum(center * center, 0, keepdims=True) * (1.0 / D)
    inverse = lax.rsqrt(spread + NORM_EPS)
    unit = center * inverse
    return unit, inverse, unit * gain + shift


def norm_backward(unit, inverse, grad_unit):
    mean_one = jnp.sum(grad_unit, 0, keepdims=True) * (1.0 / D)
    mean_two = jnp.sum(grad_unit * unit, 0, keepdims=True) * (1.0 / D)
    return inverse * (grad_unit - mean_one - unit * mean_two)


NVEC = 8 * L + 3
ROOM = TOKS // CATF


def model_kernel(
    stats_ref, labels_ref, rows_ref, slots_ref, num_ref, mask_ref,
    qkv_ref, proj_ref, in_ref, down_ref, small_ref,
    loss_ref, dmats_ref, dsmall_ref, dslots_ref,
    rows_t, qkv_t, proj_t, in_t, down_t, tok_s, scale_s, rec_s, class_s, class_t_s,
    dtok_s, dscale_s, drec_s, dclass_s, slots_acc,
    vecb, probs_s, unit_one_s, inv_one_s, normed_s, q_s, k_s, v_s, mixed_s,
    unit_two_s, inv_two_s, normed_two_s, gate_s, hidden_s, acc_s, looked_s, vt_s, wide_s, low_s, ds_s, qt_s,
    qkv_acc, proj_acc, in_acc, down_acc, num_s, mask_s, coef_s,
    *, pair, wide, narrow,
):
    width = pair * TOKS
    blocks = slots_ref.shape[0] // pair
    columns = D // wide
    own_rows = NSR // narrow
    slots = rows_ref.shape[0]
    offsets, _ = packed_offsets(narrow)
    mats_acc = (qkv_acc, proj_acc, in_acc, down_acc)
    inv_count = 1.0 / jnp.full((1, 1), stats_ref[0, CAP + 1], F32)
    data_rows = slots_ref.shape[0]
    gap = jnp.zeros((data_rows, 1), F32)
    gap_tail = jnp.zeros((data_rows, TOKS - 1 - NUMF), F32)
    masked = mask_ref[...].astype(F32)
    num_s[...] = jnp.concatenate([gap, num_ref[...], gap_tail], 1)
    mask_s[...] = jnp.concatenate([gap, masked, gap_tail], 1)
    coef_s[...] = jnp.concatenate([gap, (1.0 - masked) * num_ref[...], gap_tail], 1)

    rows_t[...] = jnp.transpose(rows_ref[...].astype(F32)).astype(BF16)
    for l in range(L):
        qkv_t[l] = jnp.transpose(qkv_ref[l].astype(F32)).astype(BF16)
        proj_t[l] = jnp.transpose(proj_ref[l].astype(F32)).astype(BF16)
        in_t[l] = jnp.transpose(in_ref[l].astype(F32)).astype(BF16)
        down_t[l] = jnp.transpose(down_ref[l].astype(F32)).astype(BF16)
    pieces = []
    for n in range(narrow):
        piece = jnp.concatenate([small_ref[n, w % 2, w // 2, :columns] for w in range(wide)], 0)
        pieces.append(piece[:, :own_rows])
    small = jnp.concatenate(pieces, 1)
    for i in range(NVEC):
        at = i if i < 8 * L else (OFF_FIN + i - 8 * L if i < 8 * L + 2 else OFF_SCALE + NUMF)
        vecb[i] = jnp.broadcast_to(small[:, at : at + 1], (D, TOKS))
    gap_one = jnp.zeros((D, 1), F32)
    gap_end = jnp.zeros((D, TOKS - 1 - NUMF), F32)
    tok_s[...] = small[:, 8 * L : OFF_SCALE]
    scale_s[...] = jnp.concatenate([gap_one, small[:, OFF_SCALE : OFF_SCALE + NUMF], gap_end], 1)
    rec_s[...] = jnp.concatenate([gap_one, small[:, OFF_FIN + 2 + NCLASS :], gap_end], 1)
    class_t = jnp.concatenate(
        [small[:, OFF_FIN + 2 : OFF_FIN + 2 + NCLASS], jnp.zeros((D, TOKS - NCLASS), F32)], 1
    )
    class_s[...] = jnp.transpose(class_t)[:16].astype(BF16)
    class_t_s[...] = jnp.concatenate([class_t[:, :16]] * 3, 1).astype(BF16)
    for ref in (loss_ref, *mats_acc, dtok_s, dscale_s, drec_s, dclass_s, acc_s):
        ref[...] = jnp.zeros_like(ref)

    def vec(i):
        return lanes(vecb[i], width)

    def head_rows(value, h, b):
        return value[h * HD : h * HD + HD, b * TOKS : b * TOKS + TOKS]

    def head_mask(h):
        lane = lax.broadcasted_iota(jnp.int32, (1, D), 1)
        return jnp.where((lane >= h * HD) & (lane < h * HD + HD), 1.0, 0.0).astype(BF16)

    def by_head(value):
        return jnp.concatenate([value * head_mask(h) for h in range(HEADS)], 0)

    def by_rows(value):
        row = lax.broadcasted_iota(jnp.int32, value.shape, 0)
        return jnp.concatenate([value * jnp.where((row >= h * HD) & (row < h * HD + HD), 1.0, 0.0).astype(BF16) for h in range(HEADS)], 1)

    def add_mats(l, which, value):
        mats_acc[which][l] += value

    def add_vec(i, value):
        acc_s[i] += fold(value)

    def forward(l, x):
        base = 8 * l
        unit, inverse, normed = norm_forward(x, vec(base), vec(base + 1))
        normed = normed.astype(BF16)
        unit_one_s[l] = unit
        inv_one_s[l] = inverse
        normed_s[l] = normed
        joined = mm(qkv_ref[l], normed)
        q_f = joined[:D] + vec(base + 4)
        k_f = joined[D : 2 * D]
        v_f = joined[2 * D :] + vec(base + 5)
        k_t = jnp.transpose(k_f).astype(BF16)
        vt_s[l] = jnp.transpose(v_f).astype(BF16)
        q_low = q_f.astype(BF16)
        qt_s[l] = jnp.transpose(q_f).astype(BF16)
        mixed_cols = []
        for b in range(pair):
            for h in range(HEADS):
                qh = head_rows(q_f, h, b).astype(BF16)
                kh = head_rows(k_f, h, b).astype(BF16)
                vh = head_rows(v_f, h, b).astype(BF16)
                u = b * HEADS + h
                q_s[l, u] = qh
                k_s[l, u] = kh
                v_s[l, u] = vh
        for b in range(pair):
            span = slice(b * TOKS, (b + 1) * TOKS)
            wide_s[b] = mm(k_t[span], by_rows(q_low[:, span]))
        for b in range(pair):
            for h in range(HEADS):
                u = b * HEADS + h
                scores = wide_s[b, :, h * TOKS : (h + 1) * TOKS]
                top = jnp.max(scores, 0, keepdims=True)
                weight = jnp.exp((scores - top) * SCALE)
                probs = weight * (1.0 / jnp.sum(weight, 0, keepdims=True))
                probs_s[l, u] = probs
                low_s[l, b, :, h * TOKS : (h + 1) * TOKS] = probs.astype(BF16)
        for b in range(pair):
            rows = []
            for h in range(HEADS):
                u = b * HEADS + h
                rows.append(mm(v_s[l, u], low_s[l, b, :, h * TOKS : (h + 1) * TOKS]))
            mixed_cols.append(jnp.concatenate(rows, 0))
        mixed = jnp.concatenate(mixed_cols, 1).astype(BF16)
        mixed_s[l] = mixed
        after = x + mm(proj_ref[l], mixed) + vec(base + 6)
        unit, inverse, normed = norm_forward(after, vec(base + 2), vec(base + 3))
        normed = normed.astype(BF16)
        unit_two_s[l] = unit
        inv_two_s[l] = inverse
        normed_two_s[l] = normed
        gate_up = mm(in_ref[l], normed)
        gate_s[l] = gate_up
        gate, up = gate_up[:FF], gate_up[FF:]
        inner = GELU_A * (gate + GELU_B * gate * gate * gate)
        hidden = (0.5 * gate * (1.0 + jnp.tanh(inner)) * up).astype(BF16)
        hidden_s[l] = hidden
        return after + mm(down_t[l], hidden) + vec(base + 7)

    def backward(l, dout):
        base = 8 * l
        add_vec(base + 7, dout)
        up_low = dout.astype(BF16)
        add_mats(l, 3, mm(hidden_s[l], up_low, 1, 1))
        dhidden = mm(down_ref[l], up_low)
        gate, up = gate_s[l, :FF], gate_s[l, FF:]
        square = gate * gate
        tanh = jnp.tanh(GELU_A * (gate + GELU_B * square * gate))
        half = 0.5 * (1.0 + tanh)
        slope = half + 0.5 * gate * (1.0 - tanh * tanh) * (GELU_A * (1.0 + 3.0 * GELU_B * square))
        dgate = dhidden * up * slope
        dup = dhidden * (gate * half)
        dgl = jnp.concatenate([dgate, dup], 0).astype(BF16)
        add_mats(l, 2, mm(dgl, normed_two_s[l], 1, 1))
        dnormed = mm(in_t[l], dgl)
        unit = unit_two_s[l]
        add_vec(base + 2, dnormed * unit)
        add_vec(base + 3, dnormed)
        dafter = dout + norm_backward(unit, inv_two_s[l], dnormed * vec(base + 2))
        add_vec(base + 6, dafter)
        after_low = dafter.astype(BF16)
        add_mats(l, 1, mm(after_low, mixed_s[l], 1, 1))
        dmixed = mm(proj_t[l], after_low)
        dmixed_low = dmixed.astype(BF16)
        dm_t = jnp.transpose(dmixed).astype(BF16)
        q_cols, k_cols, v_cols = [], [], []
        for b in range(pair):
            span = slice(b * TOKS, (b + 1) * TOKS)
            wide_s[b] = mm(vt_s[l, span], by_rows(dmixed_low[:, span]))
        for b in range(pair):
            for h in range(HEADS):
                u = b * HEADS + h
                probs = probs_s[l, u]
                dprobs = wide_s[b, :, h * TOKS : (h + 1) * TOKS]
                inner = jnp.sum(dprobs * probs, 0, keepdims=True)
                ds_s[b, :, h * TOKS : (h + 1) * TOKS] = (probs * (dprobs - inner) * SCALE).astype(BF16)
        for b in range(pair):
            q_rows = []
            for h in range(HEADS):
                u = b * HEADS + h
                q_rows.append(mm(k_s[l, u], ds_s[b, :, h * TOKS : (h + 1) * TOKS]))
            q_cols.append(jnp.concatenate(q_rows, 0))
            span = slice(b * TOKS, (b + 1) * TOKS)
            v_cols.append(mm(low_s[l, b], by_head(dm_t[span])))
            k_cols.append(mm(ds_s[b], by_head(qt_s[l, span])))
        dq = jnp.concatenate(q_cols, 1)
        dk = jnp.transpose(jnp.concatenate(k_cols, 0))
        dv = jnp.transpose(jnp.concatenate(v_cols, 0))
        add_vec(base + 4, dq)
        add_vec(base + 5, dv)
        dj = jnp.concatenate([dq, dk, dv], 0).astype(BF16)
        add_mats(l, 0, mm(dj, normed_s[l], 1, 1))
        dnormed = mm(qkv_t[l], dj)
        unit = unit_one_s[l]
        add_vec(base, dnormed * unit)
        add_vec(base + 1, dnormed)
        return dafter + norm_backward(unit, inv_one_s[l], dnormed * vec(base))

    def step(i, carry):
        def row_of(ref):
            return jnp.concatenate([ref[pl.ds(i * pair + b, 1), :] for b in range(pair)], 1)

        coef = row_of(coef_s)
        num = row_of(num_s)
        mask = row_of(mask_s)
        lane = lax.broadcasted_iota(jnp.int32, (D, TOKS), 1)
        placed = []
        for b in range(pair):
            found = looked_s[i, :, (b // ROOM) * TOKS : (b // ROOM + 1) * TOKS]
            shift = (TOKS - CATF - b * CATF) % TOKS
            moved = pltpu.roll(found, shift, 1) if shift else found
            placed.append(jnp.where(lane < TOKS - CATF, 0.0, moved))
        x = jnp.concatenate(placed, 1) + lanes(tok_s[...], width)
        x = x + coef * lanes(scale_s[...], width) + mask * vec(8 * L + 2)
        for l in range(L):
            x = forward(l, x)
        unit, inverse, final = norm_forward(x, vec(8 * L), vec(8 * L + 1))
        rec = lanes(rec_s[...], width)
        error = jnp.sum(final * rec, 0, keepdims=True) - num
        final_low = final.astype(BF16)
        logits = mm(class_s[...], final_low)
        row = lax.broadcasted_iota(jnp.int32, logits.shape, 0)
        lane = lax.broadcasted_iota(jnp.int32, logits.shape, 1)
        live = row < NCLASS
        logits = jnp.where(live, logits, -1e30)
        top = jnp.max(logits, 0, keepdims=True)
        weight = jnp.where(live, jnp.exp(logits - top), 0.0)
        sums = jnp.sum(weight, 0, keepdims=True)
        first = (lane % TOKS) == 0
        label = jnp.concatenate(
            [jnp.full((1, TOKS), labels_ref[i * pair + b], jnp.int32) for b in range(pair)], 1
        )
        hit = jnp.where(first & (row == label), 1.0, 0.0)
        firsts = jnp.where(first[:1], 1.0, 0.0)
        picked = jnp.sum(jnp.where(hit > 0, logits, 0.0), 0, keepdims=True)
        loss_ref[...] += fold(mask * error * error + firsts * (top + jnp.log(sums)) - picked)
        dlogits = (firsts * weight / sums - hit) * inv_count
        dpredict = (2.0 * inv_count) * mask * error
        parts = jnp.concatenate([p.astype(F32) for p in split_three(dlogits)], 0).astype(BF16)
        dclass_s[...] += mm(final_low, parts, 1, 1)
        drec_s[...] += fold(final * dpredict)
        dfinal = rec * dpredict + mm(class_t_s[...], parts)
        add_vec(8 * L, dfinal * unit)
        add_vec(8 * L + 1, dfinal)
        dx = norm_backward(unit, inverse, dfinal * vec(8 * L))
        for l in reversed(range(L)):
            dx = backward(l, dx)
        dtok_s[...] += fold(dx)
        dscale_s[...] += fold(coef * dx)
        acc_s[8 * L + 2] += fold(mask * dx)
        packed = [jnp.zeros((D, TOKS), F32) for _ in range(groups)]
        group = lax.broadcasted_iota(jnp.int32, (D, TOKS), 1) // CATF
        for b in range(pair):
            part = dx[:, b * TOKS : (b + 1) * TOKS]
            shift = (b * CATF + CATF) % TOKS
            if shift:
                part = pltpu.roll(part, shift, 1)
            packed[b // ROOM] = jnp.where(group == b % ROOM, part, packed[b // ROOM])
        for at in range(groups):
            looked_s[i, :, at * TOKS : (at + 1) * TOKS] = packed[at]
        return carry

    groups = -(-pair // ROOM)
    spare = groups * TOKS - pair * CATF

    def hits_of(i):
        pieces = [
            slots_ref[i * pair + b : i * pair + b + 1, TOKS - CATF :] for b in range(pair)
        ]
        if spare:
            pieces.append(jnp.full((1, spare), -1, jnp.int32))
        slot = lax.broadcasted_iota(jnp.int32, (slots, groups * TOKS), 0)
        return jnp.where(slot == jnp.concatenate(pieces, 1), 1.0, 0.0).astype(BF16)

    for i in range(blocks):
        looked_s[i] = mm(rows_t[...], hits_of(i))
    lax.fori_loop(0, blocks, step, 0)
    slots_acc[...] = jnp.zeros_like(slots_acc)
    for i in range(blocks):
        slots_acc[...] += mm(hits_of(i), looked_s[i].astype(BF16), 1, 1)

    dvec = [jnp.sum(acc_s[i], 1, keepdims=True) for i in range(NVEC)]
    dclass = dclass_s[...]
    dclass = dclass[:, :16] + dclass[:, 16:32] + dclass[:, 32:]
    dsmall = jnp.concatenate(
        dvec[: 8 * L]
        + [dtok_s[...], dscale_s[:, 1 : 1 + NUMF], dvec[8 * L + 2]]
        + dvec[8 * L : 8 * L + 2]
        + [dclass[:, :NCLASS], drec_s[:, 1 : 1 + NUMF]],
        1,
    )
    blank = jnp.zeros((D, TOKS - own_rows), F32)
    for n in range(narrow):
        piece = jnp.concatenate([dsmall[:, n * own_rows : (n + 1) * own_rows], blank], 1)
        if dsmall_ref.shape[2] == columns:
            dsmall_ref[n] = piece.reshape(wide, columns, TOKS)
        else:
            dsmall_ref[n] = jnp.zeros(dsmall_ref.shape[1:], F32)
            for w in range(wide):
                dsmall_ref[n, w, :columns] = piece[w * columns : (w + 1) * columns]

    def beside(tail):
        rows = tail.shape[0]
        tail = jnp.concatenate([tail, jnp.zeros((rows, 2 * TOKS - D), F32)], 1)
        lane = lax.broadcasted_iota(jnp.int32, (rows // 2, TOKS), 1)
        return jnp.where(
            lane < D - TOKS, tail[: rows // 2], pltpu.roll(tail[rows // 2 :], D - TOKS, 1)
        )

    for which in range(4):
        size = ROWS_OF[which] // narrow
        for l in range(L):
            for n in range(narrow):
                part = mats_acc[which][l, n * size : (n + 1) * size]
                at = offsets[which]
                dmats_ref[l, n, at : at + size] = part[:, :TOKS]
                dmats_ref[l, n, at + size : at + size + size // 2] = beside(part[:, TOKS:])

    terms = slots_acc[...]
    dslots_ref[:, :CAP] = terms[:, :TOKS].reshape(slots // CAP, CAP, TOKS).astype(BF16)
    tail = jnp.concatenate([terms[:, TOKS:], jnp.zeros((slots, 2 * TOKS - D), F32)], 1)
    tail = tail.reshape(slots // CAP, CAP, TOKS)
    low = tail[:, : CAP // 2].reshape(slots // 2, TOKS)
    high = pltpu.roll(tail[:, CAP // 2 :].reshape(slots // 2, TOKS), D - TOKS, 1)
    lane = lax.broadcasted_iota(jnp.int32, (slots // 2, TOKS), 1)
    dslots_ref[:, CAP:] = (
        jnp.where(lane < D - TOKS, low, high).reshape(slots // CAP, CAP // 2, TOKS).astype(BF16)
    )


def model_call(stats, labels, rows, slots, num, mask, mats, small, pair, wide, narrow):
    width = pair * TOKS
    used = rows.shape[0]
    _, total = packed_offsets(narrow)
    shape = jax.ShapeDtypeStruct
    outs = [
        shape((1, TOKS), F32),
        shape((L, narrow, total, TOKS), F32),
        shape((narrow, wide, small.shape[3], TOKS), F32),
        shape((used // CAP, PACK, TOKS), BF16),
    ]
    units = pair * HEADS
    vm = pltpu.VMEM
    scratch = [
        vm((D, used), BF16),
        vm((L, D, 3 * D), BF16), vm((L, D, D), BF16), vm((L, D, 2 * FF), BF16), vm((L, D, FF), BF16),
        vm((D, TOKS), F32), vm((D, TOKS), F32), vm((D, TOKS), F32), vm((16, D), BF16), vm((D, 48), BF16),
        vm((D, TOKS), F32), vm((D, TOKS), F32), vm((D, TOKS), F32), vm((D, 48), F32), vm((used, D), F32),
        vm((NVEC, D, TOKS), F32), vm((L, units, TOKS, TOKS), F32),
        vm((L, D, width), F32), vm((L, 1, width), F32), vm((L, D, width), BF16),
        vm((L, units, HD, TOKS), BF16), vm((L, units, HD, TOKS), BF16), vm((L, units, HD, TOKS), BF16),
        vm((L, D, width), BF16),
        vm((L, D, width), F32), vm((L, 1, width), F32), vm((L, D, width), BF16),
        vm((L, 2 * FF, width), F32), vm((L, FF, width), BF16),
        vm((NVEC, D, TOKS), F32), vm((slots.shape[0] // pair, D, -(-pair // ROOM) * TOKS), F32), vm((L, width, D), BF16), vm((pair, TOKS, HEADS * TOKS), F32), vm((L, pair, TOKS, HEADS * TOKS), BF16), vm((pair, TOKS, HEADS * TOKS), BF16), vm((L, width, D), BF16),
        *[vm((L, rows, D), F32) for rows in ROWS_OF],
        *[vm((slots.shape[0], TOKS), F32)] * 3,
    ]
    spec = pl.BlockSpec(memory_space=pltpu.VMEM)
    return pl.pallas_call(
        functools.partial(model_kernel, pair=pair, wide=wide, narrow=narrow),
        out_shape=outs,
        in_specs=[pl.BlockSpec(memory_space=pltpu.SMEM)] * 2 + [spec] * 9,
        out_specs=[spec] * len(outs),
        scratch_shapes=scratch,
        compiler_params=pltpu.CompilerParams(vmem_limit_bytes=62 << 20),
        name="model",
    )(stats, labels, rows, slots, num, mask, *mats, small)


def packed_rows(which, narrow):
    size = ROWS_OF[which] // narrow
    return size + size // 2


def packed_offsets(narrow):
    offsets, total = [], 0
    for which in range(4):
        offsets.append(total)
        total += packed_rows(which, narrow)
    return offsets, total


def worker_of(m, wide):
    layer, kind = m // 4, m % 4
    return (layer * 2 + kind % 2) * (wide // 8) * 2 + kind // 2


def adam_step(weight, gradient, first, second):
    first = BETA_ONE * first + (1.0 - BETA_ONE) * gradient
    second = BETA_TWO * second + (1.0 - BETA_TWO) * gradient * gradient
    ratio = first / (1.0 - BETA_ONE**STEP) / (jnp.sqrt(second / (1.0 - BETA_TWO**STEP)) + ADAM_EPS)
    return (weight - ADAM_RATE * (ratio + DECAY * weight), first, second)


def exact(left, right, left_dim=1, right_dim=0):
    return lax.dot_general(
        left, right, (((left_dim,), (right_dim,)), ((), ())), preferred_element_type=F32,
        precision=lax.Precision.HIGHEST,
    )


def finish_kernel(*refs, wide, narrow):
    refs = list(refs)

    def take(number):
        head = refs[:number]
        del refs[:number]
        return head

    levels = levels_of(narrow)
    count = wide * narrow
    columns = D // wide
    mats_any, dsmall_ref, dslots_ref, requests_ref, loss_ref, extra_any = take(6)
    moments = take(4)
    out_stats, table_any, out_small = take(3)
    x_came, out_moments = take(4), take(4)
    steps = levels + 1
    mats_held = [take(steps) for _ in range(L)]
    mats_came = [take(steps) for _ in range(L)]
    small_held, small_came = take(levels), take(levels)
    landed, hits, mats_landed, small_landed, grad_s = take(5)
    dmats_ref, out_table = take(2)
    norm_near, norm_all = take(2)
    mom_came, mom_sent, x_sent = take(4), take(4), take(4)
    x_start, x_end, gram_held, gram_came = take(4)
    (
        slot_send, slot_recv, mats_send, mats_recv, small_send, small_recv,
        block_send, block_recv, own_send, own_recv,
        near_send, near_recv, norm_send, norm_recv, get_send, get_recv, put_send, put_recv, new_send, new_recv,
        gram_send, gram_recv, mats_sem, extra_sem, table_sem,
    ) = refs
    mats_copy = pltpu.make_async_copy(mats_any, dmats_ref, mats_sem)
    extra_copy = pltpu.make_async_copy(extra_any, out_table, extra_sem)
    table_copy = pltpu.make_async_copy(out_table, table_any, table_sem)
    mats_copy.start()
    extra_copy.start()
    w, n, me = place(wide, narrow)
    barrier = greet_all(me, count, narrow)
    offsets, total = packed_offsets(narrow)
    half_rows = total // 2
    local = extra_any.shape[1]
    side = lax.rem(w, 2)

    def over_peers(origin, size, body):
        def run(k, carry):
            body(lax.rem(origin + k, size))
            return carry

        lax.fori_loop(1, size, run, 0)

    def coords(p):
        return (p // narrow, lax.rem(p, narrow))

    def narrow_partner(s):
        bit = lax.rem(n // (1 << s), 2)
        return bit, n + (1 - 2 * bit) * (1 << s)

    def plan(l):
        if l % 2:
            return list(range(levels)) + ["side"]
        return [0, "side"] + list(range(1, levels)) if levels else ["side"]

    def before(l, t):
        return dmats_ref.at[l] if t == 0 else mats_held[l][t - 1]

    def step_copies(l, t):
        move = plan(l)[t]
        source = before(l, t)
        copies = []
        if move == "side":
            for j in range(source.shape[0]):
                copies.append(
                    pltpu.make_async_remote_copy(
                        src_ref=source.at[j, pl.ds((1 - side) * half_rows, half_rows)],
                        dst_ref=mats_came[l][t].at[j],
                        send_sem=mats_send.at[l, t, j], recv_sem=mats_recv.at[l, t, j],
                        device_id=(w + 1 - 2 * side, n), device_id_type=MESH,
                    )
                )
        else:
            bit, partner = narrow_partner(move)
            for j in range(source.shape[0] // 2):
                copies.append(
                    pltpu.make_async_remote_copy(
                        src_ref=source.at[2 * j + 1 - bit], dst_ref=mats_came[l][t].at[j],
                        send_sem=mats_send.at[l, t, j], recv_sem=mats_recv.at[l, t, j],
                        device_id=(w, partner), device_id_type=MESH,
                    )
                )
        return copies

    def step_add(l, t):
        move = plan(l)[t]
        source = before(l, t)
        for j in range(mats_held[l][t].shape[0]):
            if move == "side":
                mine = source[j, pl.ds(side * half_rows, half_rows)]
            else:
                mine = source[2 * j + narrow_partner(move)[0]]
            mats_held[l][t][j] = mine + mats_came[l][t][j]

    def small_before(s):
        return dsmall_ref if s == 0 else small_held[s - 1]

    def small_copies(s):
        bit, partner = narrow_partner(s)
        return [
            pltpu.make_async_remote_copy(
                src_ref=small_before(s).at[2 * j + 1 - bit], dst_ref=small_came[s].at[j],
                send_sem=small_send.at[s, j], recv_sem=small_recv.at[s, j],
                device_id=(w, partner), device_id_type=MESH,
            )
            for j in range(narrow >> (s + 1))
        ]

    def small_add(s):
        bit, _ = narrow_partner(s)
        for j in range(narrow >> (s + 1)):
            small_held[s][j] = small_before(s)[2 * j + bit] + small_came[s][j]

    def slot_copy(p, slot):
        return pltpu.make_async_remote_copy(
            src_ref=dslots_ref.at[p], dst_ref=landed.at[slot], send_sem=slot_send.at[p],
            recv_sem=slot_recv.at[slot], device_id=coords(p), device_id_type=MESH,
        )

    def block_copy(m, slot):
        layer, kind = m // 4, m % 4
        start = offsets[kind] - half_rows * (kind // 2)
        size = packed_rows(kind, narrow)
        return pltpu.make_async_remote_copy(
            src_ref=mats_held[layer][steps - 1].at[0, pl.ds(start, size)],
            dst_ref=mats_landed.at[slot, pl.ds(0, size)],
            send_sem=block_send.at[m], recv_sem=block_recv.at[slot],
            device_id=(worker_of(m, wide), n), device_id_type=MESH,
        )

    def own_copy(p, slot):
        return pltpu.make_async_remote_copy(
            src_ref=small_held[levels - 1].at[0, p], dst_ref=small_landed.at[slot],
            send_sem=own_send.at[p], recv_sem=own_recv.at[slot], device_id=(p, n),
            device_id_type=MESH,
        )

    def near_copy(p, slot):
        return pltpu.make_async_remote_copy(
            src_ref=norm_near.at[n], dst_ref=norm_near.at[slot], send_sem=near_send.at[p],
            recv_sem=near_recv.at[slot], device_id=(w, p), device_id_type=MESH,
        )

    def norm_copy(p, slot):
        return pltpu.make_async_remote_copy(
            src_ref=norm_all.at[w], dst_ref=norm_all.at[slot], send_sem=norm_send.at[p],
            recv_sem=norm_recv.at[slot], device_id=(p, n), device_id_type=MESH,
        )

    def get_copy(m, slot):
        return pltpu.make_async_remote_copy(
            src_ref=moments[m % 4].at[m // 4], dst_ref=mom_came[m % 4].at[slot],
            send_sem=get_send.at[m], recv_sem=get_recv.at[slot],
            device_id=(worker_of(m, wide), n), device_id_type=MESH,
        )

    def put_copy(m, p):
        return pltpu.make_async_remote_copy(
            src_ref=mom_sent[m % 4].at[p], dst_ref=out_moments[m % 4].at[m // 4],
            send_sem=put_send.at[p], recv_sem=put_recv.at[m], device_id=(p, n),
            device_id_type=MESH,
        )

    def new_copy(m, p):
        return pltpu.make_async_remote_copy(
            src_ref=x_sent[m % 4].at[p], dst_ref=x_came[m % 4].at[m // 4],
            send_sem=new_send.at[p], recv_sem=new_recv.at[m], device_id=(p, n),
            device_id_type=MESH,
        )

    def gram_copy(s):
        _, partner = narrow_partner(s)
        return pltpu.make_async_remote_copy(
            src_ref=gram_held.at[s], dst_ref=gram_came.at[s], send_sem=gram_send.at[s],
            recv_sem=gram_recv.at[s], device_id=(w, partner), device_id_type=MESH,
        )

    pl.semaphore_wait(barrier, count - 1)
    mats_copy.wait()
    for l in range(L):
        for copy in step_copies(l, 0):
            copy.start()
    for copy in small_copies(0):
        copy.start()
    over_peers(me, count, lambda p: slot_copy(p, me).start())
    landed[me] = dslots_ref[me]
    for m in range(4 * L):
        @pl.when(w != worker_of(m, wide))
        def _():
            get_copy(m, w).start()

        @pl.when(w == worker_of(m, wide))
        def _():
            mom_came[m % 4][w] = moments[m % 4][m // 4]

    eye = lax.broadcasted_iota(jnp.int32, (CAP, TOKS), 0) == lax.broadcasted_iota(
        jnp.int32, (CAP, TOKS), 1
    )
    spots = lax.broadcasted_iota(jnp.int32, (CAP, local), 1)

    def find(c, carry):
        for j in range(8):
            q = c * 8 + j
            row = jnp.broadcast_to(requests_ref[q], (CAP, TOKS))
            column = jnp.sum(jnp.where(eye, row, 0.0), 1, keepdims=True).astype(jnp.int32)
            at = pl.multiple_of(q * CAP, CAP)
            hits[pl.ds(at, CAP), :] = jnp.where(spots == column, 1.0, 0.0).astype(BF16)
        return carry

    lax.fori_loop(0, count // 8, find, 0)

    def finish_step(t):
        for l in range(L):
            for copy in step_copies(l, t):
                copy.wait_recv()
            step_add(l, t)
        if t < levels:
            for copy in small_copies(t):
                copy.wait_recv()
            small_add(t)
        if t + 1 < steps:
            for l in range(L):
                for copy in step_copies(l, t + 1):
                    copy.start()
        if t + 1 < levels:
            for copy in small_copies(t + 1):
                copy.start()

    finish_step(0)

    over_peers(me, count, lambda p: slot_copy(p, p).wait_recv())
    terms_t = jnp.transpose(spread_slots(landed[...].astype(F32)))
    if steps > 2:
        finish_step(1)
    extra_copy.wait()
    out_table[...] += mm(terms_t.astype(BF16), hits[...])
    table_copy.start()
    for t in range(2 if steps > 2 else 1, steps):
        finish_step(t)

    over_peers(w, wide, lambda p: own_copy(p, w).start())
    for m in range(4 * L):
        kind = m % 4

        @pl.when((side == kind // 2) & (w != worker_of(m, wide)))
        def _():
            block_copy(m, w).start()

    table_grad = out_table[...]

    def total_of(value):
        return jnp.sum(jnp.sum(value, 0, keepdims=True), 1, keepdims=True)

    squares = total_of(table_grad * table_grad)
    loss_here = jnp.sum(loss_ref[...], 1, keepdims=True)
    x_start[...] = jnp.zeros_like(x_start)
    grad_s[...] = jnp.zeros_like(grad_s)

    over_peers(w, wide, lambda p: own_copy(p, p).wait_recv())

    def add_small(k, value):
        return value + small_landed[lax.rem(w + k, wide)]

    own_small = lax.fori_loop(1, wide, add_small, small_held[levels - 1][0, w])
    squares = squares + total_of(own_small * own_small)
    out_small[...] = own_small
    for m in range(4 * L):
        layer, kind = m // 4, m % 4

        @pl.when(w == worker_of(m, wide))
        def _():
            start = offsets[kind] - half_rows * (kind // 2)
            size = packed_rows(kind, narrow)
            whole = ROWS_OF[kind] // narrow

            def add_block(k, value):
                p = lax.rem(w // 2 + k, wide // 2) * 2 + side
                block_copy(m, p).wait_recv()
                return value + mats_landed[p, :size]

            packed = lax.fori_loop(
                1, wide // 2, add_block,
                mats_held[layer][steps - 1][0, start : start + size],
            )
            tail = packed[whole:]
            grad_s[:whole, :TOKS] = packed[:whole]
            grad_s[: whole // 2, TOKS : D] = tail[:, : D - TOKS]
            grad_s[whole // 2 : whole, TOKS : D] = tail[:, D - TOKS :]

    grad = grad_s[...]
    squares = squares + total_of(grad * grad)
    lane = lax.broadcasted_iota(jnp.int32, (1, TOKS), 1)
    norm_near[n] = jnp.where(lane == 0, squares, jnp.where(lane == 1, loss_here, 0.0))
    over_peers(n, narrow, lambda p: near_copy(p, n).start())
    grad_t = jnp.transpose(grad)[:D]
    over_peers(n, narrow, lambda p: near_copy(p, p).wait_recv())
    norm_all[w] = jnp.sum(norm_near[...], 0)
    over_peers(w, wide, lambda p: norm_copy(p, w).start())
    over_peers(w, wide, lambda p: norm_copy(p, p).wait_recv())
    sums = jnp.sum(norm_all[...], 0)
    norm = jnp.sqrt(sums)
    factor = CLIP / jnp.maximum(norm[:, :1], CLIP)
    out_stats[...] = jnp.where(lane == 0, norm, jnp.where(lane == 2, factor, sums))

    def gather_rows(ref):
        if columns % 8 == 0:
            return ref[...].reshape(D, ref.shape[2])
        return jnp.concatenate([ref[p] for p in range(wide)], 0)

    def spread_rows(ref, value):
        if columns % 8 == 0:
            ref[...] = value.reshape(ref.shape)
        else:
            for p in range(wide):
                ref[p] = value[p * columns : (p + 1) * columns]

    for m in range(4 * L):
        @pl.when(w == worker_of(m, wide))
        def _():
            over_peers(w, wide, lambda p: get_copy(m, p).wait_recv())
            size = ROWS_OF[m % 4] // narrow
            moment = MOMENTUM * gather_rows(mom_came[m % 4]) + factor * grad_t[:, :size]
            x_start[:, :size] = moment
            spread_rows(mom_sent[m % 4], moment)
            over_peers(w, wide, lambda p: put_copy(m, p).start())
            out_moments[m % 4][m // 4] = mom_sent[m % 4][w]

    x = x_start[...]
    gram = exact(x, x, 1, 1)
    rest = D - TOKS
    gram_held[0, :D] = gram[:, :TOKS]
    gram_held[0, D : D + rest] = jnp.concatenate(
        [gram[TOKS:, TOKS:], jnp.zeros((rest, TOKS - rest), F32)], 1
    )
    for s in range(levels):
        gram_copy(s).start()
        gram_copy(s).wait_recv()
        gram_held[s + 1] = gram_held[s] + gram_came[s]
    left = gram_held[levels, :D]
    corner = gram_held[levels, D : D + rest][:, :rest]
    above = jnp.transpose(
        jnp.concatenate([left[TOKS:], jnp.zeros((TOKS - rest, TOKS), F32)], 0)
    )[:, :rest]
    gram = jnp.concatenate([left, jnp.concatenate([above, corner], 0)], 1)
    eye = jnp.where(
        lax.broadcasted_iota(jnp.int32, (D, D), 0) == lax.broadcasted_iota(jnp.int32, (D, D), 1),
        1.0, 0.0,
    )
    inverse = lax.rsqrt(total_of(eye * gram) + ORTHO_EPS)
    square = gram * (inverse * inverse)
    product = None
    for step in range(5):
        polynomial = NS_ONE * eye + NS_TWO * square + NS_THREE * exact(square, square)
        product = polynomial if product is None else exact(product, polynomial)
        if step < 4:
            square = exact(polynomial, exact(square, polynomial))
    x_end[...] = exact(product, x * inverse)
    for m in range(4 * L):
        @pl.when(w == worker_of(m, wide))
        def _():
            size = ROWS_OF[m % 4] // narrow
            spread_rows(x_sent[m % 4], x_end[:, :size])
            over_peers(w, wide, lambda p: new_copy(m, p).start())
            x_came[m % 4][m // 4] = x_sent[m % 4][w]

    for m in range(4 * L):
        @pl.when(w != worker_of(m, wide))
        def _():
            new_copy(m, w).wait_recv()

    for m in range(4 * L):
        @pl.when(w != worker_of(m, wide))
        def _():
            put_copy(m, w).wait_recv()
            get_copy(m, w).wait_send()

        @pl.when((side == (m % 4) // 2) & (w != worker_of(m, wide)))
        def _():
            block_copy(m, w).wait_send()

        @pl.when(w == worker_of(m, wide))
        def _():
            over_peers(w, wide, lambda p: put_copy(m, p).wait_send())
            over_peers(w, wide, lambda p: new_copy(m, p).wait_send())

    table_copy.wait()
    for s in range(levels):
        gram_copy(s).wait_send()
        for copy in small_copies(s):
            copy.wait_send()
    for l in range(L):
        for t in range(steps):
            for copy in step_copies(l, t):
                copy.wait_send()
    over_peers(n, narrow, lambda p: near_copy(p, n).wait_send())
    over_peers(w, wide, lambda p: norm_copy(p, w).wait_send())
    over_peers(me, count, lambda p: slot_copy(p, me).wait_send())
    over_peers(w, wide, lambda p: own_copy(p, w).wait_send())


def finish_call(dmats, dsmall, dslots, requests, loss, extra, moments, wide, narrow):
    count = wide * narrow
    levels = levels_of(narrow)
    columns = D // wide
    _, total = packed_offsets(narrow)
    shape = jax.ShapeDtypeStruct
    local = extra.shape[1]
    outs = [shape((1, TOKS), F32), shape(extra.shape, F32), shape(dsmall.shape[2:], F32)]
    outs += [shape(a.shape, F32) for a in moments + moments]
    vm = pltpu.VMEM
    dma = pltpu.SemaphoreType.DMA
    steps = levels + 1

    def mats_shapes(l):
        sizes, quarters, rows = [], narrow, total
        plan = list(range(levels)) + ["side"] if l % 2 else [0, "side"] + list(range(1, levels))
        for move in plan:
            if move == "side":
                rows //= 2
            else:
                quarters //= 2
            sizes.append(vm((quarters, rows, TOKS), F32))
        return sizes

    mats = [v for l in range(L) for v in mats_shapes(l)]
    small_shapes = [vm((narrow >> (s + 1),) + dsmall.shape[1:], F32) for s in range(levels)]
    largest = max(packed_rows(which, narrow) for which in range(4))
    blocks = [vm((wide, columns, rows // narrow), F32) for rows in ROWS_OF]
    spec = pl.BlockSpec(memory_space=pltpu.VMEM)
    anywhere = pl.BlockSpec(memory_space=pl.ANY)
    return pl.pallas_call(
        functools.partial(finish_kernel, wide=wide, narrow=narrow),
        out_shape=outs,
        in_specs=[anywhere] + [spec] * 4 + [anywhere] + [spec] * 4,
        out_specs=[spec, anywhere] + [spec] * (len(outs) - 2),
        scratch_shapes=mats * 2 + small_shapes * 2
        + [
            vm(dslots.shape, BF16),
            vm((count * CAP, local), BF16),
            vm((wide, largest, TOKS), F32),
            vm((wide,) + dsmall.shape[2:], F32),
            vm((2 * TOKS, 2 * TOKS), F32),
            vm(dmats.shape, F32),
            vm(extra.shape, F32),
            vm((narrow, 1, TOKS), F32),
            vm((wide, 1, TOKS), F32),
        ]
        + blocks * 3
        + [
            vm((D, 2 * TOKS), F32), vm((D, 2 * TOKS), F32),
            vm((levels + 1, 2 * TOKS, TOKS), F32), vm((levels, 2 * TOKS, TOKS), F32),
            dma((count,)), dma((count,)),
            dma((L, steps, narrow)), dma((L, steps, narrow)),
            dma((levels, narrow // 2)), dma((levels, narrow // 2)),
            dma((4 * L,)), dma((wide,)), dma((wide,)), dma((wide,)),
            dma((narrow,)), dma((narrow,)), dma((wide,)), dma((wide,)),
            dma((4 * L,)), dma((wide,)), dma((wide,)), dma((4 * L,)),
            dma((wide,)), dma((4 * L,)), dma((levels,)), dma((levels,)),
            dma(()), dma(()), dma(()),
        ],
        compiler_params=pltpu.CompilerParams(
            collective_id=1, has_side_effects=True, vmem_limit_bytes=62 << 20
        ),
        name="finish",
    )(dmats, dsmall, dslots, requests, loss, extra, *moments)


def apply_kernel(*refs):
    refs = list(refs)

    def take(number):
        head = refs[:number]
        del refs[:number]
        return head

    stats_ref, start_ref = take(2)
    tables, (gsmall_ref,), smalls = take(4), take(1), take(3)
    weights, ortho, moments = take(4), take(4), take(4)
    out_scalars, out_tables, out_smalls = take(3), take(3), take(3)
    out_weights, out_moments = take(4), take(4)
    factor = jnp.full((1, 1), stats_ref[0, 2], F32)
    table, grad, first, second = (ref[...] for ref in tables)
    for ref, value in zip(out_tables, adam_step(table, factor * grad, first, second)):
        ref[...] = value

    @pl.when(pl.program_id(0) == 0)
    def _():
        out_scalars[0][0, 0] = stats_ref[0, 1]
        out_scalars[1][0, 0] = start_ref[0, CAP + 1]
        out_scalars[2][0, 0] = stats_ref[0, 0]
        small, first, second = (ref[...] for ref in smalls)
        grad = gsmall_ref[: small.shape[0], : small.shape[1]]
        for ref, value in zip(out_smalls, adam_step(small, factor * grad, first, second)):
            ref[...] = value
        for which in range(4):
            scale = math.sqrt(max(1.0, ROWS_OF[which] / D))
            out_weights[which][...] = (
                weights[which][...] * (1.0 - MUON_RATE * DECAY)
                - MUON_RATE * scale * ortho[which][...]
            )
            out_moments[which][...] = moments[which][...]


def apply_call(stats, start_stats, tables, gsmall, smalls, weights, ortho, moments):
    shape = jax.ShapeDtypeStruct
    smem = pl.BlockSpec(memory_space=pltpu.SMEM)
    local = tables[0].shape[1]
    rows = D // 2
    block = pl.BlockSpec((rows, local), lambda i: (i, 0))

    def whole(array):
        return pl.BlockSpec(array.shape, lambda i, nd=array.ndim: (0,) * nd)

    beside = smalls + weights + ortho + moments
    outs = smalls + weights + moments
    return pl.pallas_call(
        apply_kernel,
        grid=(D // rows,),
        out_shape=[shape((1, 1), F32)] * 3
        + [shape(tables[0].shape, F32)] * 3
        + [shape(a.shape, F32) for a in outs],
        in_specs=[smem, smem] + [block] * 4 + [whole(gsmall)] + [whole(a) for a in beside],
        out_specs=[smem] * 3 + [block] * 3 + [whole(a) for a in outs],
        compiler_params=pltpu.CompilerParams(vmem_limit_bytes=62 << 20),
        name="apply",
    )(stats, start_stats, *tables, gsmall, *beside)


def per_device(
    cat_index, num_values, cell_mask, labels, table, table_first, table_second,
    small, small_first, small_second, w_qkv, w_proj, w_in, w_down,
    mom_qkv, mom_proj, mom_in, mom_down,
):
    wide = lax.axis_size("wide")
    narrow = lax.axis_size("narrow")
    count = wide * narrow
    data_rows = num_values.shape[0]
    pair = 4 if count * CAP <= 2048 else 4
    while data_rows % pair:
        pair //= 2
    flip = lambda v: jnp.swapaxes(v, -1, -2)
    weights = [flip(v) for v in (w_qkv, w_proj, w_in, w_down)]
    moments = [flip(v) for v in (mom_qkv, mom_proj, mom_in, mom_down)]
    smalls = [flip(v) for v in (small, small_first, small_second)]
    tables = [flip(v) for v in (table, table_first, table_second)]
    qkv, proj, w_in_all, down, small_all, rows, slots, requests, stats = gather_call(
        cat_index, cell_mask, weights, smalls[0], tables[0], wide, narrow
    )
    over = stats[0, CAP] > 0.5
    flat_index = cat_index.reshape(-1)
    entries = flat_index.shape[0]

    axes = ("wide", "narrow")
    local = table.shape[0]
    me = lax.axis_index("wide") * narrow + lax.axis_index("narrow")
    ring = [(i, (i + 1) % count) for i in range(count)]

    def hits_at(owner):
        spot = flat_index - owner * local
        return (spot[:, None] == lax.iota(jnp.int32, local)[None, :]).astype(BF16)

    def general_rows(rows, slots):
        def turn(s, carry):
            block, looked = carry
            looked = looked + mm(hits_at(lax.rem(me - s + count, count)), block)
            return lax.ppermute(block, axes, ring), looked

        first = (table.astype(BF16), jnp.zeros((entries, D), F32))
        looked = lax.fori_loop(0, count, turn, first)[1].astype(BF16)
        spare = jnp.zeros((rows.shape[0] - entries, D), BF16)
        own = lax.iota(jnp.int32, entries).reshape(cat_index.shape)
        none = jnp.full((data_rows, TOKS - CATF), -1, jnp.int32)
        return jnp.concatenate([looked, spare], 0), jnp.concatenate([none, own], 1)

    def general_terms(dslots):
        tail = dslots[:, CAP:]
        tail = jnp.concatenate([tail[:, :, : D - TOKS], tail[:, :, D - TOKS :]], 1)
        terms = jnp.concatenate([dslots[:, :CAP], tail], 2).reshape(count * CAP, D)[:entries]

        def turn(s, sums):
            owner = lax.rem(me - 1 - s + 2 * count, count)
            return lax.ppermute(sums, axes, ring) + mm(terms, hits_at(owner), 0, 0)

        sums = lax.fori_loop(0, count, turn, jnp.zeros(tables[0].shape, F32))
        return sums, jnp.zeros_like(dslots)

    rows, slots = lax.cond(over, general_rows, lambda r, s: (r, s), rows, slots)
    loss, dmats, dsmall, dslots = model_call(
        stats, labels, rows, slots, num_values, cell_mask,
        (qkv, proj, w_in_all, down), small_all, pair, wide, narrow,
    )
    extra, dslots = lax.cond(
        over, general_terms, lambda d: (jnp.zeros(tables[0].shape, F32), d), dslots
    )
    outs = finish_call(dmats, dsmall, dslots, requests, loss, extra, moments, wide, narrow)
    done = apply_call(
        outs[0], stats, [tables[0], outs[1], *tables[1:]], outs[2], smalls, weights,
        list(outs[3:7]), list(outs[7:11]),
    )
    return tuple(v.reshape(()) for v in done[:3]) + tuple(flip(v) for v in done[3:])


def solution(mesh):
    rows = P(("wide", "narrow"), None)
    square = P("narrow", "wide")
    cube = P(None, "narrow", "wide")
    return jax.shard_map(
        per_device,
        mesh=mesh,
        in_specs=(rows, rows, rows, P(("wide", "narrow")), rows, rows, rows)
        + (square,) * 3 + (cube,) * 8,
        out_specs=(P(), P(), P(), rows, rows, rows) + (square,) * 3 + (cube,) * 8,
        check_vma=False,
    )
```

```python
import functools
import math

import jax
import jax.numpy as jnp
import numpy as np
from jax import lax
from jax.experimental import pallas as pl
from jax.experimental.pallas import tpu as pltpu
from jax.sharding import PartitionSpec as P

D = 192
HEADS = 8
HD = 24
FF = 256
L = 2
NUMF = 95
CATF = 32
NCLASS = 7
STEP = 10
TOKS = 128

NORM_EPS = 1e-05
CLIP = 0.002
BETA_ONE = 0.9
BETA_TWO = 0.95
ADAM_EPS = 1e-08
ADAM_RATE = 0.2
MUON_RATE = 1.0
MOMENTUM = 0.95
DECAY = 0.01
ORTHO_EPS = 1e-20
NS_ONE = 3.4445
NS_TWO = -4.775
NS_THREE = 2.0315
GELU_A = math.sqrt(2.0 / math.pi)
GELU_B = 0.044715
SCALE = HD ** (-0.5)

F32 = jnp.float32
BF16 = jnp.bfloat16
MESH = pl.DeviceIdType.MESH

ROWS_OF = (3 * D, D, 2 * FF, FF)
ORDER = (2, 0, 1, 3)
NSR = 8 * L + TOKS + NUMF + 1 + 2 + NCLASS + NUMF
OFF_SCALE = 8 * L + TOKS
OFF_FIN = OFF_SCALE + NUMF + 1
CAP = 32
PACK = CAP + CAP // 2


def mm(left, right, left_dim=1, right_dim=0):
    return lax.dot_general(
        left, right, (((left_dim,), (right_dim,)), ((), ())), preferred_element_type=F32
    )


def up_to(value, unit):
    return -(-value // unit) * unit


def split_two(value):
    high = value.astype(BF16)
    return high, (value - high.astype(F32)).astype(BF16)


def split_three(value):
    high = value.astype(BF16)
    rest = value - high.astype(F32)
    middle = rest.astype(BF16)
    return high, middle, (rest - middle.astype(F32)).astype(BF16)


def place(wide, narrow):
    w = lax.axis_index("wide")
    n = lax.axis_index("narrow")
    return w, n, w * narrow + n


def greet_all(me, count, narrow):
    barrier = pltpu.get_barrier_semaphore()

    def signal(k, carry):
        p = lax.rem(me + k, count)
        pl.semaphore_signal(
            barrier, inc=1, device_id=(p // narrow, lax.rem(p, narrow)), device_id_type=MESH
        )
        return carry

    lax.fori_loop(1, count, signal, 0)
    return barrier


def quarter_offsets(narrow):
    offsets, total = {}, 0
    for which in ORDER:
        offsets[which] = total
        total += ROWS_OF[which] // narrow
    return offsets, total


def gather_kernel(
    cat_ref, mask_ref, qkv_ref, proj_ref, in_ref, down_ref, small_ref, table_ref, pick_ref,
    out_qkv, out_proj, out_in, out_down, out_small, out_rows, out_slots, out_requests, out_stats,
    gat_one, gat_two, ask, table_s, table_low, answers, landed,
    far_send, far_recv, step_send, step_recv, ask_send, ask_recv, row_send, row_recv, table_sem,
    *, wide, narrow, chunk,
):
    count = wide * narrow
    levels = levels_of(narrow)
    w, n, me = place(wide, narrow)
    side, far = lax.rem(w, 2), w // 2
    fars = wide // 2
    table_copy = pltpu.make_async_copy(table_ref, table_s, table_sem)
    table_copy.start()
    barrier = greet_all(me, count, narrow)

    def coords(p):
        return (p // narrow, lax.rem(p, narrow))

    offsets, total = quarter_offsets(narrow)
    width = qkv_ref.shape[1]
    rows_pad = gat_one.shape[3]
    cut = gat_one.shape[4]
    shards = (qkv_ref, proj_ref, in_ref, down_ref)
    pieces = [
        jnp.concatenate([shards[which][l] for which in ORDER], 1) for l in range(L)
    ]
    if rows_pad > L * width:
        pieces.append(jnp.zeros((rows_pad - L * width, total), F32))
    packed = jnp.concatenate(pieces, 0).astype(BF16)
    gat_one[n, side, far] = packed[:, :cut]
    gat_two[n, side, far] = packed[:, cut:]
    small = small_ref[...]
    own_rows = small.shape[1]
    small_pad = out_small.shape[3]
    if small_pad > width:
        small = jnp.concatenate([small, jnp.zeros((small_pad - width, own_rows), F32)], 0)
    out_small[n, side, far] = jnp.concatenate(
        [small, jnp.zeros((small_pad, TOKS - own_rows), F32)], 1
    )

    data_rows, per_row = cat_ref.shape
    entries = data_rows * per_row
    local = table_s.shape[1]
    index_row = jnp.concatenate([cat_ref[r : r + 1, :] for r in range(data_rows)], 1)
    owner_row = jnp.zeros_like(index_row)
    for k in range(1, count):
        owner_row = owner_row + (index_row >= k * local).astype(jnp.int32)
    base_row = owner_row * local
    index_col = jnp.transpose(jnp.broadcast_to(index_row, (8, entries)))[:, :1]
    before = lax.broadcasted_iota(jnp.int32, (entries, entries), 0)
    after = lax.broadcasted_iota(jnp.int32, (entries, entries), 1)
    same = index_col == index_row
    first_col = 1.0 - jnp.max(jnp.where(same & (after < before), 1.0, 0.0), 1, keepdims=True)
    first_row = 1.0 - jnp.max(jnp.where(same & (before < after), 1.0, 0.0), 0, keepdims=True)
    lower = (index_col >= base_row) & (index_col < index_row)
    rank_row = jnp.sum(jnp.where(lower, first_col, 0.0), 0, keepdims=True).astype(jnp.int32)
    slot_row = owner_row * CAP + rank_row
    none = jnp.full((1, TOKS - per_row), -1, jnp.int32)
    for r in range(data_rows):
        out_slots[r : r + 1, :] = jnp.concatenate(
            [none, slot_row[:, r * per_row : (r + 1) * per_row]], 1
        )
    over = jnp.max(jnp.where(rank_row >= CAP, 1.0, 0.0), 1, keepdims=True)
    hidden_cells = jnp.sum(jnp.sum(mask_ref[...].astype(F32), 0, keepdims=True), 1, keepdims=True)
    place_row = index_row - base_row
    owners = lax.broadcasted_iota(jnp.int32, (count, entries), 0)
    mine = jnp.where(owners == owner_row, first_row, 0.0)
    high = lax.shift_right_logical(place_row, 6)
    low = place_row - high * 64
    at_rank = jnp.where(
        lax.broadcasted_iota(jnp.int32, (TOKS, entries), 0) == rank_row, 1.0, 0.0
    ).astype(BF16)
    wanted = 64.0 * mm((mine * high.astype(F32)).astype(BF16), at_rank, 1, 1) + mm(
        (mine * low.astype(F32)).astype(BF16), at_rank, 1, 1
    )
    lane = lax.broadcasted_iota(jnp.int32, (count, TOKS), 1)
    wanted = jnp.where(lane < CAP, wanted, 0.0)
    wanted = jnp.where(lane == CAP, over, wanted)
    wanted = jnp.where(lane == CAP + 1, hidden_cells, wanted)
    for k in range(count):
        ask[k] = wanted[k : k + 1]

    pl.semaphore_wait(barrier, count - 1)

    def over_peers(origin, size, body):
        def run(k, carry):
            body(lax.rem(origin + k, size))
            return carry

        lax.fori_loop(1, size, run, 0)

    def ask_copy(p, slot):
        return pltpu.make_async_remote_copy(
            src_ref=ask.at[p], dst_ref=out_requests.at[slot], send_sem=ask_send.at[p],
            recv_sem=ask_recv.at[slot], device_id=coords(p), device_id_type=MESH,
        )

    def row_copy(p, slot):
        return pltpu.make_async_remote_copy(
            src_ref=answers.at[p], dst_ref=landed.at[slot], send_sem=row_send.at[p],
            recv_sem=row_recv.at[slot], device_id=coords(p), device_id_type=MESH,
        )

    arrays = (gat_one, gat_two, out_small)

    def far_copies(p, slot):
        return [
            pltpu.make_async_remote_copy(
                src_ref=array.at[n, side, far], dst_ref=array.at[n, side, slot],
                send_sem=far_send.at[a, p], recv_sem=far_recv.at[a, slot],
                device_id=(p * 2 + side, n), device_id_type=MESH,
            )
            for a, array in enumerate(arrays)
        ]

    high_levels = list(range(levels - 1, 0, -1))
    plans = (
        high_levels + ["side"] + [0] * (levels > 0),
        ["side"] + high_levels + [0] * (levels > 0),
    )
    steps = len(plans[0])

    def step_copies(t):
        copies = []
        for a, array in enumerate(arrays):
            plan = plans[min(a, 1)]
            move = plan[t]
            done = plan[:t]
            lowest = min([v for v in done if v != "side"], default=levels)
            for j in range(1 << (levels - lowest)):
                block = lax.rem(n, 1 << lowest) + (j << lowest)
                if move == "side":
                    target = (w + 1 - 2 * side, n)
                else:
                    bit = lax.rem(n // (1 << move), 2)
                    target = (w, n + (1 - 2 * bit) * (1 << move))
                ref = array.at[block] if "side" in done else array.at[block, side]
                copies.append(
                    pltpu.make_async_remote_copy(
                        src_ref=ref, dst_ref=ref, send_sem=step_send.at[t, a, j],
                        recv_sem=step_recv.at[t, a, j], device_id=target, device_id_type=MESH,
                    )
                )
        return copies

    def step_arrivals(t):
        copies = []
        for a, array in enumerate(arrays):
            plan = plans[min(a, 1)]
            move = plan[t]
            done = plan[:t]
            lowest = min([v for v in done if v != "side"], default=levels)
            for j in range(1 << (levels - lowest)):
                if move == "side":
                    there, whose, target = n, 1 - side, (w + 1 - 2 * side, n)
                else:
                    bit = lax.rem(n // (1 << move), 2)
                    there, whose = n + (1 - 2 * bit) * (1 << move), side
                    target = (w, there)
                block = lax.rem(there, 1 << lowest) + (j << lowest)
                ref = array.at[block] if "side" in done else array.at[block, whose]
                copies.append(
                    pltpu.make_async_remote_copy(
                        src_ref=ref, dst_ref=ref, send_sem=step_send.at[t, a, j],
                        recv_sem=step_recv.at[t, a, j], device_id=target, device_id_type=MESH,
                    )
                )
        return copies

    def start_far(p):
        for copy in far_copies(p, far):
            copy.start()

    def end_far(p):
        for copy in far_copies(p, p):
            copy.wait_recv()

    over_peers(me, count, lambda p: ask_copy(p, me).start())
    over_peers(far, fars, start_far)
    out_requests[me] = ask[me]
    table_copy.wait()
    table_low[...] = table_s[...].astype(BF16)
    over_peers(far, fars, end_far)
    for copy in step_copies(0):
        copy.start()
    over_peers(me, count, lambda p: ask_copy(p, p).wait_recv())

    eye = lax.broadcasted_iota(jnp.int32, (CAP, TOKS), 0) == lax.broadcasted_iota(
        jnp.int32, (CAP, TOKS), 1
    )
    spots = lax.broadcasted_iota(jnp.int32, (CAP, local), 1)

    def wanted_hits(q):
        row = jnp.broadcast_to(out_requests[q], (CAP, TOKS))
        column = jnp.sum(jnp.where(eye, row, 0.0), 1, keepdims=True).astype(jnp.int32)
        return jnp.where(spots == column, 1.0, 0.0).astype(BF16)

    half_lane = lax.broadcasted_iota(jnp.int32, (CAP // 2, TOKS), 1) < D - TOKS

    def answer(c, carry):
        found = [wanted_hits(c * chunk + j) for j in range(chunk)]
        got = mm(jnp.concatenate(found, 0), table_low[...], 1, 1)
        got = jnp.concatenate([got, jnp.zeros((got.shape[0], 2 * TOKS - D), F32)], 1)
        for j in range(chunk):
            q = c * chunk + j
            part = got[j * CAP : (j + 1) * CAP]
            tail = part[:, TOKS:]
            rolled = pltpu.roll(tail[CAP // 2 :], D - TOKS, 1)
            packed = jnp.where(half_lane, tail[: CAP // 2], rolled)
            answers[q] = jnp.concatenate([part[:, :TOKS], packed], 0).astype(BF16)

            @pl.when(q != me)
            def _():
                row_copy(q, me).start()

        return carry

    def next_step(t):
        for copy in step_arrivals(t):
            copy.wait_recv()
        if t + 1 < steps:
            for copy in step_copies(t + 1):
                copy.start()

    lax.fori_loop(0, count // chunk // 2, answer, 0)
    next_step(0)
    lax.fori_loop(count // chunk // 2, count // chunk, answer, 0)
    landed[me] = answers[me]
    for t in range(1, steps):
        next_step(t)

    outs = (out_qkv, out_proj, out_in, out_down)
    for q in range(narrow):
        held = jnp.concatenate(
            [
                gat_one[q].reshape(wide * rows_pad, cut),
                gat_two[q].reshape(wide * rows_pad, total - cut),
            ],
            1,
        )
        for l in range(L):
            matrix = mm(held, pick_ref[l], 0, 0).astype(BF16)
            for which in ORDER:
                size = ROWS_OF[which] // narrow
                outs[which][l, q * size : (q + 1) * size] = matrix[
                    offsets[which] : offsets[which] + size
                ]

    requests = out_requests[...]
    reached = jnp.max(requests, 0)
    summed = jnp.sum(requests, 0)
    lane = lax.broadcasted_iota(jnp.int32, (1, TOKS), 1)
    out_stats[...] = jnp.where(lane == CAP, reached, summed)

    over_peers(me, count, lambda p: row_copy(p, p).wait_recv())
    out_rows[...] = spread_slots(landed[...].astype(F32)).astype(BF16)

    def drain_far(p):
        for copy in far_copies(p, far):
            copy.wait_send()

    over_peers(far, fars, drain_far)
    for t in range(steps):
        for copy in step_copies(t):
            copy.wait_send()
    over_peers(me, count, lambda p: ask_copy(p, me).wait_send())
    over_peers(me, count, lambda p: row_copy(p, me).wait_send())


def levels_of(size):
    return size.bit_length() - 1


def spread_slots(packed):
    owners = packed.shape[0]
    head = packed[:, :CAP].reshape(owners * CAP, TOKS)
    tail = packed[:, CAP:].reshape(owners * (CAP // 2), TOKS)
    moved = pltpu.roll(tail, D - TOKS, 1).reshape(owners, CAP // 2, TOKS)
    tail = jnp.concatenate([tail.reshape(owners, CAP // 2, TOKS), moved], 1)
    return jnp.concatenate([head, tail.reshape(owners * CAP, TOKS)[:, : D - TOKS]], 1)


def gather_call(cat_index, cell_mask, shards_t, small_t, table_t, wide, narrow):
    count = wide * narrow
    levels = levels_of(narrow)
    width = small_t.shape[0]
    rows_pad = up_to(L * width, 16)
    small_pad = up_to(width, 8)
    _, total = quarter_offsets(narrow)
    cut = up_to(total // 2, TOKS)
    pick = np.zeros((L, wide * rows_pad, D), np.float32)
    for l in range(L):
        for block in range(wide):
            at = (block % 2) * (wide // 2) + block // 2
            for c in range(width):
                pick[l, at * rows_pad + l * width + c, block * width + c] = 1.0
    local = table_t.shape[1]
    shape = jax.ShapeDtypeStruct
    outs = [shape((L, rows, D), BF16) for rows in ROWS_OF] + [
        shape((narrow, 2, wide // 2, small_pad, TOKS), F32),
        shape((count * CAP, D), BF16),
        shape((cat_index.shape[0], TOKS), jnp.int32),
        shape((count, 1, TOKS), F32),
        shape((1, TOKS), F32),
    ]
    vmem = pl.BlockSpec(memory_space=pltpu.VMEM)
    vm = pltpu.VMEM
    dma = pltpu.SemaphoreType.DMA
    return pl.pallas_call(
        functools.partial(gather_kernel, wide=wide, narrow=narrow, chunk=8),
        out_shape=outs,
        in_specs=[vmem] * 7 + [pl.BlockSpec(memory_space=pl.ANY), vmem],
        out_specs=[vmem] * len(outs),
        scratch_shapes=[
            vm((narrow, 2, wide // 2, rows_pad, cut), BF16),
            vm((narrow, 2, wide // 2, rows_pad, total - cut), BF16),
            vm((count, 1, TOKS), F32),
            vm((D, local), F32),
            vm((D, local), BF16),
            vm((count, PACK, TOKS), BF16),
            vm((count, PACK, TOKS), BF16),
            dma((3, wide // 2)), dma((3, wide // 2)),
            dma((levels + 1, 3, narrow)), dma((levels + 1, 3, narrow)),
            dma((count,)), dma((count,)), dma((count,)), dma((count,)), dma(()),
        ],
        compiler_params=pltpu.CompilerParams(
            collective_id=0, has_side_effects=True, vmem_limit_bytes=62 << 20
        ),
        name="gather",
    )(cat_index, cell_mask, *shards_t, small_t, table_t, jnp.asarray(pick, BF16))


def lanes(vector, width):
    return jnp.concatenate([vector] * (width // vector.shape[1]), 1)


def fold(value):
    total = value[:, :TOKS]
    for start in range(TOKS, value.shape[1], TOKS):
        total = total + value[:, start : start + TOKS]
    return total


def norm_forward(value, gain, shift):
    center = value - jnp.sum(value, 0, keepdims=True) * (1.0 / D)
    spread = jnp.sum(center * center, 0, keepdims=True) * (1.0 / D)
    inverse = lax.rsqrt(spread + NORM_EPS)
    unit = center * inverse
    return unit, inverse, unit * gain + shift


def norm_backward(unit, inverse, grad_unit):
    mean_one = jnp.sum(grad_unit, 0, keepdims=True) * (1.0 / D)
    mean_two = jnp.sum(grad_unit * unit, 0, keepdims=True) * (1.0 / D)
    return inverse * (grad_unit - mean_one - unit * mean_two)


NVEC = 8 * L + 3
ROOM = TOKS // CATF


def model_kernel(
    stats_ref, labels_ref, rows_ref, slots_ref, num_ref, mask_ref,
    qkv_ref, proj_ref, in_ref, down_ref, small_ref,
    loss_ref, dmats_ref, dsmall_ref, dslots_ref,
    rows_t, qkv_t, proj_t, in_t, down_t, tok_s, scale_s, rec_s, class_s, class_t_s,
    dtok_s, dscale_s, drec_s, dclass_s, slots_acc,
    vecb, probs_s, unit_one_s, inv_one_s, normed_s, k_s, v_s, mixed_s,
    unit_two_s, inv_two_s, normed_two_s, gate_s, hidden_s, acc_s, looked_s, wide_s, low_s, ds_s, qlow_s,
    qkv_acc, proj_acc, in_acc, down_acc, num_s, mask_s, coef_s,
    *, pair, wide, narrow,
):
    width = pair * TOKS
    blocks = slots_ref.shape[0] // pair
    columns = D // wide
    own_rows = NSR // narrow
    slots = rows_ref.shape[0]
    offsets, _ = packed_offsets(narrow)
    mats_acc = (qkv_acc, proj_acc, in_acc, down_acc)
    inv_count = 1.0 / jnp.full((1, 1), stats_ref[0, CAP + 1], F32)
    data_rows = slots_ref.shape[0]
    gap = jnp.zeros((data_rows, 1), F32)
    gap_tail = jnp.zeros((data_rows, TOKS - 1 - NUMF), F32)
    masked = mask_ref[...].astype(F32)
    num_s[...] = jnp.concatenate([gap, num_ref[...], gap_tail], 1)
    mask_s[...] = jnp.concatenate([gap, masked, gap_tail], 1)
    coef_s[...] = jnp.concatenate([gap, (1.0 - masked) * num_ref[...], gap_tail], 1)

    rows_t[...] = jnp.transpose(rows_ref[...].astype(F32)).astype(BF16)
    for l in range(L):
        qkv_t[l] = jnp.transpose(qkv_ref[l].astype(F32)).astype(BF16)
        proj_t[l] = jnp.transpose(proj_ref[l].astype(F32)).astype(BF16)
        in_t[l] = jnp.transpose(in_ref[l].astype(F32)).astype(BF16)
        down_t[l] = jnp.transpose(down_ref[l].astype(F32)).astype(BF16)
    pieces = []
    for n in range(narrow):
        piece = jnp.concatenate([small_ref[n, w % 2, w // 2, :columns] for w in range(wide)], 0)
        pieces.append(piece[:, :own_rows])
    small = jnp.concatenate(pieces, 1)
    for i in range(NVEC):
        at = i if i < 8 * L else (OFF_FIN + i - 8 * L if i < 8 * L + 2 else OFF_SCALE + NUMF)
        vecb[i] = jnp.broadcast_to(small[:, at : at + 1], (D, TOKS))
    gap_one = jnp.zeros((D, 1), F32)
    gap_end = jnp.zeros((D, TOKS - 1 - NUMF), F32)
    tok_s[...] = small[:, 8 * L : OFF_SCALE]
    scale_s[...] = jnp.concatenate([gap_one, small[:, OFF_SCALE : OFF_SCALE + NUMF], gap_end], 1)
    rec_s[...] = jnp.concatenate([gap_one, small[:, OFF_FIN + 2 + NCLASS :], gap_end], 1)
    class_t = jnp.concatenate(
        [small[:, OFF_FIN + 2 : OFF_FIN + 2 + NCLASS], jnp.zeros((D, TOKS - NCLASS), F32)], 1
    )
    class_s[...] = jnp.transpose(class_t)[:16].astype(BF16)
    class_t_s[...] = jnp.concatenate([class_t[:, :16]] * 3, 1).astype(BF16)
    for ref in (loss_ref, *mats_acc, dtok_s, dscale_s, drec_s, dclass_s, acc_s):
        ref[...] = jnp.zeros_like(ref)

    def vec(i):
        return lanes(vecb[i], width)

    def head_rows(value, h, b):
        return value[h * HD : h * HD + HD, b * TOKS : b * TOKS + TOKS]

    def two_heads(left, right):
        both = mm(left, right)
        return [both[:HD, :TOKS], both[HD:, TOKS:]]

    def apart(value):
        row = lax.broadcasted_iota(jnp.int32, value.shape, 0)
        upper = jnp.where(row < HD, 1.0, 0.0).astype(BF16)
        lower = jnp.where(row >= HD, 1.0, 0.0).astype(BF16)
        return jnp.concatenate([value * upper, value * lower], 1)

    def add_mats(l, which, value):
        mats_acc[which][l] += value

    def add_vec(i, value):
        acc_s[i] += fold(value)

    def forward(l, x):
        base = 8 * l
        unit, inverse, normed = norm_forward(x, vec(base), vec(base + 1))
        normed = normed.astype(BF16)
        unit_one_s[l] = unit
        inv_one_s[l] = inverse
        normed_s[l] = normed
        joined = mm(qkv_ref[l], normed)
        q_f = joined[:D] + vec(base + 4)
        k_f = joined[D : 2 * D]
        v_f = joined[2 * D :] + vec(base + 5)
        q_low = q_f.astype(BF16)
        qlow_s[l] = q_low
        mixed_cols = []
        for b in range(pair):
            for h in range(HEADS // 2):
                rows = slice(2 * h * HD, 2 * (h + 1) * HD)
                cols = slice(b * TOKS, (b + 1) * TOKS)
                k_s[l, b * HEADS // 2 + h] = k_f[rows, cols].astype(BF16)
                v_s[l, b * HEADS // 2 + h] = v_f[rows, cols].astype(BF16)
        for b in range(pair):
            span = slice(b * TOKS, (b + 1) * TOKS)
            for h in range(HEADS // 2):
                rows = slice(2 * h * HD, 2 * (h + 1) * HD)
                wide_s[b, :, 2 * h * TOKS : 2 * (h + 1) * TOKS] = mm(
                    k_s[l, b * HEADS // 2 + h], apart(q_low[rows, span]), 0, 0
                )
        for b in range(pair):
            for h in range(HEADS):
                u = b * HEADS + h
                scores = wide_s[b, :, h * TOKS : (h + 1) * TOKS]
                top = jnp.max(scores, 0, keepdims=True)
                weight = jnp.exp2((scores - top) * (SCALE * math.log2(math.e)))
                probs = weight * (1.0 / jnp.sum(weight, 0, keepdims=True))
                probs_s[l, u] = probs
                low_s[l, b, :, h * TOKS : (h + 1) * TOKS] = probs.astype(BF16)
        for b in range(pair):
            rows = []
            for h in range(HEADS // 2):
                u = b * HEADS // 2 + h
                rows += two_heads(v_s[l, u], low_s[l, b, :, 2 * h * TOKS : 2 * (h + 1) * TOKS])
            mixed_cols.append(jnp.concatenate(rows, 0))
        mixed = jnp.concatenate(mixed_cols, 1).astype(BF16)
        mixed_s[l] = mixed
        after = x + mm(proj_ref[l], mixed) + vec(base + 6)
        unit, inverse, normed = norm_forward(after, vec(base + 2), vec(base + 3))
        normed = normed.astype(BF16)
        unit_two_s[l] = unit
        inv_two_s[l] = inverse
        normed_two_s[l] = normed
        gate_up = mm(in_ref[l], normed)
        gate_s[l] = gate_up
        gate, up = gate_up[:FF], gate_up[FF:]
        inner = GELU_A * (gate + GELU_B * gate * gate * gate)
        hidden = (0.5 * gate * (1.0 + jnp.tanh(inner)) * up).astype(BF16)
        hidden_s[l] = hidden
        return after + mm(down_t[l], hidden) + vec(base + 7)

    def backward(l, dout):
        base = 8 * l
        add_vec(base + 7, dout)
        up_low = dout.astype(BF16)
        add_mats(l, 3, mm(hidden_s[l], up_low, 1, 1))
        dhidden = mm(down_ref[l], up_low)
        gate, up = gate_s[l, :FF], gate_s[l, FF:]
        square = gate * gate
        tanh = jnp.tanh(GELU_A * (gate + GELU_B * square * gate))
        half = 0.5 * (1.0 + tanh)
        slope = half + 0.5 * gate * (1.0 - tanh * tanh) * (GELU_A * (1.0 + 3.0 * GELU_B * square))
        dgate = dhidden * up * slope
        dup = dhidden * (gate * half)
        dgl = jnp.concatenate([dgate, dup], 0).astype(BF16)
        add_mats(l, 2, mm(dgl, normed_two_s[l], 1, 1))
        dnormed = mm(in_t[l], dgl)
        unit = unit_two_s[l]
        add_vec(base + 2, dnormed * unit)
        add_vec(base + 3, dnormed)
        dafter = dout + norm_backward(unit, inv_two_s[l], dnormed * vec(base + 2))
        add_vec(base + 6, dafter)
        after_low = dafter.astype(BF16)
        add_mats(l, 1, mm(after_low, mixed_s[l], 1, 1))
        dmixed = mm(proj_t[l], after_low)
        dmixed_low = dmixed.astype(BF16)
        q_cols, k_cols, v_cols = [], [], []
        for b in range(pair):
            span = slice(b * TOKS, (b + 1) * TOKS)
            for h in range(HEADS // 2):
                rows = slice(2 * h * HD, 2 * (h + 1) * HD)
                wide_s[b, :, 2 * h * TOKS : 2 * (h + 1) * TOKS] = mm(
                    v_s[l, b * HEADS // 2 + h], apart(dmixed_low[rows, span]), 0, 0
                )
        for b in range(pair):
            for h in range(HEADS):
                u = b * HEADS + h
                probs = probs_s[l, u]
                dprobs = wide_s[b, :, h * TOKS : (h + 1) * TOKS]
                inner = jnp.sum(dprobs * probs, 0, keepdims=True)
                ds_s[b, :, h * TOKS : (h + 1) * TOKS] = (probs * (dprobs - inner) * SCALE).astype(BF16)
        for b in range(pair):
            q_rows = []
            for h in range(HEADS // 2):
                u = b * HEADS // 2 + h
                q_rows += two_heads(k_s[l, u], ds_s[b, :, 2 * h * TOKS : 2 * (h + 1) * TOKS])
            q_cols.append(jnp.concatenate(q_rows, 0))
            span = slice(b * TOKS, (b + 1) * TOKS)
            v_rows, k_rows = [], []
            for h in range(HEADS // 2):
                rows = slice(2 * h * HD, 2 * (h + 1) * HD)
                both = slice(2 * h * TOKS, 2 * (h + 1) * TOKS)
                v_rows.append(mm(apart(dmixed_low[rows, span]), low_s[l, b, :, both], 1, 1))
                k_rows.append(mm(apart(qlow_s[l, rows, span]), ds_s[b, :, both], 1, 1))
            v_cols.append(jnp.concatenate(v_rows, 0))
            k_cols.append(jnp.concatenate(k_rows, 0))
        dq = jnp.concatenate(q_cols, 1)
        dk = jnp.concatenate(k_cols, 1)
        dv = jnp.concatenate(v_cols, 1)
        add_vec(base + 4, dq)
        add_vec(base + 5, dv)
        dj = jnp.concatenate([dq, dk, dv], 0).astype(BF16)
        add_mats(l, 0, mm(dj, normed_s[l], 1, 1))
        dnormed = mm(qkv_t[l], dj)
        unit = unit_one_s[l]
        add_vec(base, dnormed * unit)
        add_vec(base + 1, dnormed)
        return dafter + norm_backward(unit, inv_one_s[l], dnormed * vec(base))

    def step(i, carry):
        def row_of(ref):
            return jnp.concatenate([ref[pl.ds(i * pair + b, 1), :] for b in range(pair)], 1)

        coef = row_of(coef_s)
        num = row_of(num_s)
        mask = row_of(mask_s)
        lane = lax.broadcasted_iota(jnp.int32, (D, TOKS), 1)
        placed = []
        for b in range(pair):
            found = looked_s[i, :, (b // ROOM) * TOKS : (b // ROOM + 1) * TOKS]
            shift = (TOKS - CATF - b * CATF) % TOKS
            moved = pltpu.roll(found, shift, 1) if shift else found
            placed.append(jnp.where(lane < TOKS - CATF, 0.0, moved))
        x = jnp.concatenate(placed, 1) + lanes(tok_s[...], width)
        x = x + coef * lanes(scale_s[...], width) + mask * vec(8 * L + 2)
        for l in range(L):
            x = forward(l, x)
        unit, inverse, final = norm_forward(x, vec(8 * L), vec(8 * L + 1))
        rec = lanes(rec_s[...], width)
        error = jnp.sum(final * rec, 0, keepdims=True) - num
        final_low = final.astype(BF16)
        logits = mm(class_s[...], final_low)
        row = lax.broadcasted_iota(jnp.int32, logits.shape, 0)
        lane = lax.broadcasted_iota(jnp.int32, logits.shape, 1)
        live = row < NCLASS
        logits = jnp.where(live, logits, -1e30)
        top = jnp.max(logits, 0, keepdims=True)
        weight = jnp.where(live, jnp.exp(logits - top), 0.0)
        sums = jnp.sum(weight, 0, keepdims=True)
        first = (lane % TOKS) == 0
        label = jnp.concatenate(
            [jnp.full((1, TOKS), labels_ref[i * pair + b], jnp.int32) for b in range(pair)], 1
        )
        hit = jnp.where(first & (row == label), 1.0, 0.0)
        firsts = jnp.where(first[:1], 1.0, 0.0)
        picked = jnp.sum(jnp.where(hit > 0, logits, 0.0), 0, keepdims=True)
        loss_ref[...] += fold(mask * error * error + firsts * (top + jnp.log(sums)) - picked)
        dlogits = (firsts * weight / sums - hit) * inv_count
        dpredict = (2.0 * inv_count) * mask * error
        parts = jnp.concatenate([p.astype(F32) for p in split_three(dlogits)], 0).astype(BF16)
        dclass_s[...] += mm(final_low, parts, 1, 1)
        drec_s[...] += fold(final * dpredict)
        dfinal = rec * dpredict + mm(class_t_s[...], parts)
        add_vec(8 * L, dfinal * unit)
        add_vec(8 * L + 1, dfinal)
        dx = norm_backward(unit, inverse, dfinal * vec(8 * L))
        for l in reversed(range(L)):
            dx = backward(l, dx)
        dtok_s[...] += fold(dx)
        dscale_s[...] += fold(coef * dx)
        acc_s[8 * L + 2] += fold(mask * dx)
        packed = [jnp.zeros((D, TOKS), F32) for _ in range(groups)]
        group = lax.broadcasted_iota(jnp.int32, (D, TOKS), 1) // CATF
        for b in range(pair):
            part = dx[:, b * TOKS : (b + 1) * TOKS]
            shift = (b * CATF + CATF) % TOKS
            if shift:
                part = pltpu.roll(part, shift, 1)
            packed[b // ROOM] = jnp.where(group == b % ROOM, part, packed[b // ROOM])
        for at in range(groups):
            looked_s[i, :, at * TOKS : (at + 1) * TOKS] = packed[at]
        return carry

    groups = -(-pair // ROOM)
    spare = groups * TOKS - pair * CATF

    def hits_of(i):
        pieces = [
            slots_ref[i * pair + b : i * pair + b + 1, TOKS - CATF :] for b in range(pair)
        ]
        if spare:
            pieces.append(jnp.full((1, spare), -1, jnp.int32))
        slot = lax.broadcasted_iota(jnp.int32, (slots, groups * TOKS), 0)
        return jnp.where(slot == jnp.concatenate(pieces, 1), 1.0, 0.0).astype(BF16)

    for i in range(blocks):
        looked_s[i] = mm(rows_t[...], hits_of(i))
    lax.fori_loop(0, blocks, step, 0)
    slots_acc[...] = jnp.zeros_like(slots_acc)
    for i in range(blocks):
        slots_acc[...] += mm(hits_of(i), looked_s[i].astype(BF16), 1, 1)

    dvec = [jnp.sum(acc_s[i], 1, keepdims=True) for i in range(NVEC)]
    dclass = dclass_s[...]
    dclass = dclass[:, :16] + dclass[:, 16:32] + dclass[:, 32:]
    dsmall = jnp.concatenate(
        dvec[: 8 * L]
        + [dtok_s[...], dscale_s[:, 1 : 1 + NUMF], dvec[8 * L + 2]]
        + dvec[8 * L : 8 * L + 2]
        + [dclass[:, :NCLASS], drec_s[:, 1 : 1 + NUMF]],
        1,
    )
    blank = jnp.zeros((D, TOKS - own_rows), F32)
    for n in range(narrow):
        piece = jnp.concatenate([dsmall[:, n * own_rows : (n + 1) * own_rows], blank], 1)
        if dsmall_ref.shape[2] == columns:
            dsmall_ref[n] = piece.reshape(wide, columns, TOKS)
        else:
            dsmall_ref[n] = jnp.zeros(dsmall_ref.shape[1:], F32)
            for w in range(wide):
                dsmall_ref[n, w, :columns] = piece[w * columns : (w + 1) * columns]

    def beside(tail):
        rows = tail.shape[0]
        tail = jnp.concatenate([tail, jnp.zeros((rows, 2 * TOKS - D), F32)], 1)
        lane = lax.broadcasted_iota(jnp.int32, (rows // 2, TOKS), 1)
        return jnp.where(
            lane < D - TOKS, tail[: rows // 2], pltpu.roll(tail[rows // 2 :], D - TOKS, 1)
        )

    for which in range(4):
        size = ROWS_OF[which] // narrow
        for l in range(L):
            for n in range(narrow):
                part = mats_acc[which][l, n * size : (n + 1) * size]
                at = offsets[which]
                dmats_ref[l, n, at : at + size] = part[:, :TOKS]
                dmats_ref[l, n, at + size : at + size + size // 2] = beside(part[:, TOKS:])

    terms = slots_acc[...]
    dslots_ref[:, :CAP] = terms[:, :TOKS].reshape(slots // CAP, CAP, TOKS).astype(BF16)
    tail = jnp.concatenate([terms[:, TOKS:], jnp.zeros((slots, 2 * TOKS - D), F32)], 1)
    tail = tail.reshape(slots // CAP, CAP, TOKS)
    low = tail[:, : CAP // 2].reshape(slots // 2, TOKS)
    high = pltpu.roll(tail[:, CAP // 2 :].reshape(slots // 2, TOKS), D - TOKS, 1)
    lane = lax.broadcasted_iota(jnp.int32, (slots // 2, TOKS), 1)
    dslots_ref[:, CAP:] = (
        jnp.where(lane < D - TOKS, low, high).reshape(slots // CAP, CAP // 2, TOKS).astype(BF16)
    )


def model_call(stats, labels, rows, slots, num, mask, mats, small, pair, wide, narrow):
    width = pair * TOKS
    used = rows.shape[0]
    _, total = packed_offsets(narrow)
    shape = jax.ShapeDtypeStruct
    outs = [
        shape((1, TOKS), F32),
        shape((L, narrow, total, TOKS), F32),
        shape((narrow, wide, small.shape[3], TOKS), F32),
        shape((used // CAP, PACK, TOKS), BF16),
    ]
    units = pair * HEADS
    vm = pltpu.VMEM
    scratch = [
        vm((D, used), BF16),
        vm((L, D, 3 * D), BF16), vm((L, D, D), BF16), vm((L, D, 2 * FF), BF16), vm((L, D, FF), BF16),
        vm((D, TOKS), F32), vm((D, TOKS), F32), vm((D, TOKS), F32), vm((16, D), BF16), vm((D, 48), BF16),
        vm((D, TOKS), F32), vm((D, TOKS), F32), vm((D, TOKS), F32), vm((D, 48), F32), vm((used, D), F32),
        vm((NVEC, D, TOKS), F32), vm((L, units, TOKS, TOKS), F32),
        vm((L, D, width), F32), vm((L, 1, width), F32), vm((L, D, width), BF16),
        vm((L, units // 2, 2 * HD, TOKS), BF16), vm((L, units // 2, 2 * HD, TOKS), BF16),
        vm((L, D, width), BF16),
        vm((L, D, width), F32), vm((L, 1, width), F32), vm((L, D, width), BF16),
        vm((L, 2 * FF, width), F32), vm((L, FF, width), BF16),
        vm((NVEC, D, TOKS), F32), vm((slots.shape[0] // pair, D, -(-pair // ROOM) * TOKS), F32), vm((pair, TOKS, HEADS * TOKS), F32), vm((L, pair, TOKS, HEADS * TOKS), BF16), vm((pair, TOKS, HEADS * TOKS), BF16), vm((L, D, width), BF16),
        *[vm((L, rows, D), F32) for rows in ROWS_OF],
        *[vm((slots.shape[0], TOKS), F32)] * 3,
    ]
    spec = pl.BlockSpec(memory_space=pltpu.VMEM)
    return pl.pallas_call(
        functools.partial(model_kernel, pair=pair, wide=wide, narrow=narrow),
        out_shape=outs,
        in_specs=[pl.BlockSpec(memory_space=pltpu.SMEM)] * 2 + [spec] * 9,
        out_specs=[spec] * len(outs),
        scratch_shapes=scratch,
        compiler_params=pltpu.CompilerParams(vmem_limit_bytes=62 << 20),
        name="model",
    )(stats, labels, rows, slots, num, mask, *mats, small)


def packed_rows(which, narrow):
    size = ROWS_OF[which] // narrow
    return size + size // 2


def packed_offsets(narrow):
    offsets, total = [], 0
    for which in range(4):
        offsets.append(total)
        total += packed_rows(which, narrow)
    return offsets, total


def worker_of(m, wide):
    layer, kind = m // 4, m % 4
    return (layer * 2 + kind % 2) * (wide // 8) * 2 + kind // 2


def adam_step(weight, gradient, first, second):
    first = BETA_ONE * first + (1.0 - BETA_ONE) * gradient
    second = BETA_TWO * second + (1.0 - BETA_TWO) * gradient * gradient
    ratio = first / (1.0 - BETA_ONE**STEP) / (jnp.sqrt(second / (1.0 - BETA_TWO**STEP)) + ADAM_EPS)
    return (weight - ADAM_RATE * (ratio + DECAY * weight), first, second)


def exact(left, right, left_dim=1, right_dim=0):
    return lax.dot_general(
        left, right, (((left_dim,), (right_dim,)), ((), ())), preferred_element_type=F32,
        precision=lax.Precision.HIGHEST,
    )


def finish_kernel(*refs, wide, narrow):
    refs = list(refs)

    def take(number):
        head = refs[:number]
        del refs[:number]
        return head

    levels = levels_of(narrow)
    count = wide * narrow
    columns = D // wide
    mats_any, dsmall_ref, dslots_ref, requests_ref, loss_ref, extra_any = take(6)
    moments = take(4)
    out_stats, table_any, out_small = take(3)
    x_came, out_moments = take(4), take(4)
    steps = levels + 1
    mats_held = [take(steps) for _ in range(L)]
    mats_came = [take(steps) for _ in range(L)]
    small_held, small_came = take(levels), take(levels)
    landed, hits, mats_landed, small_landed, grad_s = take(5)
    dmats_ref, out_table = take(2)
    norm_near, norm_all = take(2)
    mom_came, mom_sent, x_sent = take(4), take(4), take(4)
    x_start, x_end, gram_held, gram_came = take(4)
    (
        slot_send, slot_recv, mats_send, mats_recv, small_send, small_recv,
        block_send, block_recv, own_send, own_recv,
        near_send, near_recv, norm_send, norm_recv, get_send, get_recv, put_send, put_recv, new_send, new_recv,
        gram_send, gram_recv, mats_sem, extra_sem, table_sem,
    ) = refs
    mats_copy = pltpu.make_async_copy(mats_any, dmats_ref, mats_sem)
    extra_copy = pltpu.make_async_copy(extra_any, out_table, extra_sem)
    table_copy = pltpu.make_async_copy(out_table, table_any, table_sem)
    mats_copy.start()
    extra_copy.start()
    w, n, me = place(wide, narrow)
    barrier = greet_all(me, count, narrow)
    offsets, total = packed_offsets(narrow)
    half_rows = total // 2
    local = extra_any.shape[1]
    side = lax.rem(w, 2)

    def over_peers(origin, size, body):
        def run(k, carry):
            body(lax.rem(origin + k, size))
            return carry

        lax.fori_loop(1, size, run, 0)

    def coords(p):
        return (p // narrow, lax.rem(p, narrow))

    def narrow_partner(s):
        bit = lax.rem(n // (1 << s), 2)
        return bit, n + (1 - 2 * bit) * (1 << s)

    def plan(l):
        if l % 2:
            return list(range(levels)) + ["side"]
        return [0, "side"] + list(range(1, levels)) if levels else ["side"]

    def before(l, t):
        return dmats_ref.at[l] if t == 0 else mats_held[l][t - 1]

    def step_copies(l, t):
        move = plan(l)[t]
        source = before(l, t)
        copies = []
        if move == "side":
            for j in range(source.shape[0]):
                copies.append(
                    pltpu.make_async_remote_copy(
                        src_ref=source.at[j, pl.ds((1 - side) * half_rows, half_rows)],
                        dst_ref=mats_came[l][t].at[j],
                        send_sem=mats_send.at[l, t, j], recv_sem=mats_recv.at[l, t, j],
                        device_id=(w + 1 - 2 * side, n), device_id_type=MESH,
                    )
                )
        else:
            bit, partner = narrow_partner(move)
            for j in range(source.shape[0] // 2):
                copies.append(
                    pltpu.make_async_remote_copy(
                        src_ref=source.at[2 * j + 1 - bit], dst_ref=mats_came[l][t].at[j],
                        send_sem=mats_send.at[l, t, j], recv_sem=mats_recv.at[l, t, j],
                        device_id=(w, partner), device_id_type=MESH,
                    )
                )
        return copies

    def step_add(l, t):
        move = plan(l)[t]
        source = before(l, t)
        for j in range(mats_held[l][t].shape[0]):
            if move == "side":
                mine = source[j, pl.ds(side * half_rows, half_rows)]
            else:
                mine = source[2 * j + narrow_partner(move)[0]]
            mats_held[l][t][j] = mine + mats_came[l][t][j]

    def small_before(s):
        return dsmall_ref if s == 0 else small_held[s - 1]

    def small_copies(s):
        bit, partner = narrow_partner(s)
        return [
            pltpu.make_async_remote_copy(
                src_ref=small_before(s).at[2 * j + 1 - bit], dst_ref=small_came[s].at[j],
                send_sem=small_send.at[s, j], recv_sem=small_recv.at[s, j],
                device_id=(w, partner), device_id_type=MESH,
            )
            for j in range(narrow >> (s + 1))
        ]

    def small_add(s):
        bit, _ = narrow_partner(s)
        for j in range(narrow >> (s + 1)):
            small_held[s][j] = small_before(s)[2 * j + bit] + small_came[s][j]

    def slot_copy(p, slot):
        return pltpu.make_async_remote_copy(
            src_ref=dslots_ref.at[p], dst_ref=landed.at[slot], send_sem=slot_send.at[p],
            recv_sem=slot_recv.at[slot], device_id=coords(p), device_id_type=MESH,
        )

    def block_copy(m, slot):
        layer, kind = m // 4, m % 4
        start = offsets[kind] - half_rows * (kind // 2)
        size = packed_rows(kind, narrow)
        return pltpu.make_async_remote_copy(
            src_ref=mats_held[layer][steps - 1].at[0, pl.ds(start, size)],
            dst_ref=mats_landed.at[slot, pl.ds(0, size)],
            send_sem=block_send.at[m], recv_sem=block_recv.at[slot],
            device_id=(worker_of(m, wide), n), device_id_type=MESH,
        )

    def own_copy(p, slot):
        return pltpu.make_async_remote_copy(
            src_ref=small_held[levels - 1].at[0, p], dst_ref=small_landed.at[slot],
            send_sem=own_send.at[p], recv_sem=own_recv.at[slot], device_id=(p, n),
            device_id_type=MESH,
        )

    def near_copy(p, slot):
        return pltpu.make_async_remote_copy(
            src_ref=norm_near.at[n], dst_ref=norm_near.at[slot], send_sem=near_send.at[p],
            recv_sem=near_recv.at[slot], device_id=(w, p), device_id_type=MESH,
        )

    def norm_copy(p, slot):
        return pltpu.make_async_remote_copy(
            src_ref=norm_all.at[w], dst_ref=norm_all.at[slot], send_sem=norm_send.at[p],
            recv_sem=norm_recv.at[slot], device_id=(p, n), device_id_type=MESH,
        )

    def get_copy(m, slot):
        return pltpu.make_async_remote_copy(
            src_ref=moments[m % 4].at[m // 4], dst_ref=mom_came[m % 4].at[slot],
            send_sem=get_send.at[m], recv_sem=get_recv.at[slot],
            device_id=(worker_of(m, wide), n), device_id_type=MESH,
        )

    def put_copy(m, p):
        return pltpu.make_async_remote_copy(
            src_ref=mom_sent[m % 4].at[p], dst_ref=out_moments[m % 4].at[m // 4],
            send_sem=put_send.at[p], recv_sem=put_recv.at[m], device_id=(p, n),
            device_id_type=MESH,
        )

    def new_copy(m, p):
        return pltpu.make_async_remote_copy(
            src_ref=x_sent[m % 4].at[p], dst_ref=x_came[m % 4].at[m // 4],
            send_sem=new_send.at[p], recv_sem=new_recv.at[m], device_id=(p, n),
            device_id_type=MESH,
        )

    def gram_copy(s):
        _, partner = narrow_partner(s)
        return pltpu.make_async_remote_copy(
            src_ref=gram_held.at[s], dst_ref=gram_came.at[s], send_sem=gram_send.at[s],
            recv_sem=gram_recv.at[s], device_id=(w, partner), device_id_type=MESH,
        )

    pl.semaphore_wait(barrier, count - 1)
    mats_copy.wait()
    for l in range(L):
        for copy in step_copies(l, 0):
            copy.start()
    for copy in small_copies(0):
        copy.start()
    over_peers(me, count, lambda p: slot_copy(p, me).start())
    landed[me] = dslots_ref[me]
    for m in range(4 * L):
        @pl.when(w != worker_of(m, wide))
        def _():
            get_copy(m, w).start()

        @pl.when(w == worker_of(m, wide))
        def _():
            mom_came[m % 4][w] = moments[m % 4][m // 4]

    eye = lax.broadcasted_iota(jnp.int32, (CAP, TOKS), 0) == lax.broadcasted_iota(
        jnp.int32, (CAP, TOKS), 1
    )
    spots = lax.broadcasted_iota(jnp.int32, (CAP, local), 1)

    def find(c, carry):
        for j in range(8):
            q = c * 8 + j
            row = jnp.broadcast_to(requests_ref[q], (CAP, TOKS))
            column = jnp.sum(jnp.where(eye, row, 0.0), 1, keepdims=True).astype(jnp.int32)
            at = pl.multiple_of(q * CAP, CAP)
            hits[pl.ds(at, CAP), :] = jnp.where(spots == column, 1.0, 0.0).astype(BF16)
        return carry

    lax.fori_loop(0, count // 8, find, 0)

    def finish_step(t):
        for l in range(L):
            for copy in step_copies(l, t):
                copy.wait_recv()
            step_add(l, t)
        if t < levels:
            for copy in small_copies(t):
                copy.wait_recv()
            small_add(t)
        if t + 1 < steps:
            for l in range(L):
                for copy in step_copies(l, t + 1):
                    copy.start()
        if t + 1 < levels:
            for copy in small_copies(t + 1):
                copy.start()

    finish_step(0)

    over_peers(me, count, lambda p: slot_copy(p, p).wait_recv())
    terms_t = jnp.transpose(spread_slots(landed[...].astype(F32)))
    if steps > 2:
        finish_step(1)
    extra_copy.wait()
    out_table[...] += mm(terms_t.astype(BF16), hits[...])
    table_copy.start()
    for t in range(2 if steps > 2 else 1, steps):
        finish_step(t)

    over_peers(w, wide, lambda p: own_copy(p, w).start())
    for m in range(4 * L):
        kind = m % 4

        @pl.when((side == kind // 2) & (w != worker_of(m, wide)))
        def _():
            block_copy(m, w).start()

    table_grad = out_table[...]

    def total_of(value):
        return jnp.sum(jnp.sum(value, 0, keepdims=True), 1, keepdims=True)

    squares = total_of(table_grad * table_grad)
    loss_here = jnp.sum(loss_ref[...], 1, keepdims=True)
    x_start[...] = jnp.zeros_like(x_start)
    grad_s[...] = jnp.zeros_like(grad_s)

    over_peers(w, wide, lambda p: own_copy(p, p).wait_recv())

    def add_small(k, value):
        return value + small_landed[lax.rem(w + k, wide)]

    own_small = lax.fori_loop(1, wide, add_small, small_held[levels - 1][0, w])
    squares = squares + total_of(own_small * own_small)
    out_small[...] = own_small
    for m in range(4 * L):
        layer, kind = m // 4, m % 4

        @pl.when(w == worker_of(m, wide))
        def _():
            start = offsets[kind] - half_rows * (kind // 2)
            size = packed_rows(kind, narrow)
            whole = ROWS_OF[kind] // narrow

            def add_block(k, value):
                p = lax.rem(w // 2 + k, wide // 2) * 2 + side
                block_copy(m, p).wait_recv()
                return value + mats_landed[p, :size]

            packed = lax.fori_loop(
                1, wide // 2, add_block,
                mats_held[layer][steps - 1][0, start : start + size],
            )
            tail = packed[whole:]
            grad_s[:whole, :TOKS] = packed[:whole]
            grad_s[: whole // 2, TOKS : D] = tail[:, : D - TOKS]
            grad_s[whole // 2 : whole, TOKS : D] = tail[:, D - TOKS :]

    grad = grad_s[...]
    squares = squares + total_of(grad * grad)
    lane = lax.broadcasted_iota(jnp.int32, (1, TOKS), 1)
    norm_near[n] = jnp.where(lane == 0, squares, jnp.where(lane == 1, loss_here, 0.0))
    over_peers(n, narrow, lambda p: near_copy(p, n).start())
    grad_t = jnp.transpose(grad)[:D]
    over_peers(n, narrow, lambda p: near_copy(p, p).wait_recv())
    norm_all[w] = jnp.sum(norm_near[...], 0)
    over_peers(w, wide, lambda p: norm_copy(p, w).start())
    over_peers(w, wide, lambda p: norm_copy(p, p).wait_recv())
    sums = jnp.sum(norm_all[...], 0)
    norm = jnp.sqrt(sums)
    factor = CLIP / jnp.maximum(norm[:, :1], CLIP)
    out_stats[...] = jnp.where(lane == 0, norm, jnp.where(lane == 2, factor, sums))

    def gather_rows(ref):
        if columns % 8 == 0:
            return ref[...].reshape(D, ref.shape[2])
        return jnp.concatenate([ref[p] for p in range(wide)], 0)

    def spread_rows(ref, value):
        if columns % 8 == 0:
            ref[...] = value.reshape(ref.shape)
        else:
            for p in range(wide):
                ref[p] = value[p * columns : (p + 1) * columns]

    for m in range(4 * L):
        @pl.when(w == worker_of(m, wide))
        def _():
            over_peers(w, wide, lambda p: get_copy(m, p).wait_recv())
            size = ROWS_OF[m % 4] // narrow
            moment = MOMENTUM * gather_rows(mom_came[m % 4]) + factor * grad_t[:, :size]
            x_start[:, :size] = moment
            spread_rows(mom_sent[m % 4], moment)
            over_peers(w, wide, lambda p: put_copy(m, p).start())
            out_moments[m % 4][m // 4] = mom_sent[m % 4][w]

    x = x_start[...]
    gram = exact(x, x, 1, 1)
    rest = D - TOKS
    gram_held[0, :D] = gram[:, :TOKS]
    gram_held[0, D : D + rest] = jnp.concatenate(
        [gram[TOKS:, TOKS:], jnp.zeros((rest, TOKS - rest), F32)], 1
    )
    for s in range(levels):
        gram_copy(s).start()
        gram_copy(s).wait_recv()
        gram_held[s + 1] = gram_held[s] + gram_came[s]
    left = gram_held[levels, :D]
    corner = gram_held[levels, D : D + rest][:, :rest]
    above = jnp.transpose(
        jnp.concatenate([left[TOKS:], jnp.zeros((TOKS - rest, TOKS), F32)], 0)
    )[:, :rest]
    gram = jnp.concatenate([left, jnp.concatenate([above, corner], 0)], 1)
    eye = jnp.where(
        lax.broadcasted_iota(jnp.int32, (D, D), 0) == lax.broadcasted_iota(jnp.int32, (D, D), 1),
        1.0, 0.0,
    )
    inverse = lax.rsqrt(total_of(eye * gram) + ORTHO_EPS)
    square = gram * (inverse * inverse)
    x = x * inverse
    for step in range(5):
        polynomial = NS_ONE * eye + NS_TWO * square + NS_THREE * exact(square, square)
        x = exact(polynomial, x)
        if step < 4:
            square = exact(polynomial, exact(square, polynomial))
    x_end[...] = x
    for m in range(4 * L):
        @pl.when(w == worker_of(m, wide))
        def _():
            size = ROWS_OF[m % 4] // narrow
            spread_rows(x_sent[m % 4], x_end[:, :size])
            over_peers(w, wide, lambda p: new_copy(m, p).start())
            x_came[m % 4][m // 4] = x_sent[m % 4][w]

    for m in range(4 * L):
        @pl.when(w != worker_of(m, wide))
        def _():
            new_copy(m, w).wait_recv()

    for m in range(4 * L):
        @pl.when(w != worker_of(m, wide))
        def _():
            put_copy(m, w).wait_recv()
            get_copy(m, w).wait_send()

        @pl.when((side == (m % 4) // 2) & (w != worker_of(m, wide)))
        def _():
            block_copy(m, w).wait_send()

        @pl.when(w == worker_of(m, wide))
        def _():
            over_peers(w, wide, lambda p: put_copy(m, p).wait_send())
            over_peers(w, wide, lambda p: new_copy(m, p).wait_send())

    table_copy.wait()
    for s in range(levels):
        gram_copy(s).wait_send()
        for copy in small_copies(s):
            copy.wait_send()
    for l in range(L):
        for t in range(steps):
            for copy in step_copies(l, t):
                copy.wait_send()
    over_peers(n, narrow, lambda p: near_copy(p, n).wait_send())
    over_peers(w, wide, lambda p: norm_copy(p, w).wait_send())
    over_peers(me, count, lambda p: slot_copy(p, me).wait_send())
    over_peers(w, wide, lambda p: own_copy(p, w).wait_send())


def finish_call(dmats, dsmall, dslots, requests, loss, extra, moments, wide, narrow):
    count = wide * narrow
    levels = levels_of(narrow)
    columns = D // wide
    _, total = packed_offsets(narrow)
    shape = jax.ShapeDtypeStruct
    local = extra.shape[1]
    outs = [shape((1, TOKS), F32), shape(extra.shape, F32), shape(dsmall.shape[2:], F32)]
    outs += [shape(a.shape, F32) for a in moments + moments]
    vm = pltpu.VMEM
    dma = pltpu.SemaphoreType.DMA
    steps = levels + 1

    def mats_shapes(l):
        sizes, quarters, rows = [], narrow, total
        plan = list(range(levels)) + ["side"] if l % 2 else [0, "side"] + list(range(1, levels))
        for move in plan:
            if move == "side":
                rows //= 2
            else:
                quarters //= 2
            sizes.append(vm((quarters, rows, TOKS), F32))
        return sizes

    mats = [v for l in range(L) for v in mats_shapes(l)]
    small_shapes = [vm((narrow >> (s + 1),) + dsmall.shape[1:], F32) for s in range(levels)]
    largest = max(packed_rows(which, narrow) for which in range(4))
    blocks = [vm((wide, columns, rows // narrow), F32) for rows in ROWS_OF]
    spec = pl.BlockSpec(memory_space=pltpu.VMEM)
    anywhere = pl.BlockSpec(memory_space=pl.ANY)
    return pl.pallas_call(
        functools.partial(finish_kernel, wide=wide, narrow=narrow),
        out_shape=outs,
        in_specs=[anywhere] + [spec] * 4 + [anywhere] + [spec] * 4,
        out_specs=[spec, anywhere] + [spec] * (len(outs) - 2),
        scratch_shapes=mats * 2 + small_shapes * 2
        + [
            vm(dslots.shape, BF16),
            vm((count * CAP, local), BF16),
            vm((wide, largest, TOKS), F32),
            vm((wide,) + dsmall.shape[2:], F32),
            vm((2 * TOKS, 2 * TOKS), F32),
            vm(dmats.shape, F32),
            vm(extra.shape, F32),
            vm((narrow, 1, TOKS), F32),
            vm((wide, 1, TOKS), F32),
        ]
        + blocks * 3
        + [
            vm((D, 2 * TOKS), F32), vm((D, 2 * TOKS), F32),
            vm((levels + 1, 2 * TOKS, TOKS), F32), vm((levels, 2 * TOKS, TOKS), F32),
            dma((count,)), dma((count,)),
            dma((L, steps, narrow)), dma((L, steps, narrow)),
            dma((levels, narrow // 2)), dma((levels, narrow // 2)),
            dma((4 * L,)), dma((wide,)), dma((wide,)), dma((wide,)),
            dma((narrow,)), dma((narrow,)), dma((wide,)), dma((wide,)),
            dma((4 * L,)), dma((wide,)), dma((wide,)), dma((4 * L,)),
            dma((wide,)), dma((4 * L,)), dma((levels,)), dma((levels,)),
            dma(()), dma(()), dma(()),
        ],
        compiler_params=pltpu.CompilerParams(
            collective_id=1, has_side_effects=True, vmem_limit_bytes=62 << 20
        ),
        name="finish",
    )(dmats, dsmall, dslots, requests, loss, extra, *moments)


def apply_kernel(*refs):
    refs = list(refs)

    def take(number):
        head = refs[:number]
        del refs[:number]
        return head

    stats_ref, start_ref = take(2)
    tables, (gsmall_ref,), smalls = take(4), take(1), take(3)
    weights, ortho, moments = take(4), take(4), take(4)
    out_scalars, out_tables, out_smalls = take(3), take(3), take(3)
    out_weights, out_moments = take(4), take(4)
    factor = jnp.full((1, 1), stats_ref[0, 2], F32)
    table, grad, first, second = (ref[...] for ref in tables)
    for ref, value in zip(out_tables, adam_step(table, factor * grad, first, second)):
        ref[...] = value

    @pl.when(pl.program_id(0) == 0)
    def _():
        out_scalars[0][0, 0] = stats_ref[0, 1]
        out_scalars[1][0, 0] = start_ref[0, CAP + 1]
        out_scalars[2][0, 0] = stats_ref[0, 0]
        small, first, second = (ref[...] for ref in smalls)
        grad = gsmall_ref[: small.shape[0], : small.shape[1]]
        for ref, value in zip(out_smalls, adam_step(small, factor * grad, first, second)):
            ref[...] = value
        for which in range(4):
            scale = math.sqrt(max(1.0, ROWS_OF[which] / D))
            out_weights[which][...] = (
                weights[which][...] * (1.0 - MUON_RATE * DECAY)
                - MUON_RATE * scale * ortho[which][...]
            )
            out_moments[which][...] = moments[which][...]


def apply_call(stats, start_stats, tables, gsmall, smalls, weights, ortho, moments):
    shape = jax.ShapeDtypeStruct
    smem = pl.BlockSpec(memory_space=pltpu.SMEM)
    local = tables[0].shape[1]
    rows = D // 2
    block = pl.BlockSpec((rows, local), lambda i: (i, 0))

    def whole(array):
        return pl.BlockSpec(array.shape, lambda i, nd=array.ndim: (0,) * nd)

    beside = smalls + weights + ortho + moments
    outs = smalls + weights + moments
    return pl.pallas_call(
        apply_kernel,
        grid=(D // rows,),
        out_shape=[shape((1, 1), F32)] * 3
        + [shape(tables[0].shape, F32)] * 3
        + [shape(a.shape, F32) for a in outs],
        in_specs=[smem, smem] + [block] * 4 + [whole(gsmall)] + [whole(a) for a in beside],
        out_specs=[smem] * 3 + [block] * 3 + [whole(a) for a in outs],
        compiler_params=pltpu.CompilerParams(vmem_limit_bytes=62 << 20),
        name="apply",
    )(stats, start_stats, *tables, gsmall, *beside)


def per_device(
    cat_index, num_values, cell_mask, labels, table, table_first, table_second,
    small, small_first, small_second, w_qkv, w_proj, w_in, w_down,
    mom_qkv, mom_proj, mom_in, mom_down,
):
    wide = lax.axis_size("wide")
    narrow = lax.axis_size("narrow")
    count = wide * narrow
    data_rows = num_values.shape[0]
    pair = 4 if count * CAP <= 2048 else 4
    while data_rows % pair:
        pair //= 2
    flip = lambda v: jnp.swapaxes(v, -1, -2)
    weights = [flip(v) for v in (w_qkv, w_proj, w_in, w_down)]
    moments = [flip(v) for v in (mom_qkv, mom_proj, mom_in, mom_down)]
    smalls = [flip(v) for v in (small, small_first, small_second)]
    tables = [flip(v) for v in (table, table_first, table_second)]
    qkv, proj, w_in_all, down, small_all, rows, slots, requests, stats = gather_call(
        cat_index, cell_mask, weights, smalls[0], tables[0], wide, narrow
    )
    over = stats[0, CAP] > 0.5
    entries = cat_index.size

    axes = ("wide", "narrow")
    local = table.shape[0]
    me = lax.axis_index("wide") * narrow + lax.axis_index("narrow")
    ring = [(i, (i + 1) % count) for i in range(count)]

    def hits_at(owner):
        spot = cat_index.reshape(-1) - owner * local
        return (spot[:, None] == lax.iota(jnp.int32, local)[None, :]).astype(BF16)

    def general_rows(rows, slots):
        def turn(s, carry):
            block, looked = carry
            looked = looked + mm(hits_at(lax.rem(me - s + count, count)), block)
            return lax.ppermute(block, axes, ring), looked

        first = (table.astype(BF16), jnp.zeros((entries, D), F32))
        looked = lax.fori_loop(0, count, turn, first)[1].astype(BF16)
        spare = jnp.zeros((rows.shape[0] - entries, D), BF16)
        own = lax.iota(jnp.int32, entries).reshape(cat_index.shape)
        none = jnp.full((data_rows, TOKS - CATF), -1, jnp.int32)
        return jnp.concatenate([looked, spare], 0), jnp.concatenate([none, own], 1)

    def general_terms(dslots):
        tail = dslots[:, CAP:]
        tail = jnp.concatenate([tail[:, :, : D - TOKS], tail[:, :, D - TOKS :]], 1)
        terms = jnp.concatenate([dslots[:, :CAP], tail], 2).reshape(count * CAP, D)[:entries]

        def turn(s, sums):
            owner = lax.rem(me - 1 - s + 2 * count, count)
            return lax.ppermute(sums, axes, ring) + mm(terms, hits_at(owner), 0, 0)

        sums = lax.fori_loop(0, count, turn, jnp.zeros(tables[0].shape, F32))
        return sums, jnp.zeros_like(dslots)

    rows, slots = lax.cond(over, general_rows, lambda r, s: (r, s), rows, slots)
    loss, dmats, dsmall, dslots = model_call(
        stats, labels, rows, slots, num_values, cell_mask,
        (qkv, proj, w_in_all, down), small_all, pair, wide, narrow,
    )
    extra, dslots = lax.cond(
        over, general_terms, lambda d: (jnp.zeros(tables[0].shape, F32), d), dslots
    )
    outs = finish_call(dmats, dsmall, dslots, requests, loss, extra, moments, wide, narrow)
    done = apply_call(
        outs[0], stats, [tables[0], outs[1], *tables[1:]], outs[2], smalls, weights,
        list(outs[3:7]), list(outs[7:11]),
    )
    return tuple(v.reshape(()) for v in done[:3]) + tuple(flip(v) for v in done[3:])


def solution(mesh):
    rows = P(("wide", "narrow"), None)
    square = P("narrow", "wide")
    cube = P(None, "narrow", "wide")
    return jax.shard_map(
        per_device,
        mesh=mesh,
        in_specs=(rows, rows, rows, P(("wide", "narrow")), rows, rows, rows)
        + (square,) * 3 + (cube,) * 8,
        out_specs=(P(), P(), P(), rows, rows, rows) + (square,) * 3 + (cube,) * 8,
        check_vma=False,
    )
```

```python
import functools
import math

import jax
import jax.numpy as jnp
import numpy as np
from jax import lax
from jax.experimental import pallas as pl
from jax.experimental.pallas import tpu as pltpu
from jax.sharding import PartitionSpec as P

D = 192
HEADS = 8
HD = 24
FF = 256
L = 2
NUMF = 95
CATF = 32
NCLASS = 7
STEP = 10
TOKS = 128

NORM_EPS = 1e-05
CLIP = 0.002
BETA_ONE = 0.9
BETA_TWO = 0.95
ADAM_EPS = 1e-08
ADAM_RATE = 0.2
MUON_RATE = 1.0
MOMENTUM = 0.95
DECAY = 0.01
ORTHO_EPS = 1e-20
NS_ONE = 3.4445
NS_TWO = -4.775
NS_THREE = 2.0315
GELU_A = math.sqrt(2.0 / math.pi)
GELU_B = 0.044715
SCALE = HD ** (-0.5)

F32 = jnp.float32
BF16 = jnp.bfloat16
MESH = pl.DeviceIdType.MESH

ROWS_OF = (3 * D, D, 2 * FF, FF)
ORDER = (2, 0, 1, 3)
NSR = 8 * L + TOKS + NUMF + 1 + 2 + NCLASS + NUMF
OFF_SCALE = 8 * L + TOKS
OFF_FIN = OFF_SCALE + NUMF + 1
CAP = 32
PACK = CAP + CAP // 2


def mm(left, right, left_dim=1, right_dim=0):
    return lax.dot_general(
        left, right, (((left_dim,), (right_dim,)), ((), ())), preferred_element_type=F32
    )


def up_to(value, unit):
    return -(-value // unit) * unit


def split_two(value):
    high = value.astype(BF16)
    return high, (value - high.astype(F32)).astype(BF16)


def split_three(value):
    high = value.astype(BF16)
    rest = value - high.astype(F32)
    middle = rest.astype(BF16)
    return high, middle, (rest - middle.astype(F32)).astype(BF16)


def place(wide, narrow):
    w = lax.axis_index("wide")
    n = lax.axis_index("narrow")
    return w, n, w * narrow + n


def greet_all(me, count, narrow):
    barrier = pltpu.get_barrier_semaphore()

    def signal(k, carry):
        p = lax.rem(me + k, count)
        pl.semaphore_signal(
            barrier, inc=1, device_id=(p // narrow, lax.rem(p, narrow)), device_id_type=MESH
        )
        return carry

    lax.fori_loop(1, count, signal, 0)
    return barrier


def quarter_offsets(narrow):
    offsets, total = {}, 0
    for which in ORDER:
        offsets[which] = total
        total += ROWS_OF[which] // narrow
    return offsets, total


def gather_kernel(
    cat_ref, mask_ref, qkv_ref, proj_ref, in_ref, down_ref, small_ref, table_ref, pick_ref,
    out_qkv, out_proj, out_in, out_down, out_small, out_rows, out_slots, out_requests, out_stats,
    gat_one, gat_two, ask, table_s, table_low, answers, landed,
    far_send, far_recv, step_send, step_recv, ask_send, ask_recv, row_send, row_recv, table_sem,
    *, wide, narrow, chunk,
):
    count = wide * narrow
    levels = levels_of(narrow)
    w, n, me = place(wide, narrow)
    side, far = lax.rem(w, 2), w // 2
    fars = wide // 2
    table_copy = pltpu.make_async_copy(table_ref, table_s, table_sem)
    table_copy.start()
    barrier = greet_all(me, count, narrow)

    def coords(p):
        return (p // narrow, lax.rem(p, narrow))

    offsets, total = quarter_offsets(narrow)
    width = qkv_ref.shape[1]
    rows_pad = gat_one.shape[3]
    cut = gat_one.shape[4]
    shards = (qkv_ref, proj_ref, in_ref, down_ref)
    pieces = [
        jnp.concatenate([shards[which][l] for which in ORDER], 1) for l in range(L)
    ]
    if rows_pad > L * width:
        pieces.append(jnp.zeros((rows_pad - L * width, total), F32))
    packed = jnp.concatenate(pieces, 0).astype(BF16)
    gat_one[n, side, far] = packed[:, :cut]
    gat_two[n, side, far] = packed[:, cut:]
    small = small_ref[...]
    own_rows = small.shape[1]
    small_pad = out_small.shape[3]
    if small_pad > width:
        small = jnp.concatenate([small, jnp.zeros((small_pad - width, own_rows), F32)], 0)
    out_small[n, side, far] = jnp.concatenate(
        [small, jnp.zeros((small_pad, TOKS - own_rows), F32)], 1
    )

    data_rows, per_row = cat_ref.shape
    entries = data_rows * per_row
    local = table_s.shape[1]
    index_row = jnp.concatenate([cat_ref[r : r + 1, :] for r in range(data_rows)], 1)
    owner_row = jnp.zeros_like(index_row)
    for k in range(1, count):
        owner_row = owner_row + (index_row >= k * local).astype(jnp.int32)
    base_row = owner_row * local
    index_col = jnp.transpose(jnp.broadcast_to(index_row, (8, entries)))[:, :1]
    before = lax.broadcasted_iota(jnp.int32, (entries, entries), 0)
    after = lax.broadcasted_iota(jnp.int32, (entries, entries), 1)
    same = index_col == index_row
    first_col = 1.0 - jnp.max(jnp.where(same & (after < before), 1.0, 0.0), 1, keepdims=True)
    first_row = 1.0 - jnp.max(jnp.where(same & (before < after), 1.0, 0.0), 0, keepdims=True)
    lower = (index_col >= base_row) & (index_col < index_row)
    rank_row = jnp.sum(jnp.where(lower, first_col, 0.0), 0, keepdims=True).astype(jnp.int32)
    slot_row = owner_row * CAP + rank_row
    none = jnp.full((1, TOKS - per_row), -1, jnp.int32)
    for r in range(data_rows):
        out_slots[r : r + 1, :] = jnp.concatenate(
            [none, slot_row[:, r * per_row : (r + 1) * per_row]], 1
        )
    over = jnp.max(jnp.where(rank_row >= CAP, 1.0, 0.0), 1, keepdims=True)
    hidden_cells = jnp.sum(jnp.sum(mask_ref[...].astype(F32), 0, keepdims=True), 1, keepdims=True)
    place_row = index_row - base_row
    owners = lax.broadcasted_iota(jnp.int32, (count, entries), 0)
    mine = jnp.where(owners == owner_row, first_row, 0.0)
    high = lax.shift_right_logical(place_row, 6)
    low = place_row - high * 64
    at_rank = jnp.where(
        lax.broadcasted_iota(jnp.int32, (TOKS, entries), 0) == rank_row, 1.0, 0.0
    ).astype(BF16)
    wanted = 64.0 * mm((mine * high.astype(F32)).astype(BF16), at_rank, 1, 1) + mm(
        (mine * low.astype(F32)).astype(BF16), at_rank, 1, 1
    )
    lane = lax.broadcasted_iota(jnp.int32, (count, TOKS), 1)
    wanted = jnp.where(lane < CAP, wanted, 0.0)
    wanted = jnp.where(lane == CAP, over, wanted)
    wanted = jnp.where(lane == CAP + 1, hidden_cells, wanted)
    for k in range(count):
        ask[k] = wanted[k : k + 1]

    pl.semaphore_wait(barrier, count - 1)

    def over_peers(origin, size, body):
        def run(k, carry):
            body(lax.rem(origin + k, size))
            return carry

        lax.fori_loop(1, size, run, 0)

    def ask_copy(p, slot):
        return pltpu.make_async_remote_copy(
            src_ref=ask.at[p], dst_ref=out_requests.at[slot], send_sem=ask_send.at[p],
            recv_sem=ask_recv.at[slot], device_id=coords(p), device_id_type=MESH,
        )

    def row_copy(p, slot):
        return pltpu.make_async_remote_copy(
            src_ref=answers.at[p], dst_ref=landed.at[slot], send_sem=row_send.at[p],
            recv_sem=row_recv.at[slot], device_id=coords(p), device_id_type=MESH,
        )

    arrays = (gat_one, gat_two, out_small)

    def far_copies(p, slot):
        return [
            pltpu.make_async_remote_copy(
                src_ref=array.at[n, side, far], dst_ref=array.at[n, side, slot],
                send_sem=far_send.at[a, p], recv_sem=far_recv.at[a, slot],
                device_id=(p * 2 + side, n), device_id_type=MESH,
            )
            for a, array in enumerate(arrays)
        ]

    high_levels = list(range(levels - 1, 0, -1))
    plans = (
        high_levels + ["side"] + [0] * (levels > 0),
        ["side"] + high_levels + [0] * (levels > 0),
    )
    steps = len(plans[0])

    def step_copies(t):
        copies = []
        for a, array in enumerate(arrays):
            plan = plans[min(a, 1)]
            move = plan[t]
            done = plan[:t]
            lowest = min([v for v in done if v != "side"], default=levels)
            for j in range(1 << (levels - lowest)):
                block = lax.rem(n, 1 << lowest) + (j << lowest)
                if move == "side":
                    target = (w + 1 - 2 * side, n)
                else:
                    bit = lax.rem(n // (1 << move), 2)
                    target = (w, n + (1 - 2 * bit) * (1 << move))
                ref = array.at[block] if "side" in done else array.at[block, side]
                copies.append(
                    pltpu.make_async_remote_copy(
                        src_ref=ref, dst_ref=ref, send_sem=step_send.at[t, a, j],
                        recv_sem=step_recv.at[t, a, j], device_id=target, device_id_type=MESH,
                    )
                )
        return copies

    def step_arrivals(t):
        copies = []
        for a, array in enumerate(arrays):
            plan = plans[min(a, 1)]
            move = plan[t]
            done = plan[:t]
            lowest = min([v for v in done if v != "side"], default=levels)
            for j in range(1 << (levels - lowest)):
                if move == "side":
                    there, whose, target = n, 1 - side, (w + 1 - 2 * side, n)
                else:
                    bit = lax.rem(n // (1 << move), 2)
                    there, whose = n + (1 - 2 * bit) * (1 << move), side
                    target = (w, there)
                block = lax.rem(there, 1 << lowest) + (j << lowest)
                ref = array.at[block] if "side" in done else array.at[block, whose]
                copies.append(
                    pltpu.make_async_remote_copy(
                        src_ref=ref, dst_ref=ref, send_sem=step_send.at[t, a, j],
                        recv_sem=step_recv.at[t, a, j], device_id=target, device_id_type=MESH,
                    )
                )
        return copies

    def start_far(p):
        for copy in far_copies(p, far):
            copy.start()

    def end_far(p):
        for copy in far_copies(p, p):
            copy.wait_recv()

    over_peers(me, count, lambda p: ask_copy(p, me).start())
    over_peers(far, fars, start_far)
    out_requests[me] = ask[me]
    table_copy.wait()
    table_low[...] = table_s[...].astype(BF16)
    over_peers(far, fars, end_far)
    for copy in step_copies(0):
        copy.start()
    over_peers(me, count, lambda p: ask_copy(p, p).wait_recv())

    eye = lax.broadcasted_iota(jnp.int32, (CAP, TOKS), 0) == lax.broadcasted_iota(
        jnp.int32, (CAP, TOKS), 1
    )
    spots = lax.broadcasted_iota(jnp.int32, (CAP, local), 1)

    def wanted_hits(q):
        row = jnp.broadcast_to(out_requests[q], (CAP, TOKS))
        column = jnp.sum(jnp.where(eye, row, 0.0), 1, keepdims=True).astype(jnp.int32)
        return jnp.where(spots == column, 1.0, 0.0).astype(BF16)

    half_lane = lax.broadcasted_iota(jnp.int32, (CAP // 2, TOKS), 1) < D - TOKS

    def answer(c, carry):
        found = [wanted_hits(c * chunk + j) for j in range(chunk)]
        got = mm(jnp.concatenate(found, 0), table_low[...], 1, 1)
        got = jnp.concatenate([got, jnp.zeros((got.shape[0], 2 * TOKS - D), F32)], 1)
        for j in range(chunk):
            q = c * chunk + j
            part = got[j * CAP : (j + 1) * CAP]
            tail = part[:, TOKS:]
            rolled = pltpu.roll(tail[CAP // 2 :], D - TOKS, 1)
            packed = jnp.where(half_lane, tail[: CAP // 2], rolled)
            answers[q] = jnp.concatenate([part[:, :TOKS], packed], 0).astype(BF16)

            @pl.when(q != me)
            def _():
                row_copy(q, me).start()

        return carry

    def next_step(t):
        for copy in step_arrivals(t):
            copy.wait_recv()
        if t + 1 < steps:
            for copy in step_copies(t + 1):
                copy.start()

    lax.fori_loop(0, count // chunk // 2, answer, 0)
    next_step(0)
    lax.fori_loop(count // chunk // 2, count // chunk, answer, 0)
    landed[me] = answers[me]
    for t in range(1, steps):
        next_step(t)

    outs = (out_qkv, out_proj, out_in, out_down)
    for q in range(narrow):
        held = jnp.concatenate(
            [
                gat_one[q].reshape(wide * rows_pad, cut),
                gat_two[q].reshape(wide * rows_pad, total - cut),
            ],
            1,
        )
        for l in range(L):
            matrix = mm(held, pick_ref[l], 0, 0).astype(BF16)
            for which in ORDER:
                size = ROWS_OF[which] // narrow
                outs[which][l, q * size : (q + 1) * size] = matrix[
                    offsets[which] : offsets[which] + size
                ]

    requests = out_requests[...]
    reached = jnp.max(requests, 0)
    summed = jnp.sum(requests, 0)
    lane = lax.broadcasted_iota(jnp.int32, (1, TOKS), 1)
    out_stats[...] = jnp.where(lane == CAP, reached, summed)

    over_peers(me, count, lambda p: row_copy(p, p).wait_recv())
    out_rows[...] = spread_slots(landed[...].astype(F32)).astype(BF16)

    def drain_far(p):
        for copy in far_copies(p, far):
            copy.wait_send()

    over_peers(far, fars, drain_far)
    for t in range(steps):
        for copy in step_copies(t):
            copy.wait_send()
    over_peers(me, count, lambda p: ask_copy(p, me).wait_send())
    over_peers(me, count, lambda p: row_copy(p, me).wait_send())


def levels_of(size):
    return size.bit_length() - 1


def spread_slots(packed):
    owners = packed.shape[0]
    head = packed[:, :CAP].reshape(owners * CAP, TOKS)
    tail = packed[:, CAP:].reshape(owners * (CAP // 2), TOKS)
    moved = pltpu.roll(tail, D - TOKS, 1).reshape(owners, CAP // 2, TOKS)
    tail = jnp.concatenate([tail.reshape(owners, CAP // 2, TOKS), moved], 1)
    return jnp.concatenate([head, tail.reshape(owners * CAP, TOKS)[:, : D - TOKS]], 1)


def gather_call(cat_index, cell_mask, shards_t, small_t, table_t, wide, narrow):
    count = wide * narrow
    levels = levels_of(narrow)
    width = small_t.shape[0]
    rows_pad = up_to(L * width, 16)
    small_pad = up_to(width, 8)
    _, total = quarter_offsets(narrow)
    cut = up_to(total // 2, TOKS)
    pick = np.zeros((L, wide * rows_pad, D), np.float32)
    for l in range(L):
        for block in range(wide):
            at = (block % 2) * (wide // 2) + block // 2
            for c in range(width):
                pick[l, at * rows_pad + l * width + c, block * width + c] = 1.0
    local = table_t.shape[1]
    shape = jax.ShapeDtypeStruct
    outs = [shape((L, rows, D), BF16) for rows in ROWS_OF] + [
        shape((narrow, 2, wide // 2, small_pad, TOKS), F32),
        shape((count * CAP, D), BF16),
        shape((cat_index.shape[0], TOKS), jnp.int32),
        shape((count, 1, TOKS), F32),
        shape((1, TOKS), F32),
    ]
    vmem = pl.BlockSpec(memory_space=pltpu.VMEM)
    vm = pltpu.VMEM
    dma = pltpu.SemaphoreType.DMA
    return pl.pallas_call(
        functools.partial(gather_kernel, wide=wide, narrow=narrow, chunk=8),
        out_shape=outs,
        in_specs=[vmem] * 7 + [pl.BlockSpec(memory_space=pl.ANY), vmem],
        out_specs=[vmem] * len(outs),
        scratch_shapes=[
            vm((narrow, 2, wide // 2, rows_pad, cut), BF16),
            vm((narrow, 2, wide // 2, rows_pad, total - cut), BF16),
            vm((count, 1, TOKS), F32),
            vm((D, local), F32),
            vm((D, local), BF16),
            vm((count, PACK, TOKS), BF16),
            vm((count, PACK, TOKS), BF16),
            dma((3, wide // 2)), dma((3, wide // 2)),
            dma((levels + 1, 3, narrow)), dma((levels + 1, 3, narrow)),
            dma((count,)), dma((count,)), dma((count,)), dma((count,)), dma(()),
        ],
        compiler_params=pltpu.CompilerParams(
            collective_id=0, has_side_effects=True, vmem_limit_bytes=62 << 20
        ),
        name="gather",
    )(cat_index, cell_mask, *shards_t, small_t, table_t, jnp.asarray(pick, BF16))


def lanes(vector, width):
    return jnp.concatenate([vector] * (width // vector.shape[1]), 1)


def fold(value):
    total = value[:, :TOKS]
    for start in range(TOKS, value.shape[1], TOKS):
        total = total + value[:, start : start + TOKS]
    return total


def norm_forward(value, gain, shift):
    center = value - jnp.sum(value, 0, keepdims=True) * (1.0 / D)
    spread = jnp.sum(center * center, 0, keepdims=True) * (1.0 / D)
    inverse = lax.rsqrt(spread + NORM_EPS)
    unit = center * inverse
    return unit, inverse, unit * gain + shift


def norm_backward(unit, inverse, grad_unit):
    mean_one = jnp.sum(grad_unit, 0, keepdims=True) * (1.0 / D)
    mean_two = jnp.sum(grad_unit * unit, 0, keepdims=True) * (1.0 / D)
    return inverse * (grad_unit - mean_one - unit * mean_two)


NVEC = 8 * L + 3
ROOM = TOKS // CATF


def model_kernel(
    stats_ref, labels_ref, rows_ref, slots_ref, num_ref, mask_ref,
    qkv_ref, proj_ref, in_ref, down_ref, small_ref,
    loss_ref, dmats_ref, dsmall_ref, dslots_ref,
    rows_t, qkv_t, proj_t, in_t, down_t, tok_s, scale_s, rec_s, class_s, class_t_s,
    dtok_s, dscale_s, drec_s, dclass_s, slots_acc,
    vecb, probs_s, unit_one_s, inv_one_s, normed_s, k_s, v_s, mixed_s,
    unit_two_s, inv_two_s, normed_two_s, gate_s, hidden_s, acc_s, looked_s, wide_s, low_s, ds_s, qlow_s,
    qkv_acc, proj_acc, in_acc, down_acc, num_s, mask_s, coef_s,
    *, pair, wide, narrow,
):
    width = pair * TOKS
    blocks = slots_ref.shape[0] // pair
    columns = D // wide
    own_rows = NSR // narrow
    slots = rows_ref.shape[0]
    offsets, _ = packed_offsets(narrow)
    mats_acc = (qkv_acc, proj_acc, in_acc, down_acc)
    inv_count = 1.0 / jnp.full((1, 1), stats_ref[0, CAP + 1], F32)
    data_rows = slots_ref.shape[0]
    gap = jnp.zeros((data_rows, 1), F32)
    gap_tail = jnp.zeros((data_rows, TOKS - 1 - NUMF), F32)
    masked = mask_ref[...].astype(F32)
    num_s[...] = jnp.concatenate([gap, num_ref[...], gap_tail], 1)
    mask_s[...] = jnp.concatenate([gap, masked, gap_tail], 1)
    coef_s[...] = jnp.concatenate([gap, (1.0 - masked) * num_ref[...], gap_tail], 1)

    rows_t[...] = jnp.transpose(rows_ref[...].astype(F32)).astype(BF16)
    for l in range(L):
        qkv_t[l] = jnp.transpose(qkv_ref[l].astype(F32)).astype(BF16)
        proj_t[l] = jnp.transpose(proj_ref[l].astype(F32)).astype(BF16)
        in_t[l] = jnp.transpose(in_ref[l].astype(F32)).astype(BF16)
        down_t[l] = jnp.transpose(down_ref[l].astype(F32)).astype(BF16)
    pieces = []
    for n in range(narrow):
        piece = jnp.concatenate([small_ref[n, w % 2, w // 2, :columns] for w in range(wide)], 0)
        pieces.append(piece[:, :own_rows])
    small = jnp.concatenate(pieces, 1)
    for i in range(NVEC):
        at = i if i < 8 * L else (OFF_FIN + i - 8 * L if i < 8 * L + 2 else OFF_SCALE + NUMF)
        vecb[i] = jnp.broadcast_to(small[:, at : at + 1], (D, TOKS))
    gap_one = jnp.zeros((D, 1), F32)
    gap_end = jnp.zeros((D, TOKS - 1 - NUMF), F32)
    tok_s[...] = small[:, 8 * L : OFF_SCALE]
    scale_s[...] = jnp.concatenate([gap_one, small[:, OFF_SCALE : OFF_SCALE + NUMF], gap_end], 1)
    rec_s[...] = jnp.concatenate([gap_one, small[:, OFF_FIN + 2 + NCLASS :], gap_end], 1)
    class_t = jnp.concatenate(
        [small[:, OFF_FIN + 2 : OFF_FIN + 2 + NCLASS], jnp.zeros((D, TOKS - NCLASS), F32)], 1
    )
    class_s[...] = jnp.transpose(class_t)[:16].astype(BF16)
    class_t_s[...] = jnp.concatenate([class_t[:, :16]] * 3, 1).astype(BF16)
    for ref in (loss_ref, *mats_acc, dtok_s, dscale_s, drec_s, dclass_s, acc_s):
        ref[...] = jnp.zeros_like(ref)

    def vec(i):
        return lanes(vecb[i], width)

    def head_rows(value, h, b):
        return value[h * HD : h * HD + HD, b * TOKS : b * TOKS + TOKS]

    def two_heads(left, right):
        both = mm(left, right)
        return [both[:HD, :TOKS], both[HD:, TOKS:]]

    def apart(value):
        row = lax.broadcasted_iota(jnp.int32, value.shape, 0)
        upper = jnp.where(row < HD, 1.0, 0.0).astype(BF16)
        lower = jnp.where(row >= HD, 1.0, 0.0).astype(BF16)
        return jnp.concatenate([value * upper, value * lower], 1)

    def add_mats(l, which, value):
        mats_acc[which][l] += value

    def add_vec(i, value):
        acc_s[i] += fold(value)

    def forward(l, x):
        base = 8 * l
        unit, inverse, normed = norm_forward(x, vec(base), vec(base + 1))
        normed = normed.astype(BF16)
        unit_one_s[l] = unit
        inv_one_s[l] = inverse
        normed_s[l] = normed
        joined = mm(qkv_ref[l], normed)
        q_f = joined[:D] + vec(base + 4)
        k_f = joined[D : 2 * D]
        v_f = joined[2 * D :] + vec(base + 5)
        q_low = q_f.astype(BF16)
        qlow_s[l] = q_low
        mixed_cols = []
        for b in range(pair):
            for h in range(HEADS // 2):
                rows = slice(2 * h * HD, 2 * (h + 1) * HD)
                cols = slice(b * TOKS, (b + 1) * TOKS)
                k_s[l, b * HEADS // 2 + h] = k_f[rows, cols].astype(BF16)
                v_s[l, b * HEADS // 2 + h] = v_f[rows, cols].astype(BF16)
        for b in range(pair):
            span = slice(b * TOKS, (b + 1) * TOKS)
            for h in range(HEADS // 2):
                rows = slice(2 * h * HD, 2 * (h + 1) * HD)
                wide_s[b, :, 2 * h * TOKS : 2 * (h + 1) * TOKS] = mm(
                    k_s[l, b * HEADS // 2 + h], apart(q_low[rows, span]), 0, 0
                )
        for b in range(pair):
            for h in range(HEADS):
                u = b * HEADS + h
                scores = wide_s[b, :, h * TOKS : (h + 1) * TOKS]
                top = jnp.max(scores, 0, keepdims=True)
                weight = jnp.exp2((scores - top) * (SCALE * math.log2(math.e)))
                probs = weight * (1.0 / jnp.sum(weight, 0, keepdims=True))
                probs_s[l, u] = probs
                low_s[l, b, :, h * TOKS : (h + 1) * TOKS] = probs.astype(BF16)
        for b in range(pair):
            rows = []
            for h in range(HEADS // 2):
                u = b * HEADS // 2 + h
                rows += two_heads(v_s[l, u], low_s[l, b, :, 2 * h * TOKS : 2 * (h + 1) * TOKS])
            mixed_cols.append(jnp.concatenate(rows, 0))
        mixed = jnp.concatenate(mixed_cols, 1).astype(BF16)
        mixed_s[l] = mixed
        after = x + mm(proj_ref[l], mixed) + vec(base + 6)
        unit, inverse, normed = norm_forward(after, vec(base + 2), vec(base + 3))
        normed = normed.astype(BF16)
        unit_two_s[l] = unit
        inv_two_s[l] = inverse
        normed_two_s[l] = normed
        gate_up = mm(in_ref[l], normed)
        gate_s[l] = gate_up
        gate, up = gate_up[:FF], gate_up[FF:]
        inner = GELU_A * (gate + GELU_B * gate * gate * gate)
        hidden = (0.5 * gate * (1.0 + jnp.tanh(inner)) * up).astype(BF16)
        hidden_s[l] = hidden
        return after + mm(down_t[l], hidden) + vec(base + 7)

    def backward(l, dout):
        base = 8 * l
        add_vec(base + 7, dout)
        up_low = dout.astype(BF16)
        add_mats(l, 3, mm(hidden_s[l], up_low, 1, 1))
        dhidden = mm(down_ref[l], up_low)
        gate, up = gate_s[l, :FF], gate_s[l, FF:]
        square = gate * gate
        tanh = jnp.tanh(GELU_A * (gate + GELU_B * square * gate))
        half = 0.5 * (1.0 + tanh)
        slope = half + 0.5 * gate * (1.0 - tanh * tanh) * (GELU_A * (1.0 + 3.0 * GELU_B * square))
        dgate = dhidden * up * slope
        dup = dhidden * (gate * half)
        dgl = jnp.concatenate([dgate, dup], 0).astype(BF16)
        add_mats(l, 2, mm(dgl, normed_two_s[l], 1, 1))
        dnormed = mm(in_t[l], dgl)
        unit = unit_two_s[l]
        add_vec(base + 2, dnormed * unit)
        add_vec(base + 3, dnormed)
        dafter = dout + norm_backward(unit, inv_two_s[l], dnormed * vec(base + 2))
        add_vec(base + 6, dafter)
        after_low = dafter.astype(BF16)
        add_mats(l, 1, mm(after_low, mixed_s[l], 1, 1))
        dmixed = mm(proj_t[l], after_low)
        dmixed_low = dmixed.astype(BF16)
        q_cols, k_cols, v_cols = [], [], []
        for b in range(pair):
            span = slice(b * TOKS, (b + 1) * TOKS)
            for h in range(HEADS // 2):
                rows = slice(2 * h * HD, 2 * (h + 1) * HD)
                wide_s[b, :, 2 * h * TOKS : 2 * (h + 1) * TOKS] = mm(
                    v_s[l, b * HEADS // 2 + h], apart(dmixed_low[rows, span]), 0, 0
                )
        for b in range(pair):
            for h in range(HEADS):
                u = b * HEADS + h
                probs = probs_s[l, u]
                dprobs = wide_s[b, :, h * TOKS : (h + 1) * TOKS]
                inner = jnp.sum(dprobs * probs, 0, keepdims=True)
                ds_s[b, :, h * TOKS : (h + 1) * TOKS] = (probs * (dprobs - inner) * SCALE).astype(BF16)
        for b in range(pair):
            q_rows = []
            for h in range(HEADS // 2):
                u = b * HEADS // 2 + h
                q_rows += two_heads(k_s[l, u], ds_s[b, :, 2 * h * TOKS : 2 * (h + 1) * TOKS])
            q_cols.append(jnp.concatenate(q_rows, 0))
            span = slice(b * TOKS, (b + 1) * TOKS)
            v_rows, k_rows = [], []
            for h in range(HEADS // 2):
                rows = slice(2 * h * HD, 2 * (h + 1) * HD)
                both = slice(2 * h * TOKS, 2 * (h + 1) * TOKS)
                v_rows.append(mm(apart(dmixed_low[rows, span]), low_s[l, b, :, both], 1, 1))
                k_rows.append(mm(apart(qlow_s[l, rows, span]), ds_s[b, :, both], 1, 1))
            v_cols.append(jnp.concatenate(v_rows, 0))
            k_cols.append(jnp.concatenate(k_rows, 0))
        dq = jnp.concatenate(q_cols, 1)
        dk = jnp.concatenate(k_cols, 1)
        dv = jnp.concatenate(v_cols, 1)
        add_vec(base + 4, dq)
        add_vec(base + 5, dv)
        dj = jnp.concatenate([dq, dk, dv], 0).astype(BF16)
        add_mats(l, 0, mm(dj, normed_s[l], 1, 1))
        dnormed = mm(qkv_t[l], dj)
        unit = unit_one_s[l]
        add_vec(base, dnormed * unit)
        add_vec(base + 1, dnormed)
        return dafter + norm_backward(unit, inv_one_s[l], dnormed * vec(base))

    def step(i, carry):
        def row_of(ref):
            return jnp.concatenate([ref[pl.ds(i * pair + b, 1), :] for b in range(pair)], 1)

        coef = row_of(coef_s)
        num = row_of(num_s)
        mask = row_of(mask_s)
        lane = lax.broadcasted_iota(jnp.int32, (D, TOKS), 1)
        placed = []
        for b in range(pair):
            found = looked_s[i, :, (b // ROOM) * TOKS : (b // ROOM + 1) * TOKS]
            shift = (TOKS - CATF - b * CATF) % TOKS
            moved = pltpu.roll(found, shift, 1) if shift else found
            placed.append(jnp.where(lane < TOKS - CATF, 0.0, moved))
        x = jnp.concatenate(placed, 1) + lanes(tok_s[...], width)
        x = x + coef * lanes(scale_s[...], width) + mask * vec(8 * L + 2)
        for l in range(L):
            x = forward(l, x)
        unit, inverse, final = norm_forward(x, vec(8 * L), vec(8 * L + 1))
        rec = lanes(rec_s[...], width)
        error = jnp.sum(final * rec, 0, keepdims=True) - num
        final_low = final.astype(BF16)
        logits = mm(class_s[...], final_low)
        row = lax.broadcasted_iota(jnp.int32, logits.shape, 0)
        lane = lax.broadcasted_iota(jnp.int32, logits.shape, 1)
        live = row < NCLASS
        logits = jnp.where(live, logits, -1e30)
        top = jnp.max(logits, 0, keepdims=True)
        weight = jnp.where(live, jnp.exp(logits - top), 0.0)
        sums = jnp.sum(weight, 0, keepdims=True)
        first = (lane % TOKS) == 0
        label = jnp.concatenate(
            [jnp.full((1, TOKS), labels_ref[i * pair + b], jnp.int32) for b in range(pair)], 1
        )
        hit = jnp.where(first & (row == label), 1.0, 0.0)
        firsts = jnp.where(first[:1], 1.0, 0.0)
        picked = jnp.sum(jnp.where(hit > 0, logits, 0.0), 0, keepdims=True)
        loss_ref[...] += fold(mask * error * error + firsts * (top + jnp.log(sums)) - picked)
        dlogits = (firsts * weight / sums - hit) * inv_count
        dpredict = (2.0 * inv_count) * mask * error
        parts = jnp.concatenate([p.astype(F32) for p in split_three(dlogits)], 0).astype(BF16)
        dclass_s[...] += mm(final_low, parts, 1, 1)
        drec_s[...] += fold(final * dpredict)
        dfinal = rec * dpredict + mm(class_t_s[...], parts)
        add_vec(8 * L, dfinal * unit)
        add_vec(8 * L + 1, dfinal)
        dx = norm_backward(unit, inverse, dfinal * vec(8 * L))
        for l in reversed(range(L)):
            dx = backward(l, dx)
        dtok_s[...] += fold(dx)
        dscale_s[...] += fold(coef * dx)
        acc_s[8 * L + 2] += fold(mask * dx)
        packed = [jnp.zeros((D, TOKS), F32) for _ in range(groups)]
        group = lax.broadcasted_iota(jnp.int32, (D, TOKS), 1) // CATF
        for b in range(pair):
            part = dx[:, b * TOKS : (b + 1) * TOKS]
            shift = (b * CATF + CATF) % TOKS
            if shift:
                part = pltpu.roll(part, shift, 1)
            packed[b // ROOM] = jnp.where(group == b % ROOM, part, packed[b // ROOM])
        for at in range(groups):
            looked_s[i, :, at * TOKS : (at + 1) * TOKS] = packed[at]
        return carry

    groups = -(-pair // ROOM)
    spare = groups * TOKS - pair * CATF

    def hits_of(i):
        pieces = [
            slots_ref[i * pair + b : i * pair + b + 1, TOKS - CATF :] for b in range(pair)
        ]
        if spare:
            pieces.append(jnp.full((1, spare), -1, jnp.int32))
        slot = lax.broadcasted_iota(jnp.int32, (slots, groups * TOKS), 0)
        return jnp.where(slot == jnp.concatenate(pieces, 1), 1.0, 0.0).astype(BF16)

    for i in range(blocks):
        looked_s[i] = mm(rows_t[...], hits_of(i))
    lax.fori_loop(0, blocks, step, 0)
    slots_acc[...] = jnp.zeros_like(slots_acc)
    for i in range(blocks):
        slots_acc[...] += mm(hits_of(i), looked_s[i].astype(BF16), 1, 1)

    dvec = [jnp.sum(acc_s[i], 1, keepdims=True) for i in range(NVEC)]
    dclass = dclass_s[...]
    dclass = dclass[:, :16] + dclass[:, 16:32] + dclass[:, 32:]
    dsmall = jnp.concatenate(
        dvec[: 8 * L]
        + [dtok_s[...], dscale_s[:, 1 : 1 + NUMF], dvec[8 * L + 2]]
        + dvec[8 * L : 8 * L + 2]
        + [dclass[:, :NCLASS], drec_s[:, 1 : 1 + NUMF]],
        1,
    )
    blank = jnp.zeros((D, TOKS - own_rows), F32)
    for n in range(narrow):
        piece = jnp.concatenate([dsmall[:, n * own_rows : (n + 1) * own_rows], blank], 1)
        if dsmall_ref.shape[2] == columns:
            dsmall_ref[n] = piece.reshape(wide, columns, TOKS)
        else:
            dsmall_ref[n] = jnp.zeros(dsmall_ref.shape[1:], F32)
            for w in range(wide):
                dsmall_ref[n, w, :columns] = piece[w * columns : (w + 1) * columns]

    def beside(tail):
        rows = tail.shape[0]
        tail = jnp.concatenate([tail, jnp.zeros((rows, 2 * TOKS - D), F32)], 1)
        lane = lax.broadcasted_iota(jnp.int32, (rows // 2, TOKS), 1)
        return jnp.where(
            lane < D - TOKS, tail[: rows // 2], pltpu.roll(tail[rows // 2 :], D - TOKS, 1)
        )

    for which in range(4):
        size = ROWS_OF[which] // narrow
        for l in range(L):
            for n in range(narrow):
                part = mats_acc[which][l, n * size : (n + 1) * size]
                at = offsets[which]
                dmats_ref[l, n, at : at + size] = part[:, :TOKS]
                dmats_ref[l, n, at + size : at + size + size // 2] = beside(part[:, TOKS:])

    terms = slots_acc[...]
    dslots_ref[:, :CAP] = terms[:, :TOKS].reshape(slots // CAP, CAP, TOKS).astype(BF16)
    tail = jnp.concatenate([terms[:, TOKS:], jnp.zeros((slots, 2 * TOKS - D), F32)], 1)
    tail = tail.reshape(slots // CAP, CAP, TOKS)
    low = tail[:, : CAP // 2].reshape(slots // 2, TOKS)
    high = pltpu.roll(tail[:, CAP // 2 :].reshape(slots // 2, TOKS), D - TOKS, 1)
    lane = lax.broadcasted_iota(jnp.int32, (slots // 2, TOKS), 1)
    dslots_ref[:, CAP:] = (
        jnp.where(lane < D - TOKS, low, high).reshape(slots // CAP, CAP // 2, TOKS).astype(BF16)
    )


def model_call(stats, labels, rows, slots, num, mask, mats, small, pair, wide, narrow):
    width = pair * TOKS
    used = rows.shape[0]
    _, total = packed_offsets(narrow)
    shape = jax.ShapeDtypeStruct
    outs = [
        shape((1, TOKS), F32),
        shape((L, narrow, total, TOKS), F32),
        shape((narrow, wide, small.shape[3], TOKS), F32),
        shape((used // CAP, PACK, TOKS), BF16),
    ]
    units = pair * HEADS
    vm = pltpu.VMEM
    scratch = [
        vm((D, used), BF16),
        vm((L, D, 3 * D), BF16), vm((L, D, D), BF16), vm((L, D, 2 * FF), BF16), vm((L, D, FF), BF16),
        vm((D, TOKS), F32), vm((D, TOKS), F32), vm((D, TOKS), F32), vm((16, D), BF16), vm((D, 48), BF16),
        vm((D, TOKS), F32), vm((D, TOKS), F32), vm((D, TOKS), F32), vm((D, 48), F32), vm((used, D), F32),
        vm((NVEC, D, TOKS), F32), vm((L, units, TOKS, TOKS), F32),
        vm((L, D, width), F32), vm((L, 1, width), F32), vm((L, D, width), BF16),
        vm((L, units // 2, 2 * HD, TOKS), BF16), vm((L, units // 2, 2 * HD, TOKS), BF16),
        vm((L, D, width), BF16),
        vm((L, D, width), F32), vm((L, 1, width), F32), vm((L, D, width), BF16),
        vm((L, 2 * FF, width), F32), vm((L, FF, width), BF16),
        vm((NVEC, D, TOKS), F32), vm((slots.shape[0] // pair, D, -(-pair // ROOM) * TOKS), F32), vm((pair, TOKS, HEADS * TOKS), F32), vm((L, pair, TOKS, HEADS * TOKS), BF16), vm((pair, TOKS, HEADS * TOKS), BF16), vm((L, D, width), BF16),
        *[vm((L, rows, D), F32) for rows in ROWS_OF],
        *[vm((slots.shape[0], TOKS), F32)] * 3,
    ]
    spec = pl.BlockSpec(memory_space=pltpu.VMEM)
    return pl.pallas_call(
        functools.partial(model_kernel, pair=pair, wide=wide, narrow=narrow),
        out_shape=outs,
        in_specs=[pl.BlockSpec(memory_space=pltpu.SMEM)] * 2 + [spec] * 9,
        out_specs=[spec] * len(outs),
        scratch_shapes=scratch,
        compiler_params=pltpu.CompilerParams(vmem_limit_bytes=62 << 20),
        name="model",
    )(stats, labels, rows, slots, num, mask, *mats, small)


def packed_rows(which, narrow):
    size = ROWS_OF[which] // narrow
    return size + size // 2


def packed_offsets(narrow):
    offsets, total = [], 0
    for which in range(4):
        offsets.append(total)
        total += packed_rows(which, narrow)
    return offsets, total


def worker_of(m, wide):
    layer, kind = m // 4, m % 4
    return (layer * 2 + kind % 2) * (wide // 8) * 2 + kind // 2


def adam_step(weight, gradient, first, second):
    first = BETA_ONE * first + (1.0 - BETA_ONE) * gradient
    second = BETA_TWO * second + (1.0 - BETA_TWO) * gradient * gradient
    ratio = first / (1.0 - BETA_ONE**STEP) / (jnp.sqrt(second / (1.0 - BETA_TWO**STEP)) + ADAM_EPS)
    return (weight - ADAM_RATE * (ratio + DECAY * weight), first, second)


def exact(left, right, left_dim=1, right_dim=0):
    return lax.dot_general(
        left, right, (((left_dim,), (right_dim,)), ((), ())), preferred_element_type=F32,
        precision=lax.Precision.HIGHEST,
    )


def finish_kernel(*refs, wide, narrow):
    refs = list(refs)

    def take(number):
        head = refs[:number]
        del refs[:number]
        return head

    levels = levels_of(narrow)
    count = wide * narrow
    columns = D // wide
    mats_any, dsmall_ref, dslots_ref, requests_ref, loss_ref, extra_any = take(6)
    moments = take(4)
    out_stats, table_any, out_small = take(3)
    x_came, out_moments = take(4), take(4)
    steps = levels + 1
    mats_held = [take(steps) for _ in range(L)]
    mats_came = [take(steps) for _ in range(L)]
    small_held, small_came = take(levels), take(levels)
    landed, hits, mats_landed, small_landed, grad_s = take(5)
    dmats_ref, out_table = take(2)
    norm_near, norm_all = take(2)
    mom_came, mom_sent, x_sent = take(4), take(4), take(4)
    x_start, x_end, square_s, gram_held, gram_came = take(5)
    (
        slot_send, slot_recv, mats_send, mats_recv, small_send, small_recv,
        block_send, block_recv, own_send, own_recv,
        near_send, near_recv, norm_send, norm_recv, get_send, get_recv, put_send, put_recv, new_send, new_recv,
        gram_send, gram_recv, mats_sem, extra_sem, table_sem,
    ) = refs
    mats_copy = pltpu.make_async_copy(mats_any, dmats_ref, mats_sem)
    extra_copy = pltpu.make_async_copy(extra_any, out_table, extra_sem)
    table_copy = pltpu.make_async_copy(out_table, table_any, table_sem)
    mats_copy.start()
    extra_copy.start()
    w, n, me = place(wide, narrow)
    barrier = greet_all(me, count, narrow)
    offsets, total = packed_offsets(narrow)
    half_rows = total // 2
    local = extra_any.shape[1]
    side = lax.rem(w, 2)

    def over_peers(origin, size, body):
        def run(k, carry):
            body(lax.rem(origin + k, size))
            return carry

        lax.fori_loop(1, size, run, 0)

    def coords(p):
        return (p // narrow, lax.rem(p, narrow))

    def narrow_partner(s):
        bit = lax.rem(n // (1 << s), 2)
        return bit, n + (1 - 2 * bit) * (1 << s)

    def plan(l):
        if l % 2:
            return list(range(levels)) + ["side"]
        return [0, "side"] + list(range(1, levels)) if levels else ["side"]

    def before(l, t):
        return dmats_ref.at[l] if t == 0 else mats_held[l][t - 1]

    def step_copies(l, t):
        move = plan(l)[t]
        source = before(l, t)
        copies = []
        if move == "side":
            for j in range(source.shape[0]):
                copies.append(
                    pltpu.make_async_remote_copy(
                        src_ref=source.at[j, pl.ds((1 - side) * half_rows, half_rows)],
                        dst_ref=mats_came[l][t].at[j],
                        send_sem=mats_send.at[l, t, j], recv_sem=mats_recv.at[l, t, j],
                        device_id=(w + 1 - 2 * side, n), device_id_type=MESH,
                    )
                )
        else:
            bit, partner = narrow_partner(move)
            for j in range(source.shape[0] // 2):
                copies.append(
                    pltpu.make_async_remote_copy(
                        src_ref=source.at[2 * j + 1 - bit], dst_ref=mats_came[l][t].at[j],
                        send_sem=mats_send.at[l, t, j], recv_sem=mats_recv.at[l, t, j],
                        device_id=(w, partner), device_id_type=MESH,
                    )
                )
        return copies

    def step_add(l, t):
        move = plan(l)[t]
        source = before(l, t)
        for j in range(mats_held[l][t].shape[0]):
            if move == "side":
                mine = source[j, pl.ds(side * half_rows, half_rows)]
            else:
                mine = source[2 * j + narrow_partner(move)[0]]
            mats_held[l][t][j] = mine + mats_came[l][t][j]

    def small_before(s):
        return dsmall_ref if s == 0 else small_held[s - 1]

    def small_copies(s):
        bit, partner = narrow_partner(s)
        return [
            pltpu.make_async_remote_copy(
                src_ref=small_before(s).at[2 * j + 1 - bit], dst_ref=small_came[s].at[j],
                send_sem=small_send.at[s, j], recv_sem=small_recv.at[s, j],
                device_id=(w, partner), device_id_type=MESH,
            )
            for j in range(narrow >> (s + 1))
        ]

    def small_add(s):
        bit, _ = narrow_partner(s)
        for j in range(narrow >> (s + 1)):
            small_held[s][j] = small_before(s)[2 * j + bit] + small_came[s][j]

    def slot_copy(p, slot):
        return pltpu.make_async_remote_copy(
            src_ref=dslots_ref.at[p], dst_ref=landed.at[slot], send_sem=slot_send.at[p],
            recv_sem=slot_recv.at[slot], device_id=coords(p), device_id_type=MESH,
        )

    def block_copy(m, slot):
        layer, kind = m // 4, m % 4
        start = offsets[kind] - half_rows * (kind // 2)
        size = packed_rows(kind, narrow)
        return pltpu.make_async_remote_copy(
            src_ref=mats_held[layer][steps - 1].at[0, pl.ds(start, size)],
            dst_ref=mats_landed.at[slot, pl.ds(0, size)],
            send_sem=block_send.at[m], recv_sem=block_recv.at[slot],
            device_id=(worker_of(m, wide), n), device_id_type=MESH,
        )

    def own_copy(p, slot):
        return pltpu.make_async_remote_copy(
            src_ref=small_held[levels - 1].at[0, p], dst_ref=small_landed.at[slot],
            send_sem=own_send.at[p], recv_sem=own_recv.at[slot], device_id=(p, n),
            device_id_type=MESH,
        )

    def near_copy(p, slot):
        return pltpu.make_async_remote_copy(
            src_ref=norm_near.at[n], dst_ref=norm_near.at[slot], send_sem=near_send.at[p],
            recv_sem=near_recv.at[slot], device_id=(w, p), device_id_type=MESH,
        )

    def norm_copy(p, slot):
        return pltpu.make_async_remote_copy(
            src_ref=norm_all.at[w], dst_ref=norm_all.at[slot], send_sem=norm_send.at[p],
            recv_sem=norm_recv.at[slot], device_id=(p, n), device_id_type=MESH,
        )

    def get_copy(m, slot):
        return pltpu.make_async_remote_copy(
            src_ref=moments[m % 4].at[m // 4], dst_ref=mom_came[m % 4].at[slot],
            send_sem=get_send.at[m], recv_sem=get_recv.at[slot],
            device_id=(worker_of(m, wide), n), device_id_type=MESH,
        )

    def put_copy(m, p):
        return pltpu.make_async_remote_copy(
            src_ref=mom_sent[m % 4].at[p], dst_ref=out_moments[m % 4].at[m // 4],
            send_sem=put_send.at[p], recv_sem=put_recv.at[m], device_id=(p, n),
            device_id_type=MESH,
        )

    def new_copy(m, p):
        return pltpu.make_async_remote_copy(
            src_ref=x_sent[m % 4].at[p], dst_ref=x_came[m % 4].at[m // 4],
            send_sem=new_send.at[p], recv_sem=new_recv.at[m], device_id=(p, n),
            device_id_type=MESH,
        )

    def gram_copy(s):
        _, partner = narrow_partner(s)
        return pltpu.make_async_remote_copy(
            src_ref=gram_held.at[s], dst_ref=gram_came.at[s], send_sem=gram_send.at[s],
            recv_sem=gram_recv.at[s], device_id=(w, partner), device_id_type=MESH,
        )

    pl.semaphore_wait(barrier, count - 1)
    mats_copy.wait()
    for l in range(L):
        for copy in step_copies(l, 0):
            copy.start()
    for copy in small_copies(0):
        copy.start()
    over_peers(me, count, lambda p: slot_copy(p, me).start())
    landed[me] = dslots_ref[me]
    for m in range(4 * L):
        @pl.when(w != worker_of(m, wide))
        def _():
            get_copy(m, w).start()

        @pl.when(w == worker_of(m, wide))
        def _():
            mom_came[m % 4][w] = moments[m % 4][m // 4]

    eye = lax.broadcasted_iota(jnp.int32, (CAP, TOKS), 0) == lax.broadcasted_iota(
        jnp.int32, (CAP, TOKS), 1
    )
    spots = lax.broadcasted_iota(jnp.int32, (CAP, local), 1)

    def find(c, carry):
        for j in range(8):
            q = c * 8 + j
            row = jnp.broadcast_to(requests_ref[q], (CAP, TOKS))
            column = jnp.sum(jnp.where(eye, row, 0.0), 1, keepdims=True).astype(jnp.int32)
            at = pl.multiple_of(q * CAP, CAP)
            hits[pl.ds(at, CAP), :] = jnp.where(spots == column, 1.0, 0.0).astype(BF16)
        return carry

    lax.fori_loop(0, count // 8, find, 0)

    def finish_step(t):
        for l in range(L):
            for copy in step_copies(l, t):
                copy.wait_recv()
            step_add(l, t)
        if t < levels:
            for copy in small_copies(t):
                copy.wait_recv()
            small_add(t)
        if t + 1 < steps:
            for l in range(L):
                for copy in step_copies(l, t + 1):
                    copy.start()
        if t + 1 < levels:
            for copy in small_copies(t + 1):
                copy.start()

    finish_step(0)

    over_peers(me, count, lambda p: slot_copy(p, p).wait_recv())
    terms_t = jnp.transpose(spread_slots(landed[...].astype(F32)))
    if steps > 2:
        finish_step(1)
    extra_copy.wait()
    out_table[...] += mm(terms_t.astype(BF16), hits[...])
    table_copy.start()
    for t in range(2 if steps > 2 else 1, steps):
        finish_step(t)

    over_peers(w, wide, lambda p: own_copy(p, w).start())
    for m in range(4 * L):
        kind = m % 4

        @pl.when((side == kind // 2) & (w != worker_of(m, wide)))
        def _():
            block_copy(m, w).start()

    table_grad = out_table[...]

    def total_of(value):
        return jnp.sum(jnp.sum(value, 0, keepdims=True), 1, keepdims=True)

    squares = total_of(table_grad * table_grad)
    loss_here = jnp.sum(loss_ref[...], 1, keepdims=True)
    x_start[...] = jnp.zeros_like(x_start)
    grad_s[...] = jnp.zeros_like(grad_s)

    over_peers(w, wide, lambda p: own_copy(p, p).wait_recv())

    def add_small(k, value):
        return value + small_landed[lax.rem(w + k, wide)]

    own_small = lax.fori_loop(1, wide, add_small, small_held[levels - 1][0, w])
    squares = squares + total_of(own_small * own_small)
    out_small[...] = own_small
    for m in range(4 * L):
        layer, kind = m // 4, m % 4

        @pl.when(w == worker_of(m, wide))
        def _():
            start = offsets[kind] - half_rows * (kind // 2)
            size = packed_rows(kind, narrow)
            whole = ROWS_OF[kind] // narrow

            def add_block(k, value):
                p = lax.rem(w // 2 + k, wide // 2) * 2 + side
                block_copy(m, p).wait_recv()
                return value + mats_landed[p, :size]

            packed = lax.fori_loop(
                1, wide // 2, add_block,
                mats_held[layer][steps - 1][0, start : start + size],
            )
            tail = packed[whole:]
            grad_s[:whole, :TOKS] = packed[:whole]
            grad_s[: whole // 2, TOKS : D] = tail[:, : D - TOKS]
            grad_s[whole // 2 : whole, TOKS : D] = tail[:, D - TOKS :]

    grad = grad_s[...]
    squares = squares + total_of(grad * grad)
    lane = lax.broadcasted_iota(jnp.int32, (1, TOKS), 1)
    norm_near[n] = jnp.where(lane == 0, squares, jnp.where(lane == 1, loss_here, 0.0))
    over_peers(n, narrow, lambda p: near_copy(p, n).start())
    grad_t = jnp.transpose(grad)[:D]
    over_peers(n, narrow, lambda p: near_copy(p, p).wait_recv())
    norm_all[w] = jnp.sum(norm_near[...], 0)
    over_peers(w, wide, lambda p: norm_copy(p, w).start())
    over_peers(w, wide, lambda p: norm_copy(p, p).wait_recv())
    sums = jnp.sum(norm_all[...], 0)
    norm = jnp.sqrt(sums)
    factor = CLIP / jnp.maximum(norm[:, :1], CLIP)
    out_stats[...] = jnp.where(lane == 0, norm, jnp.where(lane == 2, factor, sums))

    def gather_rows(ref):
        if columns % 8 == 0:
            return ref[...].reshape(D, ref.shape[2])
        return jnp.concatenate([ref[p] for p in range(wide)], 0)

    def spread_rows(ref, value):
        if columns % 8 == 0:
            ref[...] = value.reshape(ref.shape)
        else:
            for p in range(wide):
                ref[p] = value[p * columns : (p + 1) * columns]

    for m in range(4 * L):
        @pl.when(w == worker_of(m, wide))
        def _():
            over_peers(w, wide, lambda p: get_copy(m, p).wait_recv())
            size = ROWS_OF[m % 4] // narrow
            moment = MOMENTUM * gather_rows(mom_came[m % 4]) + factor * grad_t[:, :size]
            x_start[:, :size] = moment
            spread_rows(mom_sent[m % 4], moment)
            over_peers(w, wide, lambda p: put_copy(m, p).start())
            out_moments[m % 4][m // 4] = mom_sent[m % 4][w]

    x = x_start[...]
    gram = exact(x, x, 1, 1)
    rest = D - TOKS
    gram_held[0, :D] = gram[:, :TOKS]
    gram_held[0, D : D + rest] = jnp.concatenate(
        [gram[TOKS:, TOKS:], jnp.zeros((rest, TOKS - rest), F32)], 1
    )
    for s in range(levels):
        gram_copy(s).start()
        gram_copy(s).wait_recv()
        gram_held[s + 1] = gram_held[s] + gram_came[s]
    left = gram_held[levels, :D]
    corner = gram_held[levels, D : D + rest][:, :rest]
    above = jnp.transpose(
        jnp.concatenate([left[TOKS:], jnp.zeros((TOKS - rest, TOKS), F32)], 0)
    )[:, :rest]
    gram = jnp.concatenate([left, jnp.concatenate([above, corner], 0)], 1)
    eye = jnp.where(
        lax.broadcasted_iota(jnp.int32, (D, D), 0) == lax.broadcasted_iota(jnp.int32, (D, D), 1),
        1.0, 0.0,
    )
    inverse = lax.rsqrt(total_of(eye * gram) + ORTHO_EPS)
    x_end[...] = x * inverse
    square_s[...] = gram * (inverse * inverse)

    def ortho_step(step, carry):
        square = square_s[...]
        polynomial = NS_ONE * eye + NS_TWO * square + NS_THREE * exact(square, square)
        x_end[...] = exact(polynomial, x_end[...])
        square_s[...] = exact(polynomial, exact(square, polynomial))
        return carry

    lax.fori_loop(0, 4, ortho_step, 0)
    square = square_s[...]
    polynomial = NS_ONE * eye + NS_TWO * square + NS_THREE * exact(square, square)
    x_end[...] = exact(polynomial, x_end[...])
    for m in range(4 * L):
        @pl.when(w == worker_of(m, wide))
        def _():
            size = ROWS_OF[m % 4] // narrow
            spread_rows(x_sent[m % 4], x_end[:, :size])
            over_peers(w, wide, lambda p: new_copy(m, p).start())
            x_came[m % 4][m // 4] = x_sent[m % 4][w]

    for m in range(4 * L):
        @pl.when(w != worker_of(m, wide))
        def _():
            new_copy(m, w).wait_recv()

    for m in range(4 * L):
        @pl.when(w != worker_of(m, wide))
        def _():
            put_copy(m, w).wait_recv()
            get_copy(m, w).wait_send()

        @pl.when((side == (m % 4) // 2) & (w != worker_of(m, wide)))
        def _():
            block_copy(m, w).wait_send()

        @pl.when(w == worker_of(m, wide))
        def _():
            over_peers(w, wide, lambda p: put_copy(m, p).wait_send())
            over_peers(w, wide, lambda p: new_copy(m, p).wait_send())

    table_copy.wait()
    for s in range(levels):
        gram_copy(s).wait_send()
        for copy in small_copies(s):
            copy.wait_send()
    for l in range(L):
        for t in range(steps):
            for copy in step_copies(l, t):
                copy.wait_send()
    over_peers(n, narrow, lambda p: near_copy(p, n).wait_send())
    over_peers(w, wide, lambda p: norm_copy(p, w).wait_send())
    over_peers(me, count, lambda p: slot_copy(p, me).wait_send())
    over_peers(w, wide, lambda p: own_copy(p, w).wait_send())


def finish_call(dmats, dsmall, dslots, requests, loss, extra, moments, wide, narrow):
    count = wide * narrow
    levels = levels_of(narrow)
    columns = D // wide
    _, total = packed_offsets(narrow)
    shape = jax.ShapeDtypeStruct
    local = extra.shape[1]
    outs = [shape((1, TOKS), F32), shape(extra.shape, F32), shape(dsmall.shape[2:], F32)]
    outs += [shape(a.shape, F32) for a in moments + moments]
    vm = pltpu.VMEM
    dma = pltpu.SemaphoreType.DMA
    steps = levels + 1

    def mats_shapes(l):
        sizes, quarters, rows = [], narrow, total
        plan = list(range(levels)) + ["side"] if l % 2 else [0, "side"] + list(range(1, levels))
        for move in plan:
            if move == "side":
                rows //= 2
            else:
                quarters //= 2
            sizes.append(vm((quarters, rows, TOKS), F32))
        return sizes

    mats = [v for l in range(L) for v in mats_shapes(l)]
    small_shapes = [vm((narrow >> (s + 1),) + dsmall.shape[1:], F32) for s in range(levels)]
    largest = max(packed_rows(which, narrow) for which in range(4))
    blocks = [vm((wide, columns, rows // narrow), F32) for rows in ROWS_OF]
    spec = pl.BlockSpec(memory_space=pltpu.VMEM)
    anywhere = pl.BlockSpec(memory_space=pl.ANY)
    return pl.pallas_call(
        functools.partial(finish_kernel, wide=wide, narrow=narrow),
        out_shape=outs,
        in_specs=[anywhere] + [spec] * 4 + [anywhere] + [spec] * 4,
        out_specs=[spec, anywhere] + [spec] * (len(outs) - 2),
        scratch_shapes=mats * 2 + small_shapes * 2
        + [
            vm(dslots.shape, BF16),
            vm((count * CAP, local), BF16),
            vm((wide, largest, TOKS), F32),
            vm((wide,) + dsmall.shape[2:], F32),
            vm((2 * TOKS, 2 * TOKS), F32),
            vm(dmats.shape, F32),
            vm(extra.shape, F32),
            vm((narrow, 1, TOKS), F32),
            vm((wide, 1, TOKS), F32),
        ]
        + blocks * 3
        + [
            vm((D, 2 * TOKS), F32), vm((D, 2 * TOKS), F32), vm((D, D), F32),
            vm((levels + 1, 2 * TOKS, TOKS), F32), vm((levels, 2 * TOKS, TOKS), F32),
            dma((count,)), dma((count,)),
            dma((L, steps, narrow)), dma((L, steps, narrow)),
            dma((levels, narrow // 2)), dma((levels, narrow // 2)),
            dma((4 * L,)), dma((wide,)), dma((wide,)), dma((wide,)),
            dma((narrow,)), dma((narrow,)), dma((wide,)), dma((wide,)),
            dma((4 * L,)), dma((wide,)), dma((wide,)), dma((4 * L,)),
            dma((wide,)), dma((4 * L,)), dma((levels,)), dma((levels,)),
            dma(()), dma(()), dma(()),
        ],
        compiler_params=pltpu.CompilerParams(
            collective_id=1, has_side_effects=True, vmem_limit_bytes=62 << 20
        ),
        name="finish",
    )(dmats, dsmall, dslots, requests, loss, extra, *moments)


def apply_kernel(*refs):
    refs = list(refs)

    def take(number):
        head = refs[:number]
        del refs[:number]
        return head

    stats_ref, start_ref = take(2)
    tables, (gsmall_ref,), smalls = take(4), take(1), take(3)
    weights, ortho, moments = take(4), take(4), take(4)
    out_scalars, out_tables, out_smalls = take(3), take(3), take(3)
    out_weights, out_moments = take(4), take(4)
    factor = jnp.full((1, 1), stats_ref[0, 2], F32)
    table, grad, first, second = (ref[...] for ref in tables)
    for ref, value in zip(out_tables, adam_step(table, factor * grad, first, second)):
        ref[...] = value

    @pl.when(pl.program_id(0) == 0)
    def _():
        out_scalars[0][0, 0] = stats_ref[0, 1]
        out_scalars[1][0, 0] = start_ref[0, CAP + 1]
        out_scalars[2][0, 0] = stats_ref[0, 0]
        small, first, second = (ref[...] for ref in smalls)
        grad = gsmall_ref[: small.shape[0], : small.shape[1]]
        for ref, value in zip(out_smalls, adam_step(small, factor * grad, first, second)):
            ref[...] = value
        for which in range(4):
            scale = math.sqrt(max(1.0, ROWS_OF[which] / D))
            out_weights[which][...] = (
                weights[which][...] * (1.0 - MUON_RATE * DECAY)
                - MUON_RATE * scale * ortho[which][...]
            )
            out_moments[which][...] = moments[which][...]


def apply_call(stats, start_stats, tables, gsmall, smalls, weights, ortho, moments):
    shape = jax.ShapeDtypeStruct
    smem = pl.BlockSpec(memory_space=pltpu.SMEM)
    local = tables[0].shape[1]
    rows = D // 2
    block = pl.BlockSpec((rows, local), lambda i: (i, 0))

    def whole(array):
        return pl.BlockSpec(array.shape, lambda i, nd=array.ndim: (0,) * nd)

    beside = smalls + weights + ortho + moments
    outs = smalls + weights + moments
    return pl.pallas_call(
        apply_kernel,
        grid=(D // rows,),
        out_shape=[shape((1, 1), F32)] * 3
        + [shape(tables[0].shape, F32)] * 3
        + [shape(a.shape, F32) for a in outs],
        in_specs=[smem, smem] + [block] * 4 + [whole(gsmall)] + [whole(a) for a in beside],
        out_specs=[smem] * 3 + [block] * 3 + [whole(a) for a in outs],
        compiler_params=pltpu.CompilerParams(vmem_limit_bytes=62 << 20),
        name="apply",
    )(stats, start_stats, *tables, gsmall, *beside)


def per_device(
    cat_index, num_values, cell_mask, labels, table, table_first, table_second,
    small, small_first, small_second, w_qkv, w_proj, w_in, w_down,
    mom_qkv, mom_proj, mom_in, mom_down,
):
    wide = lax.axis_size("wide")
    narrow = lax.axis_size("narrow")
    count = wide * narrow
    data_rows = num_values.shape[0]
    pair = 8 if count * CAP <= 2048 else 4
    while data_rows % pair:
        pair //= 2
    flip = lambda v: jnp.swapaxes(v, -1, -2)
    weights = [flip(v) for v in (w_qkv, w_proj, w_in, w_down)]
    moments = [flip(v) for v in (mom_qkv, mom_proj, mom_in, mom_down)]
    smalls = [flip(v) for v in (small, small_first, small_second)]
    tables = [flip(v) for v in (table, table_first, table_second)]
    qkv, proj, w_in_all, down, small_all, rows, slots, requests, stats = gather_call(
        cat_index, cell_mask, weights, smalls[0], tables[0], wide, narrow
    )
    over = stats[0, CAP] > 0.5
    entries = cat_index.size

    axes = ("wide", "narrow")
    local = table.shape[0]
    me = lax.axis_index("wide") * narrow + lax.axis_index("narrow")
    ring = [(i, (i + 1) % count) for i in range(count)]

    def hits_at(owner):
        spot = cat_index.reshape(-1) - owner * local
        return (spot[:, None] == lax.iota(jnp.int32, local)[None, :]).astype(BF16)

    def general_rows(rows, slots):
        def turn(s, carry):
            block, looked = carry
            looked = looked + mm(hits_at(lax.rem(me - s + count, count)), block)
            return lax.ppermute(block, axes, ring), looked

        first = (table.astype(BF16), jnp.zeros((entries, D), F32))
        looked = lax.fori_loop(0, count, turn, first)[1].astype(BF16)
        spare = jnp.zeros((rows.shape[0] - entries, D), BF16)
        own = lax.iota(jnp.int32, entries).reshape(cat_index.shape)
        none = jnp.full((data_rows, TOKS - CATF), -1, jnp.int32)
        return jnp.concatenate([looked, spare], 0), jnp.concatenate([none, own], 1)

    def general_terms(dslots):
        tail = dslots[:, CAP:]
        tail = jnp.concatenate([tail[:, :, : D - TOKS], tail[:, :, D - TOKS :]], 1)
        terms = jnp.concatenate([dslots[:, :CAP], tail], 2).reshape(count * CAP, D)[:entries]

        def turn(s, sums):
            owner = lax.rem(me - 1 - s + 2 * count, count)
            return lax.ppermute(sums, axes, ring) + mm(terms, hits_at(owner), 0, 0)

        sums = lax.fori_loop(0, count, turn, jnp.zeros(tables[0].shape, F32))
        return sums, jnp.zeros_like(dslots)

    rows, slots = lax.cond(over, general_rows, lambda r, s: (r, s), rows, slots)
    loss, dmats, dsmall, dslots = model_call(
        stats, labels, rows, slots, num_values, cell_mask,
        (qkv, proj, w_in_all, down), small_all, pair, wide, narrow,
    )
    extra, dslots = lax.cond(
        over, general_terms, lambda d: (jnp.zeros(tables[0].shape, F32), d), dslots
    )
    outs = finish_call(dmats, dsmall, dslots, requests, loss, extra, moments, wide, narrow)
    done = apply_call(
        outs[0], stats, [tables[0], outs[1], *tables[1:]], outs[2], smalls, weights,
        list(outs[3:7]), list(outs[7:11]),
    )
    return tuple(v.reshape(()) for v in done[:3]) + tuple(flip(v) for v in done[3:])


def solution(mesh):
    rows = P(("wide", "narrow"), None)
    square = P("narrow", "wide")
    cube = P(None, "narrow", "wide")
    return jax.shard_map(
        per_device,
        mesh=mesh,
        in_specs=(rows, rows, rows, P(("wide", "narrow")), rows, rows, rows)
        + (square,) * 3 + (cube,) * 8,
        out_specs=(P(), P(), P(), rows, rows, rows) + (square,) * 3 + (cube,) * 8,
        check_vma=False,
    )
```
